32 devices in a mesh: section: 2 (over core), tensor: 4 (over y, x), dp: 4 (over z).
Axes of the slice: x: 2, y: 2, z: 4, core: 2. Of those that a mesh axis runs over, the one named last changes fastest.
Arguments:
- inputs: bfloat16 [8, 1024, 768], P('dp', 'tensor'), may hold values from -6 to 6
- lengths: int32 [8], P('dp'), may hold values from 512 to 1024, as said below
- gains: bfloat16 [2, 2, 768], P('section', None, 'dp'), may hold values from 0.099609375 to 1.8984375
- w_qkv: bfloat16 [2, 768, 3, 768], P('section', 'dp', None, 'tensor'), may hold values from -0.21875 to 0.21875
- w_out: bfloat16 [2, 768, 768], P('section', 'tensor', 'dp'), may hold values from -1.75 to 1.75
- w_up: bfloat16 [2, 768, 3072], P('section', 'dp', 'tensor'), may hold values from -0.21875 to 0.21875
- w_down: bfloat16 [2, 3072, 768], P('section', 'tensor', 'dp'), may hold values from -0.109375 to 0.109375
- cotangent: bfloat16 [8, 1024, 768], P('dp', 'tensor'), may hold values from -6 to 6
Outputs:
- activations: bfloat16 [2, 8, 1024, 768], P('section', 'dp', 'tensor')
- input_grads: bfloat16 [2, 8, 1024, 768], P('section', 'dp', 'tensor')
- gain_grads: float32 [2, 2, 768], P('section', None, ('tensor', 'dp'))
- qkv_grads: float32 [2, 768, 3, 768], P('section', 'dp', None, 'tensor')
- out_grads: float32 [2, 768, 768], P('section', 'tensor', 'dp')
- up_grads: float32 [2, 768, 3072], P('section', 'dp', 'tensor')
- down_grads: float32 [2, 3072, 768], P('section', 'tensor', 'dp')
The draws below stay inside these ranges and needn't reach their ends.
Inputs may be any that keep to these rules, and one draw needn't show every extreme that they name: `lengths`: each entry is the first document's length in a bucket of 1024 positions, either 1024 // 2 or 1024; the rest of the bucket is a second document. Among the 2 buckets of each data group one holds a single document and another holds two.
All inputs are finite; a program needn't handle non-finite values.
Results may differ from the reference program's by a relative error of at most 0.038.
Values may be sent and summed in bfloat16 or wider, within the bound.
A program may use at most 192 MiB of HBM per device.

```python
import jax
import jax.numpy as jnp
from jax import lax

D = 768
HEADS = 12
HEAD = 64
FF = 3072
BUCKET = 1024
MB = 2
HD = 768
BUCKETS = 8


def draw_lengths(key, part):
    key = jax.random.fold_in(key, 7)
    groups = BUCKETS // MB
    key_pick, key_full, key_step = jax.random.split(key, 3)
    picked = jax.random.randint(key_pick, (groups, MB), 0, 2)
    full_slot = jax.random.randint(key_full, (groups, 1), 0, MB)
    short_slot = (full_slot + jax.random.randint(key_step, (groups, 1), 1, MB)) % MB
    slots = jnp.arange(MB, dtype=jnp.int32)[None, :]
    picked = jnp.where(slots == full_slot, 1, picked)
    picked = jnp.where(slots == short_slot, 0, picked)
    return jnp.where(picked == 1, BUCKET, BUCKET // 2).reshape(BUCKETS).astype(jnp.int32)


def spiked(drawn, stream_key, source, target, parts, factor):
    def block_of(axis_at):
        return (jnp.arange(drawn.shape[axis_at]) // (drawn.shape[axis_at] // parts)).reshape((-1,) + (1,) * (drawn.ndim - 1 - axis_at))

    one_side = jax.random.permutation(stream_key, parts)[block_of(target)]
    far = (block_of(target) + parts // 2) % parts
    return jnp.where((block_of(source) == one_side) | (block_of(source) == far), factor * drawn, drawn)


def steps_of(own_key, dims, shards, smallest, largest):
    loudness, own = 1.0, jax.random.fold_in(own_key, 6)
    for position, parts in shards:
        heights = jnp.exp(jax.random.uniform(jax.random.fold_in(own, position), (parts,), jnp.float32, smallest / len(shards), largest / len(shards)))
        loudness = loudness * jnp.repeat(heights, dims[position] // parts).reshape([-1 if axis == position else 1 for axis in range(len(dims))])
    return loudness


def noise(stream_key, extent, deviation, reach, pieces=(), kind=jnp.bfloat16):
    entries = deviation * jax.random.normal(stream_key, extent, jnp.float32)
    if pieces:
        entries = entries * steps_of(stream_key, extent, pieces, -0.22, 0.18)
    return jnp.clip(entries, -reach, reach).astype(kind)


def heavy_noise(key, dims, width, bound, shards, heavy, held_as=jnp.bfloat16):
    drawn = width * jax.random.normal(key, dims, jnp.float32)
    if shards:
        drawn = drawn * steps_of(key, dims, shards, -0.22, 0.18)
    return jnp.clip(spiked(drawn, jax.random.fold_in(key, 3), *heavy), -bound, bound).astype(held_as)


def setup_inputs(seed: int = 0) -> dict:
    key_list = jax.random.split(jax.random.key(seed), 9)
    inputs = noise(key_list[0], (BUCKETS, BUCKET, D), 1.0, 6.0, ((0, 4), (1, 4)))
    lengths = draw_lengths(jax.random.fold_in(key_list[8], 71), 0)
    gains = jnp.clip(1.0 + 0.18 * jax.random.normal(key_list[2], (2, 2, D), jnp.float32), 0.099609375, 1.8984375).astype(jnp.bfloat16)
    w_qkv = noise(key_list[3], (2, D, 3, HD), D ** -0.5, 0.21875, ((0, 2), (1, 4), (3, 4)))
    w_out = noise(key_list[4], (2, HD, D), (max(HD * 16 // BUCKET, 1)) ** -0.5, 1.75, ((0, 2), (1, 4), (2, 4)))
    w_up = noise(key_list[5], (2, D, FF), D ** -0.5, 0.21875, ((0, 2), (1, 4), (2, 4)))
    w_down = noise(key_list[6], (2, FF, D), FF ** -0.5, 0.109375, ((0, 2), (1, 4), (2, 4)))
    cotangent = heavy_noise(key_list[7], (BUCKETS, BUCKET, D), 1.0, 6.0, ((0, 4), (1, 4)), (0, 2, 4, 2.0))
    return dict(inputs=inputs, lengths=lengths, gains=gains, w_qkv=w_qkv, w_out=w_out, w_up=w_up, w_down=w_down, cotangent=cotangent)


epsilon = 1e-05

@jax.custom_vjp
def low(v):
    return lax.optimization_barrier(v.astype(jnp.bfloat16)).astype(jnp.float32)

@jax.custom_vjp
def low_back(v):
    return v

def low_keep(v):
    return (low(v), None)

def low_pass(kept, grad):
    return (grad,)

def back_keep(v):
    return (v, None)

def back_low(kept, grad):
    return (low(grad),)
low.defvjp(low_keep, low_pass)
low_back.defvjp(back_keep, back_low)

def normalize(row_block, gain_row):
    centre = row_block - lax.optimization_barrier(jnp.mean(row_block, axis=-1, keepdims=True))
    spread = lax.optimization_barrier(jnp.mean(centre * centre, axis=-1, keepdims=True))
    return centre * lax.rsqrt(spread + epsilon) * gain_row

def smooth_gelu(value_rows):
    return jax.nn.gelu(value_rows, approximate=True)

def score_terms(scores, cog_share):
    radius = jnp.sqrt(scores * scores + 1.0)
    magnitude = cog_share * radius + (1.0 - cog_share) * scores
    direction = cog_share * scores / radius + (1.0 - cog_share)
    return (radius, magnitude, direction)

def visible_pairs(first_len, row_start, row_total, key_total):
    query_pos = row_start + lax.broadcasted_iota(jnp.int32, (row_total, key_total), 0)
    key_pos = lax.broadcasted_iota(jnp.int32, (row_total, key_total), 1)
    return (key_pos <= query_pos) & ((query_pos >= first_len) == (key_pos >= first_len))

def product(left, right):
    return jnp.dot(left, right, precision=lax.Precision.HIGHEST)

def attend(query_rows, key_rows, value_rows, first_len, cog_share):
    row_count = query_rows.shape[0]
    block_rows = min(512, row_count)
    score_scale = query_rows.shape[-1] ** (-0.5)

    def per_block(block_index):
        row_start = block_index * block_rows
        query_block = lax.dynamic_slice_in_dim(query_rows, row_start, block_rows, 0)
        scores = low_back(jnp.einsum('qhd,khd->hqk', query_block, key_rows, precision=lax.Precision.HIGHEST) * score_scale)
        radius, magnitude, direction = score_terms(scores, cog_share)
        visible = visible_pairs(first_len, row_start, block_rows, row_count)[None]
        masked_mag = jnp.where(visible, magnitude, -1e+30)
        row_max = lax.optimization_barrier(jnp.max(masked_mag, axis=-1, keepdims=True))
        weights = jnp.exp(masked_mag - row_max)
        probabilities = low(direction * weights / lax.optimization_barrier(jnp.sum(weights, axis=-1, keepdims=True)))
        return jnp.einsum('hqk,khd->qhd', probabilities, value_rows, precision=lax.Precision.HIGHEST)
    out_blocks = lax.map(jax.checkpoint(per_block), jnp.arange(row_count // block_rows, dtype=jnp.int32))
    return out_blocks.reshape(row_count, -1)

def layer_pass(row_block, first_len, cog_share, gain_pair, qkv_weight, out_weight, up_weight, down_weight):
    row_count = row_block.shape[0]
    norm_one = low(normalize(row_block, gain_pair[0]))
    packed = low_back(low(product(norm_one, qkv_weight.reshape(qkv_weight.shape[0], -1))))
    packed = packed.reshape(row_count, 3, HEADS, HEAD)
    attn_rows = low_back(low(attend(packed[:, 0], packed[:, 1], packed[:, 2], first_len, cog_share)))
    middle = row_block + low_back(product(attn_rows, out_weight))
    norm_two = low(normalize(middle, gain_pair[1]))
    hidden_pre = low_back(product(norm_two, up_weight))
    hidden = low(smooth_gelu(hidden_pre))
    return middle + low_back(product(hidden, down_weight))

def reference(inputs, lengths, gains, w_qkv, w_out, w_up, w_down, cotangent):
    row_data = inputs.astype(jnp.float32)
    params = (gains.astype(jnp.float32), w_qkv.astype(jnp.float32), w_out.astype(jnp.float32), w_up.astype(jnp.float32), w_down.astype(jnp.float32))

    def forward(row_data, gain_all, qkv_all, out_all, up_all, down_all, offset_rows):

        def per_bucket(bucket_item):
            bucket, first_len, offset = bucket_item
            earlier = low_back(low(layer_pass(bucket, first_len, 1.0, gain_all[0], qkv_all[0], out_all[0], up_all[0], down_all[0]))) + offset
            lagging = layer_pass(earlier, first_len, 0.0, gain_all[1], qkv_all[1], out_all[1], up_all[1], down_all[1])
            return (earlier, lagging)
        return lax.map(jax.checkpoint(per_bucket), (row_data, lengths, offset_rows))
    (earlier, lagging), pullback = jax.vjp(forward, row_data, *params, jnp.zeros_like(row_data))
    grads = pullback((jnp.zeros_like(earlier), cotangent.astype(jnp.float32)))
    activations = jnp.stack([earlier, lagging]).astype(jnp.bfloat16)
    input_grads = jnp.stack([grads[0], grads[6]]).astype(jnp.bfloat16)
    return (activations, input_grads, grads[1], grads[2], grads[3], grads[4], grads[5])
```

```python
import functools

import jax
import jax.numpy as jnp
from jax import lax
from jax.experimental import pallas as pl
from jax.experimental.pallas import tpu as pltpu
from jax.sharding import PartitionSpec as P

HEAD = 64
EPSILON = 1e-05
MASKED = -1e30
CHUNKS = 4
BF16 = jnp.bfloat16
F32 = jnp.float32
MESH = pl.DeviceIdType.MESH
TILE = 256


def nn(left, right):
    return lax.dot_general(left, right, (((1,), (0,)), ((), ())), preferred_element_type=F32)


def nt(left, right):
    return lax.dot_general(left, right, (((1,), (1,)), ((), ())), preferred_element_type=F32)


def tn(left, right):
    return lax.dot_general(left, right, (((0,), (0,)), ((), ())), preferred_element_type=F32)


def unit_rows(rows):
    centre = rows - jnp.mean(rows, axis=-1, keepdims=True)
    spread = jnp.mean(centre * centre, axis=-1, keepdims=True)
    scale = lax.rsqrt(spread + EPSILON)
    return centre * scale, scale


def norm_back(unit, scale, gain, grad):
    wide = grad * gain
    inner = jnp.mean(wide * unit, axis=-1, keepdims=True)
    return scale * (wide - jnp.mean(wide, axis=-1, keepdims=True) - unit * inner)


def gelu_parts(x):
    root = 0.7978845608028654
    square = x * x
    bend = jnp.tanh(root * x * (1.0 + 0.044715 * square))
    half = 0.5 + 0.5 * bend
    slope = half + 0.5 * x * (1.0 - bend * bend) * (root * (1.0 + 0.134145 * square))
    return x * half, slope


AG_NORM2 = (0, 1)
AG_MIDDLE = 2
AG_DA = (3, 4)
AG_DR = 5
RS_ATTN = (0, 1)
RS_MLP = (2, 3)
RS_DMLP = (4, 5)
RS_DATTN = (6, 7)


def block_kernel(
    inp,
    cot,
    w_in,
    gains,
    bias,
    acts,
    igr,
    grads,
    gain_out,
    W,
    X0,
    Y0,
    CT,
    DR,
    N1,
    N2,
    QKV,
    KT,
    VT,
    ATT,
    ATTT,
    LSE,
    PRE,
    HID,
    DPRE,
    DQKV,
    DA,
    DKV,
    DATH,
    DATT,
    DQT,
    MID,
    DMID,
    PART,
    RC,
    XS,
    RX,
    LAST,
    STG,
    w_sem,
    in_send,
    in_recv,
    ag_send,
    ag_recv,
    rs_send,
    rs_recv,
    out_send,
    out_recv,
    full_send,
    full_recv,
    stg_sem,
):
    s = lax.axis_index("section")
    t = lax.axis_index("tensor")
    z = lax.axis_index("dp")
    x = lax.rem(t, 2)
    y = lax.div(t, 2)
    rank = 2 * s + x
    t_x = 2 * y + 1 - x
    t_y = 2 * (1 - y) + x
    peer_c = (1 - s, t, z)
    peer_x = (s, t_x, z)
    rank_x = 2 * s + 1 - x
    chunk = X0.shape[0] // CHUNKS
    piece = chunk // 4
    half = CHUNKS // 2
    width = X0.shape[1]
    tiles = width // TILE
    heads = KT.shape[1]

    barrier = pltpu.get_barrier_semaphore()
    for other_s in range(2):
        for other in range(CHUNKS):

            @pl.when((s != other_s) | (t != other))
            def _():
                pl.semaphore_signal(
                    barrier, inc=1, device_id=(other_s, other, z), device_id_type=MESH
                )

    def remote(src, dst, send_sem, recv_sem, device):
        return pltpu.make_async_remote_copy(
            src_ref=src,
            dst_ref=dst,
            send_sem=send_sem,
            recv_sem=recv_sem,
            device_id=device,
            device_id_type=MESH,
        )

    def arrived(ref, sem):
        pltpu.make_async_copy(ref, ref, sem).wait()

    def rows_of(j):
        return pl.ds(pl.multiple_of(j * chunk, chunk), chunk)

    def piece_of(j, r):
        return pl.ds(pl.multiple_of(j * chunk + r * piece, piece), piece)

    def own_of(j):
        return pl.ds(pl.multiple_of(j * piece, piece), piece)

    def columns(n):
        return pl.ds(pl.multiple_of(n * TILE, TILE), TILE)

    weight_copies = [
        pltpu.make_async_copy(w_in.at[l], W.at[l], w_sem.at[l]) for l in range(2)
    ]
    for copy in weight_copies:
        copy.start()

    pl.semaphore_wait(barrier, 2 * CHUNKS - 1)

    def spread(source, target, which):
        pltpu.make_async_copy(
            source.at[y], target.at[rows_of(t)], in_recv.at[which, t]
        ).start()
        for other in range(CHUNKS):

            @pl.when(t != other)
            def _():
                remote(
                    source.at[other // 2],
                    target.at[rows_of(t)],
                    in_send.at[which, other],
                    in_recv.at[which, t],
                    (s, other, z),
                ).start()

    def spread_done(source, which):
        for other in range(CHUNKS):

            @pl.when(t != other)
            def _():
                arrived(source.at[other // 2], in_send.at[which, other])

    spread(inp, X0, 0)
    spread(cot, CT, 1)

    def gather_start(stage, ref, j):
        own = ref.at[piece_of(j, rank)]
        remote(own, own, ag_send.at[stage, 0, j], ag_recv.at[stage, 0, j], peer_x).start()
        remote(own, own, ag_send.at[stage, 1, j], ag_recv.at[stage, 1, j], peer_c).start()

    def gather_relay(stage, ref, j):
        theirs = ref.at[piece_of(j, rank_x)]
        arrived(theirs, ag_recv.at[stage, 0, j])
        remote(
            theirs, theirs, ag_send.at[stage, 2, j], ag_recv.at[stage, 2, j], peer_c
        ).start()

    def gather_wait(stage, ref, j):
        some = ref.at[piece_of(j, rank)]
        arrived(some, ag_recv.at[stage, 1, j])
        arrived(some, ag_recv.at[stage, 2, j])

    def sum_start(stage, b, j):
        half_rows = pl.ds(pl.multiple_of(j * chunk + (1 - s) * 2 * piece, 2 * piece), 2 * piece)
        remote(
            PART.at[b, half_rows],
            RC.at[b, j],
            rs_send.at[stage, 0, j],
            rs_recv.at[stage, 0, j],
            peer_c,
        ).start()

    def sum_pass(stage, b, j):
        arrived(RC.at[b, j], rs_recv.at[stage, 0, j])
        XS[b, j] = (
            PART[b, piece_of(j, rank_x), :].astype(F32)
            + RC[b, j, own_of(1 - x), :].astype(F32)
        ).astype(BF16)
        remote(
            XS.at[b, j], RX.at[b, j], rs_send.at[stage, 1, j], rs_recv.at[stage, 1, j], peer_x
        ).start()

    def sum_wait(stage, b, j):
        arrived(RX.at[b, j], rs_recv.at[stage, 1, j])
        total = (
            PART[b, piece_of(j, rank), :].astype(F32)
            + RC[b, j, own_of(x), :].astype(F32)
            + RX[b, j].astype(F32)
        )
        arrived(RC.at[b, j], rs_send.at[stage, 0, j])
        arrived(XS.at[b, j], rs_send.at[stage, 1, j])
        return total

    key_index = lax.broadcasted_iota(jnp.int32, (chunk, chunk), 0)
    query_index = lax.broadcasted_iota(jnp.int32, (chunk, chunk), 1)
    causal = key_index <= query_index

    def scores(l, st, i, j, diagonal):
        if l == 0:
            grown = st * st + 1.0
            inverse = lax.rsqrt(grown)
            magnitude = grown * inverse
            sign = st * inverse
        else:
            inverse, magnitude, sign = None, st, None
        if diagonal:
            magnitude = jnp.where(causal, magnitude, MASKED)
        else:
            apart = (j >= half) & (i < half)
            magnitude = magnitude + jnp.where(apart, bias[0:1, 0:chunk], 0.0)
        return inverse, magnitude, sign

    def attn_forward(l, j):
        rows = rows_of(j)
        source = X0 if l == 0 else Y0
        if l == 0:
            arrived(X0.at[rows], in_recv.at[0, j])
        else:
            gather_wait(AG_MIDDLE, Y0, j)

        @pl.loop(0, 4)
        def _(q):
            part = piece_of(j, q)
            unit, _ = unit_rows(source[part, :].astype(F32))
            N1[l, part, :] = (unit * gains[2 * l : 2 * l + 1, :]).astype(BF16)

        packed = nn(N1[l, rows, :], W[l, :, 0 : 3 * heads * HEAD]).astype(BF16)
        for h in range(heads):
            QKV[l, h, rows, :] = packed[:, h * HEAD : (h + 1) * HEAD] * jnp.asarray(
                HEAD**-0.5, BF16
            )
        for h in range(heads, 3 * heads):
            QKV[l, h, rows, :] = packed[:, h * HEAD : (h + 1) * HEAD]
        turned = packed[:, heads * HEAD :].astype(F32).T.astype(BF16)
        for h in range(heads):
            KT[l, h, :, rows] = turned[h * HEAD : (h + 1) * HEAD]
            VT[h, :, rows] = turned[(heads + h) * HEAD : (heads + h + 1) * HEAD]

        @pl.loop(0, heads)
        def _(h):
            query = QKV[l, h, rows, :]

            def block(i, carry, diagonal):
                top, total, out = carry
                keys = rows_of(i)
                st = nt(QKV[l, heads + h, keys, :], query)
                _, magnitude, sign = scores(l, st, i, j, diagonal)
                new_top = jnp.maximum(top, jnp.max(magnitude, axis=0, keepdims=True))
                weights = jnp.exp(magnitude - new_top)
                shrink = jnp.exp(top - new_top)
                total = total * shrink + jnp.sum(weights, axis=0, keepdims=True)
                signed = weights if l == 1 else sign * weights
                out = out * shrink + nn(VT[h, :, keys], signed.astype(BF16))
                return new_top, total, out

            carry = (
                jnp.full((1, chunk), MASKED, F32),
                jnp.zeros((1, chunk), F32),
                jnp.zeros((HEAD, chunk), F32),
            )
            carry = block(j, carry, True)
            top, total, out = lax.fori_loop(0, j, lambda i, c: block(i, c, False), carry)
            ATTT[l, h, :, rows] = out / total
            LSE[l, h, :, rows] = top + jnp.log(total)

        joined = jnp.concatenate(
            [jnp.zeros((HEAD, chunk), F32)] + [ATTT[l, h, :, rows] for h in range(heads)], axis=0
        )
        ATT[l, rows, :] = joined.T.astype(BF16)
        for n in range(tiles):
            PART[0, rows, n * TILE : (n + 1) * TILE] = nt(
                ATT[l, rows, :], W[l, n * TILE : (n + 1) * TILE, 512:768]
            ).astype(BF16)
        sum_start(RS_ATTN[l], 0, j)

    def attn_sum(l, j):
        total = sum_wait(RS_ATTN[l], 0, j)
        source = X0 if l == 0 else Y0
        own = piece_of(j, rank)
        middle = source[own, :].astype(F32) + total
        MID[l, own_of(j), :] = middle
        unit, _ = unit_rows(middle)
        N2[l, own, :] = (unit * gains[2 * l + 1 : 2 * l + 2, :]).astype(BF16)
        gather_start(AG_NORM2[l], N2.at[l], j)

    def mlp_forward(l, j):
        rows = rows_of(j)
        gather_wait(AG_NORM2[l], N2.at[l], j)
        for n in range(tiles):
            here = slice(n * TILE, (n + 1) * TILE)
            pre = nn(N2[l, rows, :], W[l, :, width + n * TILE : width + (n + 1) * TILE])
            PRE[l, rows, here] = pre.astype(BF16)
            HID[rows, here] = gelu_parts(pre)[0].astype(BF16)
        for n in range(tiles):
            here = slice(n * TILE, (n + 1) * TILE)
            PART[1, rows, here] = nt(HID[rows, :], W[l, here, 2 * width : 3 * width]).astype(BF16)
        sum_start(RS_MLP[l], 1, j)

    def last_out(which, j, section, out):
        LAST_rows = LAST.at[which, own_of(j)]
        target = out.at[y, pl.ds(pl.multiple_of(rank * piece, piece), piece)]

        @pl.when((s == section) & (t == j))
        def _():
            pltpu.make_async_copy(LAST_rows, target, out_recv.at[which, y, rank]).start()

        @pl.when((s != section) | (t != j))
        def _():
            remote(
                LAST_rows,
                target,
                out_send.at[which, j],
                out_recv.at[which, y, rank],
                (section, j, z),
            ).start()

    def last_out_done(which, section, out):
        for j in range(CHUNKS):

            @pl.when((s != section) | (t != j))
            def _():
                arrived(LAST.at[which, own_of(j)], out_send.at[which, j])

        @pl.when(s == section)
        def _():
            for m in range(2):
                for r in range(4):
                    arrived(
                        out.at[m, r * piece : (r + 1) * piece], out_recv.at[which, m, r]
                    )

    def full_out(which, section, ref, out):
        @pl.when(s == section)
        def _():
            pltpu.make_async_copy(
                ref.at[rows_of(t)], out.at[y], full_recv.at[which, y]
            ).start()
            remote(
                ref.at[rows_of(t_y)],
                out.at[y],
                full_send.at[which],
                full_recv.at[which, y],
                (s, t_y, z),
            ).start()

    def full_out_done(which, section, ref, out):
        @pl.when(s == section)
        def _():
            arrived(out.at[0], full_recv.at[which, 0])
            arrived(out.at[1], full_recv.at[which, 1])
            arrived(ref.at[rows_of(t_y)], full_send.at[which])

    def mlp_sum(l, j):
        result = MID[l, own_of(j), :] + sum_wait(RS_MLP[l], 1, j)
        if l == 0:
            Y0[piece_of(j, rank), :] = result.astype(BF16)
            gather_start(AG_MIDDLE, Y0, j)
        else:
            LAST[0, own_of(j), :] = result.astype(BF16)
            last_out(0, j, 1, acts)

    def mlp_backward(l, j):
        rows = rows_of(j)
        source = CT if l == 1 else DR
        if l == 1:
            arrived(CT.at[rows], in_recv.at[1, j])
        else:
            gather_wait(AG_DR, DR, j)
        for n in range(tiles):
            here = slice(n * TILE, (n + 1) * TILE)
            back = nn(source[rows, :], W[l, :, 2 * width + n * TILE : 2 * width + (n + 1) * TILE])
            hidden, slope = gelu_parts(PRE[l, rows, here].astype(F32))
            HID[rows, here] = hidden.astype(BF16)
            DPRE[rows, here] = (slope * back).astype(BF16)
        for n in range(tiles):
            here = slice(n * TILE, (n + 1) * TILE)
            PART[0, rows, here] = nt(DPRE[rows, :], W[l, here, width : 2 * width]).astype(BF16)
        sum_start(RS_DMLP[l], 0, j)

    def mlp_back_sum(l, j):
        total = sum_wait(RS_DMLP[l], 0, j)
        source = CT if l == 1 else DR
        own = piece_of(j, rank)
        unit, scale = unit_rows(MID[l, own_of(j), :])
        row = 2 * l + 1
        gain_out[row : row + 1, :] += jnp.sum(total * unit, axis=0, keepdims=True)
        grad = source[own, :].astype(F32) + norm_back(
            unit, scale, gains[row : row + 1, :], total
        )
        DMID[own_of(j), :] = grad
        DA[l, own, :] = grad.astype(BF16)
        gather_start(AG_DA[l], DA.at[l], j)

    def attn_backward(l, j):
        rows = rows_of(j)
        gather_wait(AG_DA[l], DA.at[l], j)

        @pl.when(j == CHUNKS - 1)
        def _():
            DKV[...] = jnp.zeros_like(DKV)

        back = nn(DA[l, rows, :], W[l, :, 512:768]).astype(BF16)
        turned = back.astype(F32).T.astype(BF16)
        for h in range(heads):
            DATH[h] = back[:, (h + 1) * HEAD : (h + 2) * HEAD]
            DATT[h] = turned[(h + 1) * HEAD : (h + 2) * HEAD]

        @pl.loop(0, heads)
        def _(h):
            query = QKV[l, h, rows, :]
            grad = DATH[h]
            grad_t = DATT[h]
            inner = jnp.sum(grad_t.astype(F32) * ATTT[l, h, :, rows], axis=0, keepdims=True)
            log_total = LSE[l, h, :, rows]

            def block(i, query_grad, diagonal):
                keys = rows_of(i)
                st = nt(QKV[l, heads + h, keys, :], query)
                dp = nn(QKV[l, 2 * heads + h, keys, :], grad_t)
                inverse, magnitude, sign = scores(l, st, i, j, diagonal)
                weights = jnp.exp(magnitude - log_total)
                if l == 0:
                    signed = sign * weights
                    ds = weights * (
                        sign * (sign * dp - inner) + dp * (inverse * inverse * inverse)
                    )
                else:
                    signed = weights
                    ds = weights * (dp - inner)
                ds = ds.astype(BF16)
                DKV[h, keys, :] += nn(ds, query)
                DKV[heads + h, keys, :] += nn(signed.astype(BF16), grad)
                return query_grad + nn(KT[l, h, :, keys], ds)

            query_grad = block(j, jnp.zeros((HEAD, chunk), F32), True)
            query_grad = lax.fori_loop(0, j, lambda i, c: block(i, c, False), query_grad)
            DQT[h] = query_grad * HEAD**-0.5

        turned = jnp.concatenate([DQT[h] for h in range(heads)], axis=0).T
        DQKV[rows, :] = jnp.concatenate(
            [turned] + [DKV[h, rows, :] for h in range(2 * heads)], axis=1
        ).astype(BF16)
        for n in range(tiles):
            here = slice(n * TILE, (n + 1) * TILE)
            PART[1, rows, here] = nt(
                DQKV[rows, :], W[l, here, 0 : 3 * heads * HEAD]
            ).astype(BF16)
        sum_start(RS_DATTN[l], 1, j)

    def attn_back_sum(l, j):
        total = sum_wait(RS_DATTN[l], 1, j)
        source = X0 if l == 0 else Y0
        own = piece_of(j, rank)
        unit, scale = unit_rows(source[own, :].astype(F32))
        row = 2 * l
        gain_out[row : row + 1, :] += jnp.sum(total * unit, axis=0, keepdims=True)
        result = DMID[own_of(j), :] + norm_back(unit, scale, gains[row : row + 1, :], total)
        if l == 1:
            DR[own, :] = result.astype(BF16)
            gather_start(AG_DR, DR, j)
        else:
            LAST[1, own_of(j), :] = result.astype(BF16)
            last_out(1, j, 0, igr)

    def weight_grad(l, group):
        @pl.loop(0, tiles)
        def _(n):
            slot = lax.rem(n, 2)
            target = grads.at[l, columns(n), group * width : (group + 1) * width]

            @pl.when(n >= 2)
            def _():
                arrived(STG.at[slot], stg_sem.at[slot])

            if group == 0:
                STG[slot, :, 0 : 3 * heads * HEAD] = tn(N1[l, :, columns(n)], DQKV[...]).astype(
                    BF16
                )
                out_part = tn(DA[l, :, columns(n)], ATT[l])
                STG[slot, :, 3 * heads * HEAD :] = out_part[:, HEAD:].astype(BF16)
            elif group == 1:
                STG[slot] = tn(N2[l, :, columns(n)], DPRE[...]).astype(BF16)
            else:
                source = CT if l == 1 else DR
                STG[slot] = tn(source[:, columns(n)], HID[...]).astype(BF16)
            pltpu.make_async_copy(STG.at[slot], target, stg_sem.at[slot]).start()

        arrived(STG.at[0], stg_sem.at[0])
        arrived(STG.at[1], stg_sem.at[1])

    def at(j, task, *args):
        @pl.when((j >= 0) & (j < CHUNKS))
        def _():
            task(*args, j)

    def back_at(j, task, *args):
        @pl.when((j >= 0) & (j < CHUNKS))
        def _():
            task(*args, CHUNKS - 1 - j)

    gain_out[...] = jnp.zeros_like(gain_out)
    weight_copies[0].wait()

    @pl.loop(0, 11)
    def _(k):
        for l in range(2):
            at(k - 4 * l - 1, lambda l, j: sum_pass(RS_ATTN[l], 0, j), l)
            at(k - 4 * l - 3, lambda l, j: sum_pass(RS_MLP[l], 1, j), l)
        at(k, attn_forward, 0)
        for l in range(2):
            at(k - 4 * l - 2, lambda l, j: gather_relay(AG_NORM2[l], N2.at[l], j), l)
        at(k - 4, lambda j: gather_relay(AG_MIDDLE, Y0, j))
        for l in range(2):
            at(k - 4 * l - 1, attn_sum, l)
        at(k - 2, mlp_forward, 0)
        for l in range(2):
            at(k - 4 * l - 3, mlp_sum, l)

        @pl.when(k == 4)
        def _():
            weight_copies[1].wait()

        at(k - 4, attn_forward, 1)
        at(k - 6, mlp_forward, 1)

        @pl.when(k == 8)
        def _():
            full_out(0, 0, Y0, acts)

    @pl.loop(0, 11)
    def _(k):
        for l in (1, 0):
            lag = 4 * (1 - l)
            back_at(k - lag - 1, lambda l, j: sum_pass(RS_DMLP[l], 0, j), l)
            back_at(k - lag - 3, lambda l, j: sum_pass(RS_DATTN[l], 1, j), l)
        back_at(k, mlp_backward, 1)
        for l in (1, 0):
            lag = 4 * (1 - l)
            back_at(k - lag - 2, lambda l, j: gather_relay(AG_DA[l], DA.at[l], j), l)
        back_at(k - 4, lambda j: gather_relay(AG_DR, DR, j))
        for l in (1, 0):
            back_at(k - 4 * (1 - l) - 1, mlp_back_sum, l)
        back_at(k - 2, attn_backward, 1)
        for l in (1, 0):
            back_at(k - 4 * (1 - l) - 3, attn_back_sum, l)

        @pl.when(k == 4)
        def _():
            weight_grad(1, 2)
            weight_grad(1, 1)

        back_at(k - 4, mlp_backward, 0)

        @pl.when(k == 6)
        def _():
            weight_grad(1, 0)

        back_at(k - 6, attn_backward, 0)

        @pl.when(k == 8)
        def _():
            full_out(1, 1, DR, igr)
            weight_grad(0, 2)
            weight_grad(0, 1)

    weight_grad(0, 0)

    spread_done(inp, 0)
    spread_done(cot, 1)

    @pl.loop(0, CHUNKS)
    def _(j):
        for stage in range(6):
            for kind in range(3):
                arrived(RX.at[0, 0], ag_send.at[stage, kind, j])

    full_out_done(0, 0, Y0, acts)
    full_out_done(1, 1, DR, igr)
    last_out_done(0, 1, acts)
    last_out_done(1, 0, igr)


def run_blocks(inputs, cotangent, weights, gains, bias):
    buckets, chunk, width = inputs.shape
    rows = CHUNKS * chunk
    piece = chunk // 4
    all_columns = weights.shape[2]
    heads = (all_columns - 2 * width) // (4 * HEAD)
    vmem, dma = pltpu.VMEM, pltpu.SemaphoreType.DMA
    scratch = [
        vmem(weights.shape, BF16),
        vmem((rows, width), BF16),
        vmem((rows, width), BF16),
        vmem((rows, width), BF16),
        vmem((rows, width), BF16),
        vmem((2, rows, width), BF16),
        vmem((2, rows, width), BF16),
        vmem((2, 3 * heads, rows, HEAD), BF16),
        vmem((2, heads, HEAD, rows), BF16),
        vmem((heads, HEAD, rows), BF16),
        vmem((2, rows, (heads + 1) * HEAD), BF16),
        vmem((2, heads, HEAD, rows), F32),
        vmem((2, heads, 1, rows), F32),
        vmem((2, rows, width), BF16),
        vmem((rows, width), BF16),
        vmem((rows, width), BF16),
        vmem((rows, 3 * heads * HEAD), BF16),
        vmem((2, rows, width), BF16),
        vmem((2 * heads, rows, HEAD), F32),
        vmem((heads, chunk, HEAD), BF16),
        vmem((heads, HEAD, chunk), BF16),
        vmem((heads, HEAD, chunk), F32),
        vmem((2, chunk, width), F32),
        vmem((chunk, width), F32),
        vmem((2, rows, width), BF16),
        vmem((2, CHUNKS, 2 * piece, width), BF16),
        vmem((2, CHUNKS, piece, width), BF16),
        vmem((2, CHUNKS, piece, width), BF16),
        vmem((2, chunk, width), BF16),
        vmem((2, TILE, width), BF16),
        dma((2,)),
        dma((2, CHUNKS)),
        dma((2, CHUNKS)),
        dma((6, 3, CHUNKS)),
        dma((6, 3, CHUNKS)),
        dma((8, 2, CHUNKS)),
        dma((8, 2, CHUNKS)),
        dma((2, CHUNKS)),
        dma((2, 2, 4)),
        dma((2,)),
        dma((2, 2)),
        dma((2,)),
    ]
    hbm = pl.BlockSpec(memory_space=pl.ANY)
    in_vmem = pl.BlockSpec(memory_space=pltpu.VMEM)
    return pl.pallas_call(
        block_kernel,
        out_shape=(
            jax.ShapeDtypeStruct(inputs.shape, BF16),
            jax.ShapeDtypeStruct(inputs.shape, BF16),
            jax.ShapeDtypeStruct(weights.shape, BF16),
            jax.ShapeDtypeStruct(gains.shape, F32),
        ),
        in_specs=[hbm, hbm, hbm, in_vmem, in_vmem],
        out_specs=(hbm, hbm, hbm, in_vmem),
        scratch_shapes=scratch,
        compiler_params=pltpu.CompilerParams(
            collective_id=0, has_side_effects=True, vmem_limit_bytes=60 << 20
        ),
        cost_estimate=pl.CostEstimate(
            flops=27_000_000_000, bytes_accessed=40_000_000, transcendentals=20_000_000
        ),
        name="blocks",
    )(inputs, cotangent, weights, gains, bias)


def shards(inputs, lengths, gains, w_qkv, w_out, w_up, w_down, cotangent):
    local_rows, width = inputs.shape[1:]
    y = lax.div(lax.axis_index("tensor"), 2)
    section = lax.axis_index("section")
    own = jnp.concatenate(
        [w_qkv[0].reshape(w_qkv.shape[1], -1), w_out[0].T, w_up[0], w_down[0].T], axis=1
    )
    whole = lax.all_gather(own, "dp", axis=0, tiled=True)
    axes = ("section", "tensor")
    weights = []
    for l in range(2):
        parts = []
        for to_y in range(2):
            pairs = [(4 * l + 2 * c + x, 4 * c + 2 * to_y + x) for c in range(2) for x in range(2)]
            parts.append(lax.ppermute(whole, axes, pairs))
        weights.append(jnp.where(y == 0, parts[0], parts[1]))
    weights = jnp.stack(weights)
    gain_rows = lax.all_gather(gains, "dp", axis=2, tiled=True)
    gain_rows = lax.all_gather(gain_rows, "section", axis=0, tiled=True)
    gain_rows = gain_rows.reshape(4, width).astype(F32)
    gain_rows = jnp.concatenate([gain_rows, jnp.zeros_like(gain_rows)], axis=0)
    first_len = lengths[y]
    bias = jnp.where(first_len == CHUNKS * local_rows, 0.0, MASKED).astype(F32)
    bias = jnp.broadcast_to(bias, (8, local_rows))

    acts, input_grads, partial, gain_part = run_blocks(
        inputs, cotangent, weights, gain_rows, bias
    )

    total = jnp.zeros(partial.shape[1:], F32)
    for l in range(2):
        for from_y in range(2):
            pairs = [
                (4 * c + 2 * from_y + x, 4 * l + 2 * c + x) for c in range(2) for x in range(2)
            ]
            total = total + lax.ppermute(partial[l], axes, pairs).astype(F32)
    total = lax.psum_scatter(total.astype(BF16), "dp", scatter_dimension=0, tiled=True)
    total = total.astype(F32)
    columns = 3 * w_qkv.shape[3]
    out_columns = w_out.shape[1]
    qkv_grads = total[:, :columns].reshape(w_qkv.shape)
    out_grads = total[:, columns : columns + out_columns].T[None]
    columns += out_columns
    up_grads = total[:, columns : columns + w_up.shape[2]][None]
    down_grads = total[:, columns + w_up.shape[2] :].T[None]
    gain_part = lax.psum(gain_part[:4].reshape(2, 2, width), "section")
    gain_part = lax.dynamic_slice_in_dim(gain_part, section, 1, 0)
    gain_grads = lax.psum_scatter(
        gain_part, ("tensor", "dp"), scatter_dimension=2, tiled=True
    )
    return (
        acts[None],
        input_grads[None],
        gain_grads,
        qkv_grads,
        out_grads,
        up_grads,
        down_grads,
    )


def solution(mesh):
    in_specs = (
        P("dp", "tensor", None),
        P("dp"),
        P("section", None, "dp"),
        P("section", "dp", None, "tensor"),
        P("section", "tensor", "dp"),
        P("section", "dp", "tensor"),
        P("section", "tensor", "dp"),
        P("dp", "tensor", None),
    )
    out_specs = (
        P("section", "dp", "tensor", None),
        P("section", "dp", "tensor", None),
        P("section", None, ("tensor", "dp")),
        P("section", "dp", None, "tensor"),
        P("section", "tensor", "dp"),
        P("section", "dp", "tensor"),
        P("section", "tensor", "dp"),
    )
    return jax.shard_map(shards, mesh=mesh, in_specs=in_specs, out_specs=out_specs, check_vma=False)
```

```python
import functools

import jax
import jax.numpy as jnp
from jax import lax
from jax.experimental import pallas as pl
from jax.experimental.pallas import tpu as pltpu
from jax.sharding import PartitionSpec as P

HEAD = 64
EPSILON = 1e-05
MASKED = -1e30
CHUNKS = 4
PARTS = 3
VMEM_LIMIT = 63 << 20
TILE = 256
BF16 = jnp.bfloat16
F32 = jnp.float32
MESH = pl.DeviceIdType.MESH

SUM_ATTN = (0, 2)
SUM_MLP = (1, 3)
SUM_DMLP = (6, 4)
SUM_DATTN = (7, 5)
PAIR_N2 = (0, 1)
PAIR_MIDDLE = 2
PAIR_DA = (4, 3)
PAIR_DR = 5


def nn(left, right):
    return lax.dot_general(left, right, (((1,), (0,)), ((), ())), preferred_element_type=F32)


def nt(left, right):
    return lax.dot_general(left, right, (((1,), (1,)), ((), ())), preferred_element_type=F32)


def tn(left, right):
    return lax.dot_general(left, right, (((0,), (0,)), ((), ())), preferred_element_type=F32)


def unit_rows(rows):
    centre = rows - jnp.mean(rows, axis=-1, keepdims=True)
    spread = jnp.mean(centre * centre, axis=-1, keepdims=True)
    scale = lax.rsqrt(spread + EPSILON)
    return centre * scale, scale


def norm_back(unit, scale, gain, grad):
    wide = grad * gain
    inner = jnp.mean(wide * unit, axis=-1, keepdims=True)
    return scale * (wide - jnp.mean(wide, axis=-1, keepdims=True) - unit * inner)


def gelu_parts(x):
    root = 0.7978845608028654
    square = x * x
    bend = jnp.tanh(root * x * (1.0 + 0.044715 * square))
    half = 0.5 + 0.5 * bend
    slope = half + 0.5 * x * (1.0 - bend * bend) * (root * (1.0 + 0.134145 * square))
    return x * half, slope


class Names:
    pass


def block_kernel(inside, steps, names, *refs):
    n = Names()
    for name, ref in zip(names, refs, strict=True):
        setattr(n, name, ref)
    s = lax.axis_index("section")
    t = lax.axis_index("tensor")
    z = lax.axis_index("dp")
    x = lax.rem(t, 2)
    y = lax.div(t, 2)
    t_y = 2 * (1 - y) + x
    mate = (1 - s, t, z)
    peer_x = (s, 2 * y + 1 - x, z)
    peer_y = (s, t_y, z)
    hub = s == y
    rows_all, width = n.X0.shape
    chunk = rows_all // CHUNKS
    part = chunk // 2
    half = CHUNKS // 2
    heads = n.KT.shape[1]
    tiles = width // TILE
    depth = lax.axis_size("dp")
    slab = width // depth
    q_columns = 2 * heads * HEAD
    o_columns = 3 * heads * HEAD

    def remote(src, dst, send_sem, recv_sem, device):
        return pltpu.make_async_remote_copy(
            src_ref=src,
            dst_ref=dst,
            send_sem=send_sem,
            recv_sem=recv_sem,
            device_id=device,
            device_id_type=MESH,
        )

    def done(ref, sem):
        pltpu.make_async_copy(ref, ref, sem).wait()

    def rows_of(j):
        return pl.ds(pl.multiple_of(j * chunk, chunk), chunk)

    def half_of(j, c):
        return pl.ds(pl.multiple_of(j * chunk + c * part, part), part)

    def own_of(j):
        return pl.ds(pl.multiple_of(j * part, part), part)

    def slab_of(i):
        return pl.ds(pl.multiple_of(i * slab, slab), slab)

    def bytes_of(count):
        return n.PART.at[0, 0:count]

    barrier = pltpu.get_barrier_semaphore()
    greeted = 0
    for other_s in range(2):
        for other in range(CHUNKS):
            greeted += 1

            @pl.when((s != other_s) | (t != other))
            def _():
                pl.semaphore_signal(
                    barrier, inc=1, device_id=(other_s, other, z), device_id_type=MESH
                )

        if inside:
            for other in range(depth):
                greeted += 1

                @pl.when(z != other)
                def _():
                    pl.semaphore_signal(
                        barrier, inc=1, device_id=(other_s, t, other), device_id_type=MESH
                    )

    pl.semaphore_wait(barrier, greeted - 1 - (2 if inside else 0))

    def weights_send(l, p):
        if not inside:
            pltpu.make_async_copy(n.w_whole.at[l, p], n.W.at[l, p], n.w_recv.at[l, p, 0]).start()
            return
        own = (n.own_a, n.own_b, n.own_c)[p]

        @pl.when(s == l)
        def _():
            for far in range(depth):
                @pl.when(hub & (z == far))
                def _():
                    pltpu.make_async_copy(
                        own, n.W.at[l, p, slab_of(z)], n.w_recv.at[l, p, z]
                    ).start()

                @pl.when(jnp.logical_not(hub & (z == far)))
                def _():
                    remote(
                        own,
                        n.W.at[l, p, slab_of(z)],
                        n.w_send.at[p, far],
                        n.w_recv.at[l, p, z],
                        (y, t, far),
                    ).start()

    def weights_sent(p):
        own = (n.own_a, n.own_b, n.own_c)[p]
        for far in range(depth):

            @pl.when(jnp.logical_not(hub & (z == far)))
            def _():
                done(own, n.w_send.at[p, far])

    def weights_relay(l, p):
        if not inside:
            return

        @pl.when(hub)
        def _():
            for step in range(depth):
                far = lax.rem(z + step, depth)
                here = n.W.at[l, p, slab_of(far)]
                done(here, n.w_recv.at[l, p, far])
                remote(
                    here, here, n.relay_send.at[l, p, far], n.w_recv.at[l, p, far], peer_y
                ).start()

    def weights_wait(l, p):
        if not inside:
            done(n.W.at[l, p], n.w_recv.at[l, p, 0])
            return

        @pl.when(jnp.logical_not(hub))
        def _():
            for far in range(depth):
                done(n.W.at[l, p, slab_of(far)], n.w_recv.at[l, p, far])

    def spread(which, source, target):
        pltpu.make_async_copy(
            source.at[y], target.at[rows_of(t)], n.in_recv.at[which, t]
        ).start()
        for other in range(CHUNKS):

            @pl.when(t != other)
            def _():
                remote(
                    source.at[other // 2, half_of(0, s)],
                    target.at[half_of(t, s)],
                    n.in_send.at[which, other],
                    n.in_recv.at[which, t],
                    (s, other, z),
                ).start()

    def spread_pass(which, target, j):
        @pl.when(j == t)
        def _():
            done(target.at[rows_of(j)], n.in_recv.at[which, j])

        @pl.when(j != t)
        def _():
            here = target.at[half_of(j, s)]
            done(here, n.in_recv.at[which, j])
            remote(
                here, here, n.mate_send.at[which, j], n.mate_recv.at[which, j], mate
            ).start()

    def spread_wait(which, target, j):
        @pl.when(j != t)
        def _():
            done(target.at[half_of(j, s)], n.mate_recv.at[which, j])

    def spread_done(which):
        for other in range(CHUNKS):

            @pl.when(t != other)
            def _():
                done(bytes_of(part), n.in_send.at[which, other])
                done(bytes_of(part), n.mate_send.at[which, other])

    def pair_start(stage, ref, j):
        here = ref.at[half_of(j, s)]
        remote(here, here, n.pair_send.at[stage, j], n.pair_recv.at[stage, j], mate).start()

    def pair_wait(stage, j):
        done(bytes_of(part), n.pair_recv.at[stage, j])

    def sum_start(stage, j):
        b = stage % 2
        remote(
            n.PART.at[b, half_of(j, 1 - s)],
            n.RC.at[b, j],
            n.rs_send.at[stage, 0, j],
            n.rs_recv.at[stage, 0, j],
            mate,
        ).start()

    def sum_pass(stage, j):
        b = lax.rem(stage, 2)
        here = half_of(j, s)
        done(n.RC.at[b, j], n.rs_recv.at[stage, 0, j])
        n.PART[b, here, :] = (
            n.PART[b, here, :].astype(F32) + n.RC[b, j].astype(F32)
        ).astype(BF16)
        remote(
            n.PART.at[b, here],
            n.RX.at[b, j],
            n.rs_send.at[stage, 1, j],
            n.rs_recv.at[stage, 1, j],
            peer_x,
        ).start()
        done(n.RC.at[b, j], n.rs_send.at[stage, 0, j])

    def sum_wait(stage, j):
        b = stage % 2
        done(n.RX.at[b, j], n.rs_recv.at[stage, 1, j])
        total = n.PART[b, half_of(j, s), :].astype(F32) + n.RX[b, j].astype(F32)
        done(n.RX.at[b, j], n.rs_send.at[stage, 1, j])
        return total

    key_index = lax.broadcasted_iota(jnp.int32, (chunk, chunk), 0)
    query_index = lax.broadcasted_iota(jnp.int32, (chunk, chunk), 1)
    causal = key_index <= query_index

    def scores(l, st, i, j, diagonal):
        if l == 0:
            grown = st * st + 1.0
            inverse = lax.rsqrt(grown)
            magnitude = grown * inverse
            sign = st * inverse
        else:
            inverse, magnitude, sign = None, st, None
        if diagonal:
            magnitude = jnp.where(causal, magnitude, MASKED)
        else:
            apart = (j >= half) & (i < half)
            magnitude = magnitude + jnp.where(apart, n.bias[0:1, 0:chunk], 0.0)
        return inverse, magnitude, sign

    def norm_qkv(l, j):
        rows = rows_of(j)
        if l == 0:
            spread_wait(0, n.X0, j)
        else:
            pair_wait(PAIR_MIDDLE, j)
        source = n.X0 if l == 0 else n.Y0

        @pl.loop(0, 4)
        def _(i):
            some = pl.ds(pl.multiple_of(j * chunk + i * (chunk // 4), chunk // 4), chunk // 4)
            unit, _ = unit_rows(source[some, :].astype(F32))
            n.N1[l, some, :] = (unit * n.GAINS[2 * l : 2 * l + 1, :]).astype(BF16)

        kv = nn(n.N1[l, rows, :], n.W[l, 0, :, 0:q_columns])
        kv_low = kv.astype(BF16)
        turned = kv.T.astype(BF16)
        for h in range(heads):
            n.KV[l, h, rows, :] = kv_low[:, 2 * h * HEAD : 2 * (h + 1) * HEAD]
            n.KT[l, h, :, rows] = turned[2 * h * HEAD : (2 * h + 1) * HEAD]
            n.VT[h, :, rows] = turned[(2 * h + 1) * HEAD : (2 * h + 2) * HEAD]
        q = nn(n.N1[l, rows, :], n.W[l, 0, :, q_columns:o_columns]).astype(BF16)
        blank = jnp.zeros((chunk, HEAD), BF16)
        for h in range(heads):
            q_h = q[:, h * HEAD : (h + 1) * HEAD] * jnp.asarray(HEAD**-0.5, BF16)
            n.Q[l, h, rows, :] = jnp.concatenate([q_h, blank], axis=1)

    def attend(l, j, h):
        rows = rows_of(j)
        query = n.Q[l, h, rows, :]

        def block(i, carry, diagonal):
            top, total, out = carry
            keys = rows_of(i)
            st = nt(n.KV[l, h, keys, :], query)
            _, magnitude, sign = scores(l, st, i, j, diagonal)
            new_top = jnp.maximum(top, jnp.max(magnitude, axis=0, keepdims=True))
            weights = jnp.exp(magnitude - new_top)
            shrink = jnp.exp(top - new_top)
            total = total * shrink + jnp.sum(weights, axis=0, keepdims=True)
            signed = weights if l == 1 else sign * weights
            out = out * shrink + nn(n.VT[h, :, keys], signed.astype(BF16))
            return new_top, total, out

        carry = (
            jnp.full((1, chunk), MASKED, F32),
            jnp.zeros((1, chunk), F32),
            jnp.zeros((HEAD, chunk), F32),
        )
        carry = block(j, carry, True)
        top, total, out = lax.fori_loop(0, j, lambda i, c: block(i, c, False), carry)
        n.ATTT[l, h, :, rows] = out / total
        n.LSE[l, h, :, rows] = top + jnp.log(total)

    def out_product(l, j):
        rows = rows_of(j)
        joined = jnp.concatenate(
            [jnp.zeros((HEAD, chunk), F32)] + [n.ATTT[l, h, :, rows] for h in range(heads)],
            axis=0,
        )
        n.ATT[l, rows, :] = joined.T.astype(BF16)
        for i in range(tiles):
            here = slice(i * TILE, (i + 1) * TILE)
            n.PART[0, rows, here] = nt(
                n.ATT[l, rows, :], n.W[l, 0, here, o_columns - HEAD : width]
            ).astype(BF16)
        sum_start(SUM_ATTN[l], j)

    def attn_sum(l, j):
        source = n.X0 if l == 0 else n.Y0
        own = half_of(j, s)
        middle = source[own, :].astype(F32) + sum_wait(SUM_ATTN[l], j)
        n.MID[l, own_of(j), :] = middle
        unit, _ = unit_rows(middle)
        n.N2[l, own, :] = (unit * n.GAINS[2 * l + 1 : 2 * l + 2, :]).astype(BF16)
        pair_start(PAIR_N2[l], n.N2.at[l], j)

    def up_product(l, j):
        rows = rows_of(j)
        pair_wait(PAIR_N2[l], j)
        for i in range(tiles):
            here = slice(i * TILE, (i + 1) * TILE)
            pre = nn(n.N2[l, rows, :], n.W[l, 1, :, here])
            n.PRE[l, rows, here] = pre.astype(BF16)
            n.HID[rows, here] = gelu_parts(pre)[0].astype(BF16)

    def down_product(l, j):
        rows = rows_of(j)
        for i in range(tiles):
            here = slice(i * TILE, (i + 1) * TILE)
            n.PART[1, rows, here] = nt(n.HID[rows, :], n.W[l, 2, here, :]).astype(BF16)
        sum_start(SUM_MLP[l], j)

    def mlp_sum(l, j):
        result = n.MID[l, own_of(j), :] + sum_wait(SUM_MLP[l], j)
        if l == 0:
            n.Y0[half_of(j, s), :] = result.astype(BF16)
            pair_start(PAIR_MIDDLE, n.Y0, j)
        else:
            n.PART[1, half_of(j, s), :] = result.astype(BF16)
            last_out(0, 1, n.acts, j)

    def last_out(which, section, out, j):
        here = n.PART.at[1, half_of(j, s)]
        target = out.at[y, half_of(0, s)]

        @pl.when((s == section) & (t == j))
        def _():
            copy = pltpu.make_async_copy(here, target, n.out_send.at[which, j])
            copy.start()
            copy.wait()

        @pl.when((lax.rem(j, 2) == x) & ((s != section) | (t != j)))
        def _():
            remote(
                here,
                target,
                n.out_send.at[which, j],
                n.out_recv.at[which, y, s],
                (section, j, z),
            ).start()

    def last_out_sent(which, section, j):
        @pl.when((lax.rem(j, 2) == x) & ((s != section) | (t != j)))
        def _():
            done(bytes_of(part), n.out_send.at[which, j])

    def last_out_done(which, section, out):
        @pl.when(s == section)
        def _():
            for m in range(2):
                for c in range(2):

                    @pl.when((y != m) | (s != c))
                    def _():
                        done(bytes_of(part), n.out_recv.at[which, m, c])

    def full_out(which, section, ref, out):
        @pl.when(s == section)
        def _():
            pltpu.make_async_copy(
                ref.at[rows_of(t)], out.at[y], n.full_recv.at[which, y]
            ).start()
            remote(
                ref.at[rows_of(t_y)],
                out.at[y],
                n.full_send.at[which],
                n.full_recv.at[which, y],
                peer_y,
            ).start()

    def full_out_done(which, section):
        @pl.when(s == section)
        def _():
            done(bytes_of(chunk), n.full_recv.at[which, 0])
            done(bytes_of(chunk), n.full_recv.at[which, 1])
            done(bytes_of(chunk), n.full_send.at[which])

    def hidden_back(l, j):
        rows = rows_of(j)
        if l == 1:
            spread_wait(1, n.CT, j)
        else:
            pair_wait(PAIR_DR, j)
        source = n.CT if l == 1 else n.DR
        for i in range(tiles):
            here = slice(i * TILE, (i + 1) * TILE)
            back = nn(source[rows, :], n.W[l, 2, :, here])
            hidden, slope = gelu_parts(n.PRE[l, rows, here].astype(F32))
            n.HID[rows, here] = hidden.astype(BF16)
            n.DPRE[rows, here] = (slope * back).astype(BF16)

    def up_back(l, j):
        rows = rows_of(j)
        for i in range(tiles):
            here = slice(i * TILE, (i + 1) * TILE)
            n.PART[0, rows, here] = nt(n.DPRE[rows, :], n.W[l, 1, here, :]).astype(BF16)
        sum_start(SUM_DMLP[l], j)

    def mlp_back_sum(l, j):
        total = sum_wait(SUM_DMLP[l], j)
        source = n.CT if l == 1 else n.DR
        own = half_of(j, s)
        unit, scale = unit_rows(n.MID[l, own_of(j), :])
        n.GACC[l, 1:2, :] += jnp.sum(total * unit, axis=0, keepdims=True)
        gain = n.GAINS[2 * l + 1 : 2 * l + 2, :]
        grad = source[own, :].astype(F32) + norm_back(unit, scale, gain, total)
        n.DMID[own_of(j), :] = grad
        n.DA[l, own, :] = grad.astype(BF16)
        pair_start(PAIR_DA[l], n.DA.at[l], j)

    def attn_grad(l, j):
        rows = rows_of(j)
        pair_wait(PAIR_DA[l], j)

        @pl.when(j == CHUNKS - 1)
        def _():
            n.DKV[...] = jnp.zeros_like(n.DKV)

        back = nn(n.DA[l, rows, :], n.W[l, 0, :, o_columns - HEAD : width])
        low = back.astype(BF16)
        turned = low.astype(F32).T
        blank = jnp.zeros((chunk, HEAD), BF16)
        for h in range(heads):
            here = slice((h + 1) * HEAD, (h + 2) * HEAD)
            n.GRAD[h] = jnp.concatenate([blank, low[:, here]], axis=1)
            inner = jnp.sum(turned[here] * n.ATTT[l, h, :, rows], axis=0, keepdims=True)
            n.GRADT[h] = inner

    def attend_back(l, j, h):
        rows = rows_of(j)
        query = n.Q[l, h, rows, :]
        grad = n.GRAD[h]
        inner = n.GRADT[h]
        log_total = n.LSE[l, h, :, rows]

        def block(i, query_grad, diagonal):
            keys = rows_of(i)
            kv = n.KV[l, h, keys, :]
            st = nt(kv, query)
            dp = nt(kv, grad)
            inverse, magnitude, sign = scores(l, st, i, j, diagonal)
            weights = jnp.exp(magnitude - log_total)
            if l == 0:
                signed = sign * weights
                ds = weights * (sign * (sign * dp - inner) + dp * (inverse * inverse * inverse))
            else:
                signed = weights
                ds = weights * (dp - inner)
            ds = ds.astype(BF16)
            n.DKV[h, keys, :] += nn(ds, query) + nn(signed.astype(BF16), grad)
            return query_grad + nn(n.KT[l, h, :, keys], ds)

        query_grad = block(j, jnp.zeros((HEAD, chunk), F32), True)
        query_grad = lax.fori_loop(0, j, lambda i, c: block(i, c, False), query_grad)
        n.DQT[h] = query_grad * HEAD**-0.5

    def qkv_back(l, j):
        rows = rows_of(j)
        turned = jnp.concatenate([n.DQT[h] for h in range(heads)], axis=0).T
        for h in range(heads):
            n.DQKV[rows, 2 * h * HEAD : 2 * (h + 1) * HEAD] = n.DKV[h, rows, :].astype(BF16)
        n.DQKV[rows, q_columns:] = turned.astype(BF16)
        if l == 1:
            last_out_sent(0, 1, j)
        for i in range(tiles):
            here = slice(i * TILE, (i + 1) * TILE)
            n.PART[1, rows, here] = nt(n.DQKV[rows, :], n.W[l, 0, here, 0:o_columns]).astype(
                BF16
            )
        sum_start(SUM_DATTN[l], j)

    def attn_back_sum(l, j):
        total = sum_wait(SUM_DATTN[l], j)
        source = n.X0 if l == 0 else n.Y0
        own = half_of(j, s)
        unit, scale = unit_rows(source[own, :].astype(F32))
        n.GACC[l, 0:1, :] += jnp.sum(total * unit, axis=0, keepdims=True)
        gain = n.GAINS[2 * l : 2 * l + 1, :]
        result = n.DMID[own_of(j), :] + norm_back(unit, scale, gain, total)
        if l == 1:
            n.DR[own, :] = result.astype(BF16)
            pair_start(PAIR_DR, n.DR, j)
        else:
            n.PART[1, own, :] = result.astype(BF16)
            last_out(1, 0, n.igr, j)

    long = width // 2
    grad_order = ((1, 2), (1, 1), (1, 0), (0, 2), (0, 1), (0, 0))
    grad_to = 2 * s + x

    def kept_here(l):
        return hub & (s == l)

    def grad_sent(l, p, i):
        if not inside:
            done(n.STG.at[i], n.stg_send.at[l, p, i])
            return

        @pl.when(jnp.logical_not(kept_here(l)))
        def _():
            done(n.STG.at[i], n.stg_send.at[l, p, i])

    def weight_grad(l, p, i):
        at = grad_order.index((l, p))
        if at > 0:
            grad_sent(*grad_order[at - 1], i)
        rows = pl.ds(pl.multiple_of(i * long, long), long)
        if p == 0:
            left = n.N1[l, :, rows]
            n.STG[i, :, 0:256] = tn(left, n.DQKV[:, 0:256]).astype(BF16)
            n.STG[i, :, 256:512] = tn(left, n.DQKV[:, 256:512]).astype(BF16)
            last = tn(left, n.DQKV[:, 512:o_columns])
            out_part = tn(n.DA[l, :, rows], n.ATT[l])
            n.STG[i, :, 512:width] = jnp.concatenate([last, out_part[:, HEAD:]], axis=1).astype(
                BF16
            )
        else:
            if p == 1:
                left, right = n.N2[l, :, rows], n.DPRE
            else:
                left, right = (n.CT if l == 1 else n.DR)[:, rows], n.HID
            for k in range(tiles):
                here = slice(k * TILE, (k + 1) * TILE)
                n.STG[i, :, here] = tn(left, right[:, here]).astype(BF16)
        if not inside:
            pltpu.make_async_copy(
                n.STG.at[i], n.grads.at[l, p, rows], n.stg_send.at[l, p, i]
            ).start()
            return

        @pl.when(kept_here(l))
        def _():
            n.GR[0, p, rows, :] = n.STG[i]

        @pl.when(jnp.logical_not(kept_here(l)))
        def _():
            way = jnp.where(hub, 0, 1)
            remote(
                n.STG.at[i],
                n.GR.at[way, p, rows],
                n.stg_send.at[l, p, i],
                n.gr_recv.at[way, p, i],
                (l, grad_to, z),
            ).start()

    def slot_of(source, target):
        return jnp.where(source > target, source - 1, source)

    def grad_pass(l, p, i):
        if not inside:
            return

        @pl.when(s == l)
        def _():
            rows = pl.ds(pl.multiple_of(i * long, long), long)

            @pl.when(jnp.logical_not(hub))
            def _():
                done(n.GR.at[0, p, rows], n.gr_recv.at[0, p, i])

            done(n.GR.at[1, p, rows], n.gr_recv.at[1, p, i])
            for k in range(depth // 2):
                far = i * (depth // 2) + k

                @pl.when(z != far)
                def _():
                    here = slab_of(far)
                    n.GR[0, p, here, :] = (
                        n.GR[0, p, here, :].astype(F32) + n.GR[1, p, here, :].astype(F32)
                    ).astype(BF16)
                    slot = slot_of(z, far)
                    remote(
                        n.GR.at[0, p, here],
                        n.ZR.at[slot, p],
                        n.z_send.at[p, far],
                        n.z_recv.at[p, slot],
                        (s, t, far),
                    ).start()

    def grad_final(l, p):
        if not inside:
            return

        @pl.when(s == l)
        def _():
            here = slab_of(z)
            total = n.GR[0, p, here, :].astype(F32) + n.GR[1, p, here, :].astype(F32)
            for slot in range(depth - 1):
                done(n.ZR.at[slot, p], n.z_recv.at[p, slot])
                total = total + n.ZR[slot, p].astype(F32)
            n.FIN[p] = total
            pltpu.make_async_copy(n.FIN.at[p], n.gsum.at[p], n.fin_send.at[p]).start()

    def grads_done():
        if not inside:
            grad_sent(*grad_order[-1], 0)
            grad_sent(*grad_order[-1], 1)
            return
        grad_sent(*grad_order[-1], 0)
        grad_sent(*grad_order[-1], 1)
        for p in range(PARTS):
            for far in range(depth):

                @pl.when(z != far)
                def _():
                    done(n.ZR.at[0, p], n.z_send.at[p, far])

            done(n.FIN.at[p], n.fin_send.at[p])

    def gains_send():
        if not inside:
            n.GAINS[...] = n.gain_rows[...]
            return
        n.GIN[s, z] = n.gain_rows[...]
        for c in range(2):
            for far in range(depth):

                @pl.when((s != c) | (z != far))
                def _():
                    remote(
                        n.gain_rows,
                        n.GIN.at[s, z],
                        n.gin_send.at[c, far],
                        n.gin_recv.at[s, z],
                        (c, t, far),
                    ).start()

    def gains_wait():
        if not inside:
            return
        for c in range(2):
            for far in range(depth):

                @pl.when((s != c) | (z != far))
                def _():
                    done(n.gain_rows, n.gin_recv.at[c, far])
                    done(n.gain_rows, n.gin_send.at[c, far])

                for k in range(2):
                    n.GAINS[2 * c + k : 2 * c + k + 1, far * slab : (far + 1) * slab] = n.GIN[
                        c, far, k : k + 1, 0:slab
                    ]

    def gain_grads():
        if not inside:
            n.gain_out[...] = jnp.concatenate([n.GACC[0, 0:2], n.GACC[1, 0:2], n.GACC[0, 4:8]])
            return
        remote(n.GACC.at[1 - s], n.GC, n.gg_send.at[0], n.gg_recv.at[0], mate).start()
        done(n.GC, n.gg_recv.at[0])
        n.GACC[s] += n.GC[...]
        remote(n.GACC.at[s], n.GY, n.gg_send.at[1], n.gg_recv.at[1], peer_y).start()
        done(n.GY, n.gg_recv.at[1])
        n.GC[...] = n.GACC[s] + n.GY[...]
        for far in range(depth):

            @pl.when(z != far)
            def _():
                slot = slot_of(z, far)
                remote(
                    n.GC, n.GZ.at[slot], n.gg_send.at[2 + far], n.gg_recv.at[2 + slot], (s, t, far)
                ).start()

    def gain_grads_done():
        if not inside:
            return
        total = n.GC[...]
        for slot in range(depth - 1):
            done(n.GZ.at[slot], n.gg_recv.at[2 + slot])
            total = total + n.GZ[slot]
        n.gain_out[...] = total
        done(n.GC, n.gg_send.at[0])
        done(n.GC, n.gg_send.at[1])
        for far in range(depth):

            @pl.when(z != far)
            def _():
                done(n.GC, n.gg_send.at[2 + far])

    tasks = {"none": lambda h, j: None}
    for l in range(2):
        tasks[f"nq{l}"] = lambda h, j, l=l: norm_qkv(l, j)
        tasks[f"at{l}"] = lambda h, j, l=l: attend(l, j, h)
        tasks[f"op{l}"] = lambda h, j, l=l: out_product(l, j)
        tasks[f"sa{l}"] = lambda h, j, l=l: attn_sum(l, j)
        tasks[f"up{l}"] = lambda h, j, l=l: up_product(l, j)
        tasks[f"dn{l}"] = lambda h, j, l=l: down_product(l, j)
        tasks[f"sm{l}"] = lambda h, j, l=l: mlp_sum(l, j)
        tasks[f"hb{l}"] = lambda h, j, l=l: hidden_back(l, j)
        tasks[f"ub{l}"] = lambda h, j, l=l: up_back(l, j)
        tasks[f"sd{l}"] = lambda h, j, l=l: mlp_back_sum(l, j)
        tasks[f"ag{l}"] = lambda h, j, l=l: attn_grad(l, j)
        tasks[f"ab{l}"] = lambda h, j, l=l: attend_back(l, j, h)
        tasks[f"qb{l}"] = lambda h, j, l=l: qkv_back(l, j)
        tasks[f"sb{l}"] = lambda h, j, l=l: attn_back_sum(l, j)
        for p in range(PARTS):
            tasks[f"wg{l}{p}"] = lambda h, j, l=l, p=p: weight_grad(l, p, j)
    for p in range(PARTS):
        tasks[f"ws{p}"] = lambda h, j, p=p: weights_send(1, p)
    tasks["r"] = lambda h, j: sum_pass(h, j)
    tasks["x0"] = lambda h, j: spread_pass(0, n.X0, j)
    tasks["x1"] = lambda h, j: spread_pass(1, n.CT, j)
    tasks["wr"] = lambda h, j: weights_relay(h, j)
    tasks["ww"] = lambda h, j: weights_wait(h, j)
    tasks["gp"] = lambda h, j: grad_pass(lax.div(j, 2), h, lax.rem(j, 2))
    tasks["gf"] = lambda h, j: grad_final(j, h)
    tasks["fy"] = lambda h, j: full_out(0, 0, n.Y0, n.acts)
    tasks["fd"] = lambda h, j: full_out(1, 1, n.DR, n.igr)
    tasks["gw"] = lambda h, j: gains_wait()
    tasks["cs"] = lambda h, j: spread(1, n.cot, n.CT)
    order = list(tasks)
    run = [tasks[name] for name in order]

    weights_send(0, 0)
    gains_send()
    spread(0, n.inp, n.X0)
    weights_send(0, 1)
    weights_send(0, 2)
    n.GACC[...] = jnp.zeros_like(n.GACC)

    group = 12
    codes = [order.index(name) * 32 + h * 4 + j for name, h, j in steps]
    codes += [0] * (-len(codes) % group)
    pairs = [codes[i] + 4096 * codes[i + 1] for i in range(0, len(codes), 2)]
    per_group = group // 2
    groups = len(pairs) // per_group

    def pick(index, values):
        value = values[0]
        for at in range(1, len(values)):
            value = jnp.where(index == at, values[at], value)
        return value

    def dispatch(low, high, op, h, j):
        if high - low == 1:
            run[low](h, j)
            return
        middle = (low + high) // 2
        lax.cond(
            op < middle,
            lambda: dispatch(low, middle, op, h, j),
            lambda: dispatch(middle, high, op, h, j),
        )

    @pl.loop(0, groups)
    def _(g):
        words = [
            pick(g, [pairs[q * per_group + w] for q in range(groups)]) for w in range(per_group)
        ]

        @pl.loop(0, group)
        def _(i):
            word = pick(lax.div(i, 2), words)
            code = jnp.where(lax.rem(i, 2) == 0, lax.rem(word, 4096), lax.div(word, 4096))
            dispatch(
                0, len(run), lax.div(code, 32), lax.rem(lax.div(code, 4), 8), lax.rem(code, 4)
            )

    gain_grads()

    if inside:
        for p in range(PARTS):
            weights_sent(p)
            for l in range(2):

                @pl.when(hub)
                def _():
                    for far in range(depth):
                        done(n.W.at[l, p, slab_of(far)], n.relay_send.at[l, p, far])

    spread_done(0)
    spread_done(1)

    @pl.loop(0, CHUNKS)
    def _(j):
        for stage in range(6):
            done(bytes_of(part), n.pair_send.at[stage, j])
        last_out_sent(1, 0, j)

    full_out_done(0, 0)
    full_out_done(1, 1)
    last_out_done(0, 1, n.acts)
    last_out_done(1, 0, n.igr)
    grads_done()
    gain_grads_done()


def schedule():
    steps = []

    def add(name, j=0, h=0):
        steps.append((name, h, j))

    def when(name, j, h=0):
        if 0 <= j < CHUNKS:
            add(name, j, h)

    def back(name, j, h=0):
        if 0 <= j < CHUNKS:
            add(name, CHUNKS - 1 - j, h)

    add("gw")
    add("wr", 0, 0)
    for k in range(11):
        for l in range(2):
            when("r", k - 4 * l - 1, SUM_ATTN[l])
            when("r", k - 4 * l - 3, SUM_MLP[l])
        if k < CHUNKS:
            add("x0", k)
            if k == 0:
                add("ww", 0, 0)
        for l in range(2):
            if l == 1 and k == 4:
                add("wr", 0, 1)
                add("ww", 0, 1)
            for name in ("nq", "at", "op"):
                for h in range(3 if name == "at" else 1):
                    when(f"{name}{l}", k - 4 * l, h)
            if l == 0:
                for m in range(2):
                    when(f"sa{m}", k - 4 * m - 1)
                if k == 0:
                    add("wr", 1, 0)
                if k == 1:
                    add("wr", 2, 0)
                    for p in range(PARTS):
                        add(f"ws{p}")
                    add("cs")
                if k == 2:
                    add("ww", 1, 0)
                    add("ww", 2, 0)
                when("up0", k - 2)
                when("dn0", k - 2)
                for m in range(2):
                    when(f"sm{m}", k - 4 * m - 3)
        if k == 5:
            add("wr", 1, 1)
            add("wr", 2, 1)
        if k == 6:
            add("ww", 1, 1)
            add("ww", 2, 1)
            for j in range(CHUNKS):
                add("x1", j)
        when("up1", k - 6)
        when("dn1", k - 6)
        if k == 8:
            add("fy")
    for k in range(11):
        for l in (1, 0):
            lag = 4 * (1 - l)
            back("r", k - lag - 1, SUM_DMLP[l])
            back("r", k - lag - 3, SUM_DATTN[l])
        back("hb1", k)
        back("ub1", k)
        for l in (1, 0):
            back(f"sd{l}", k - 4 * (1 - l) - 1)
        back("ag1", k - 2)
        for h in range(3):
            back("ab1", k - 2, h)
        back("qb1", k - 2)
        for l in (1, 0):
            back(f"sb{l}", k - 4 * (1 - l) - 3)
        if k == 4:
            for p in (2, 1):
                add(f"wg1{p}", 0)
                add(f"wg1{p}", 1)
        back("hb0", k - 4)
        back("ub0", k - 4)
        if k == 6:
            add("wg10", 0)
            add("wg10", 1)
            for p in (2, 1):
                add("gp", 2, p)
                add("gp", 3, p)
        back("ag0", k - 6)
        for h in range(3):
            back("ab0", k - 6, h)
        back("qb0", k - 6)
        if k == 8:
            add("fd")
            for p in (2, 1):
                add(f"wg0{p}", 0)
                add(f"wg0{p}", 1)
            add("gp", 2, 0)
            add("gp", 3, 0)
            add("gf", 1, 2)
            add("gf", 1, 1)
    add("wg00", 0)
    add("wg00", 1)
    for p in (2, 1):
        add("gp", 0, p)
        add("gp", 1, p)
    add("gp", 0, 0)
    add("gp", 1, 0)
    add("gf", 1, 0)
    for p in (2, 1, 0):
        add("gf", 0, p)
    return steps


def run_blocks(inputs, cotangent, weights, gain_rows, bias, depth, inside):
    buckets, chunk, width = inputs.shape
    rows = CHUNKS * chunk
    part = chunk // 2
    heads = width // 4 // HEAD
    vmem, dma = pltpu.VMEM, pltpu.SemaphoreType.DMA
    scratch = dict(
        W=vmem((2, PARTS, width, width), BF16),
        X0=vmem((rows, width), BF16),
        Y0=vmem((rows, width), BF16),
        CT=vmem((rows, width), BF16),
        DR=vmem((rows, width), BF16),
        N1=vmem((2, rows, width), BF16),
        N2=vmem((2, rows, width), BF16),
        Q=vmem((2, heads, rows, 2 * HEAD), BF16),
        KV=vmem((2, heads, rows, 2 * HEAD), BF16),
        KT=vmem((2, heads, HEAD, rows), BF16),
        VT=vmem((heads, HEAD, rows), BF16),
        ATT=vmem((2, rows, (heads + 1) * HEAD), BF16),
        ATTT=vmem((2, heads, HEAD, rows), F32),
        LSE=vmem((2, heads, 1, rows), F32),
        PRE=vmem((2, rows, width), BF16),
        HID=vmem((rows, width), BF16),
        DPRE=vmem((rows, width), BF16),
        DQKV=vmem((rows, 3 * heads * HEAD), BF16),
        DA=vmem((2, rows, width), BF16),
        DKV=vmem((heads, rows, 2 * HEAD), F32),
        GRAD=vmem((heads, chunk, 2 * HEAD), BF16),
        GRADT=vmem((heads, 1, chunk), F32),
        DQT=vmem((heads, HEAD, chunk), F32),
        MID=vmem((2, CHUNKS * part, width), F32),
        DMID=vmem((CHUNKS * part, width), F32),
        PART=vmem((2, rows, width), BF16),
        RC=vmem((2, CHUNKS, part, width), BF16),
        RX=vmem((2, CHUNKS, part, width), BF16),
        STG=vmem((2, width // 2, width), BF16),
        GAINS=vmem((8, width), F32),
        GACC=vmem((2, 8, width), F32),
        in_send=dma((2, CHUNKS)),
        in_recv=dma((2, CHUNKS)),
        mate_send=dma((2, CHUNKS)),
        mate_recv=dma((2, CHUNKS)),
        pair_send=dma((6, CHUNKS)),
        pair_recv=dma((6, CHUNKS)),
        rs_send=dma((8, 2, CHUNKS)),
        rs_recv=dma((8, 2, CHUNKS)),
        w_recv=dma((2, PARTS, depth if inside else 1)),
        stg_send=dma((2, PARTS, 2)),
        out_send=dma((2, CHUNKS)),
        out_recv=dma((2, 2, 2)),
        full_send=dma((2,)),
        full_recv=dma((2, 2)),
    )
    outs = dict(
        acts=jax.ShapeDtypeStruct(inputs.shape, BF16), igr=jax.ShapeDtypeStruct(inputs.shape, BF16)
    )
    if inside:
        slab = width // depth
        scratch.update(
            GR=vmem((2, PARTS, width, width), BF16),
            ZR=vmem((depth - 1, PARTS, slab, width), BF16),
            FIN=vmem((PARTS, slab, width), F32),
            GIN=vmem((2, depth) + gain_rows.shape, F32),
            GC=vmem((8, width), F32),
            GY=vmem((8, width), F32),
            GZ=vmem((depth - 1, 8, width), F32),
            w_send=dma((PARTS, depth)),
            relay_send=dma((2, PARTS, depth)),
            gr_recv=dma((2, PARTS, 2)),
            z_send=dma((PARTS, depth)),
            z_recv=dma((PARTS, depth - 1)),
            fin_send=dma((PARTS,)),
            gin_send=dma((2, depth)),
            gin_recv=dma((2, depth)),
            gg_send=dma((2 + depth,)),
            gg_recv=dma((1 + depth,)),
        )
        own = dict(own_a=weights[0], own_b=weights[1], own_c=weights[2])
        outs["gsum"] = jax.ShapeDtypeStruct((PARTS, slab, width), F32)
    else:
        own = dict(w_whole=weights)
        outs["grads"] = jax.ShapeDtypeStruct(weights.shape, BF16)
    outs["gain_out"] = jax.ShapeDtypeStruct((8, width), F32)
    given = dict(inp=inputs, cot=cotangent, **own, gain_rows=gain_rows, bias=bias)
    hbm = pl.BlockSpec(memory_space=pl.ANY)
    in_vmem = pl.BlockSpec(memory_space=pltpu.VMEM)
    small = ("gain_rows", "bias", "gain_out")
    return pl.pallas_call(
        functools.partial(
            block_kernel, inside, schedule(), list(given) + list(outs) + list(scratch)
        ),
        out_shape=tuple(outs.values()),
        in_specs=[in_vmem if name in small else hbm for name in given],
        out_specs=tuple(in_vmem if name in small else hbm for name in outs),
        scratch_shapes=list(scratch.values()),
        compiler_params=pltpu.CompilerParams(
            collective_id=0, has_side_effects=True, vmem_limit_bytes=VMEM_LIMIT
        ),
        cost_estimate=pl.CostEstimate(
            flops=27_000_000_000, bytes_accessed=40_000_000, transcendentals=20_000_000
        ),
        name="blocks",
    )(*given.values())


def shards(inputs, lengths, gains, w_qkv, w_out, w_up, w_down, cotangent):
    local_rows, width = inputs.shape[1:]
    slab = w_up.shape[1]
    heads = w_qkv.shape[3] // HEAD
    depth = lax.axis_size("dp")
    y = lax.div(lax.axis_index("tensor"), 2)
    section = lax.axis_index("section")
    inside = slab % 16 == 0 and depth % 2 == 0
    split = (slab, heads, HEAD)
    kv = jnp.stack([w_qkv[0, :, 1].reshape(split), w_qkv[0, :, 2].reshape(split)], axis=2)
    own = (
        jnp.concatenate([kv.reshape(slab, -1), w_qkv[0, :, 0], w_out[0].T], axis=1),
        w_up[0],
        w_down[0].T,
    )
    bias = jnp.where(lengths[y] == CHUNKS * local_rows, 0.0, MASKED).astype(F32)
    bias = jnp.broadcast_to(bias, (8, local_rows))
    axes = ("section", "tensor")
    if inside:
        gain_rows = jnp.pad(gains[0].astype(F32), ((0, 6), (0, -slab % 128)))
        acts, input_grads, total, gain_part = run_blocks(
            inputs, cotangent, own, gain_rows, bias, depth, inside
        )
        gain_part = gain_part[None, :2]
        at = lax.axis_index("tensor") * depth + lax.axis_index("dp")
        share = width // (depth * lax.axis_size("tensor"))
        gain_grads = lax.dynamic_slice_in_dim(gain_part, at * share, share, 2)
    else:
        whole = lax.all_gather(jnp.stack(own), "dp", axis=1, tiled=True)
        weights = []
        for l in range(2):
            parts = []
            for to_y in range(2):
                pairs = [
                    (4 * l + 2 * c + x, 4 * c + 2 * to_y + x) for c in range(2) for x in range(2)
                ]
                parts.append(lax.ppermute(whole, axes, pairs))
            weights.append(jnp.where(y == 0, parts[0], parts[1]))
        weights = jnp.stack(weights)
        gain_rows = lax.all_gather(gains, "dp", axis=2, tiled=True)
        gain_rows = lax.all_gather(gain_rows, "section", axis=0, tiled=True)
        gain_rows = jnp.pad(gain_rows.reshape(4, width).astype(F32), ((0, 4), (0, 0)))
        acts, input_grads, partial, gain_part = run_blocks(
            inputs, cotangent, weights, gain_rows, bias, depth, inside
        )
        total = jnp.zeros(partial.shape[1:], F32)
        for l in range(2):
            for from_y in range(2):
                pairs = [
                    (4 * c + 2 * from_y + x, 4 * l + 2 * c + x) for c in range(2) for x in range(2)
                ]
                total = total + lax.ppermute(partial[l], axes, pairs).astype(F32)
        total = lax.psum_scatter(total.astype(BF16), "dp", scatter_dimension=1, tiled=True)
        total = total.astype(F32)
        gain_part = lax.psum(gain_part[:4].reshape(2, 2, width), "section")
        gain_part = lax.dynamic_slice_in_dim(gain_part, section, 1, 0)
        gain_grads = 0.5 * lax.psum_scatter(
            gain_part, ("tensor", "dp"), scatter_dimension=2, tiled=True
        )
    columns = heads * HEAD
    kv = total[0, :, : 2 * columns].reshape(slab, heads, 2, HEAD)
    q = total[0, :, 2 * columns : 3 * columns]
    qkv_grads = jnp.stack([q, kv[:, :, 0].reshape(q.shape), kv[:, :, 1].reshape(q.shape)], axis=1)
    return (
        acts[None],
        input_grads[None],
        gain_grads,
        qkv_grads[None],
        total[0, :, 3 * columns :].T[None],
        total[1][None],
        total[2].T[None],
    )


def solution(mesh):
    in_specs = (
        P("dp", "tensor", None),
        P("dp"),
        P("section", None, "dp"),
        P("section", "dp", None, "tensor"),
        P("section", "tensor", "dp"),
        P("section", "dp", "tensor"),
        P("section", "tensor", "dp"),
        P("dp", "tensor", None),
    )
    out_specs = (
        P("section", "dp", "tensor", None),
        P("section", "dp", "tensor", None),
        P("section", None, ("tensor", "dp")),
        P("section", "dp", None, "tensor"),
        P("section", "tensor", "dp"),
        P("section", "dp", "tensor"),
        P("section", "tensor", "dp"),
    )
    return jax.shard_map(shards, mesh=mesh, in_specs=in_specs, out_specs=out_specs, check_vma=False)
```

```python
import functools

import jax
import jax.numpy as jnp
from jax import lax
from jax.experimental import pallas as pl
from jax.experimental.pallas import tpu as pltpu
from jax.sharding import PartitionSpec as P

HEAD = 64
EPSILON = 1e-05
MASKED = -1e30
CHUNKS = 4
PARTS = 3
VMEM_LIMIT = 63 << 20
TILE = 256
BF16 = jnp.bfloat16
F32 = jnp.float32
MESH = pl.DeviceIdType.MESH

SUM_ATTN = (0, 2)
SUM_MLP = (1, 3)
SUM_DMLP = (6, 4)
SUM_DATTN = (7, 5)
PAIR_N2 = (0, 1)
PAIR_MIDDLE = 2
PAIR_DA = (4, 3)
PAIR_DR = 5


def nn(left, right):
    return lax.dot_general(left, right, (((1,), (0,)), ((), ())), preferred_element_type=F32)


def nt(left, right):
    return lax.dot_general(left, right, (((1,), (1,)), ((), ())), preferred_element_type=F32)


def tn(left, right):
    return lax.dot_general(left, right, (((0,), (0,)), ((), ())), preferred_element_type=F32)


def unit_rows(rows):
    centre = rows - jnp.mean(rows, axis=-1, keepdims=True)
    spread = jnp.mean(centre * centre, axis=-1, keepdims=True)
    scale = lax.rsqrt(spread + EPSILON)
    return centre * scale, scale


def norm_back(unit, scale, gain, grad):
    wide = grad * gain
    inner = jnp.mean(wide * unit, axis=-1, keepdims=True)
    return scale * (wide - jnp.mean(wide, axis=-1, keepdims=True) - unit * inner)


def gelu_parts(x):
    root = 0.7978845608028654
    square = x * x
    bend = jnp.tanh(root * x * (1.0 + 0.044715 * square))
    half = 0.5 + 0.5 * bend
    slope = half + 0.5 * x * (1.0 - bend * bend) * (root * (1.0 + 0.134145 * square))
    return x * half, slope


class Names:
    pass


def block_kernel(inside, steps, names, *refs):
    n = Names()
    for name, ref in zip(names, refs, strict=True):
        setattr(n, name, ref)
    s = lax.axis_index("section")
    t = lax.axis_index("tensor")
    z = lax.axis_index("dp")
    x = lax.rem(t, 2)
    y = lax.div(t, 2)
    t_y = 2 * (1 - y) + x
    mate = (1 - s, t, z)
    peer_x = (s, 2 * y + 1 - x, z)
    peer_y = (s, t_y, z)
    hub = s == y
    rows_all, width = n.X0.shape
    chunk = rows_all // CHUNKS
    part = chunk // 2
    half = CHUNKS // 2
    heads = n.KT.shape[1]
    tiles = width // TILE
    depth = lax.axis_size("dp")
    slab = width // depth
    q_columns = 2 * heads * HEAD
    o_columns = 3 * heads * HEAD

    def remote(src, dst, send_sem, recv_sem, device):
        return pltpu.make_async_remote_copy(
            src_ref=src,
            dst_ref=dst,
            send_sem=send_sem,
            recv_sem=recv_sem,
            device_id=device,
            device_id_type=MESH,
        )

    def done(ref, sem):
        pltpu.make_async_copy(ref, ref, sem).wait()

    def rows_of(j):
        return pl.ds(pl.multiple_of(j * chunk, chunk), chunk)

    def half_of(j, c):
        return pl.ds(pl.multiple_of(j * chunk + c * part, part), part)

    def own_of(j):
        return pl.ds(pl.multiple_of(j * part, part), part)

    def slab_of(i):
        return pl.ds(pl.multiple_of(i * slab, slab), slab)

    def bytes_of(count):
        return n.PART.at[0, 0:count]

    barrier = pltpu.get_barrier_semaphore()
    greeted = 0
    for other_s in range(2):
        for other in range(CHUNKS):
            greeted += 1

            @pl.when((s != other_s) | (t != other))
            def _():
                pl.semaphore_signal(
                    barrier, inc=1, device_id=(other_s, other, z), device_id_type=MESH
                )

        if inside:
            for other in range(depth):
                greeted += 1

                @pl.when(z != other)
                def _():
                    pl.semaphore_signal(
                        barrier, inc=1, device_id=(other_s, t, other), device_id_type=MESH
                    )

    pl.semaphore_wait(barrier, greeted - 1 - (2 if inside else 0))

    def weights_send(l, p):
        if not inside:
            pltpu.make_async_copy(n.w_whole.at[l, p], n.W.at[l, p], n.w_recv.at[l, p, 0]).start()
            return
        own = (n.own_a, n.own_b, n.own_c)[p]

        @pl.when(s == l)
        def _():
            for far in range(depth):
                @pl.when(hub & (z == far))
                def _():
                    pltpu.make_async_copy(
                        own, n.W.at[l, p, slab_of(z)], n.w_recv.at[l, p, z]
                    ).start()

                @pl.when(jnp.logical_not(hub & (z == far)))
                def _():
                    remote(
                        own,
                        n.W.at[l, p, slab_of(z)],
                        n.w_send.at[p, far],
                        n.w_recv.at[l, p, z],
                        (y, t, far),
                    ).start()

    def weights_sent(p):
        own = (n.own_a, n.own_b, n.own_c)[p]
        for far in range(depth):

            @pl.when(jnp.logical_not(hub & (z == far)))
            def _():
                done(own, n.w_send.at[p, far])

    def weights_relay(l, p):
        if not inside:
            return

        @pl.when(hub)
        def _():
            for step in range(depth):
                far = lax.rem(z + step, depth)
                here = n.W.at[l, p, slab_of(far)]
                done(here, n.w_recv.at[l, p, far])
                remote(
                    here, here, n.relay_send.at[l, p, far], n.w_recv.at[l, p, far], peer_y
                ).start()

    def weights_wait(l, p):
        if not inside:
            done(n.W.at[l, p], n.w_recv.at[l, p, 0])
            return

        @pl.when(jnp.logical_not(hub))
        def _():
            for far in range(depth):
                done(n.W.at[l, p, slab_of(far)], n.w_recv.at[l, p, far])

    def spread(which, source, target):
        pltpu.make_async_copy(
            source.at[y], target.at[rows_of(t)], n.in_recv.at[which, t]
        ).start()
        for other in range(CHUNKS):

            @pl.when(t != other)
            def _():
                remote(
                    source.at[other // 2, half_of(0, s)],
                    target.at[half_of(t, s)],
                    n.in_send.at[which, other],
                    n.in_recv.at[which, t],
                    (s, other, z),
                ).start()

    def spread_pass(which, target, j):
        @pl.when(j == t)
        def _():
            done(target.at[rows_of(j)], n.in_recv.at[which, j])

        @pl.when(j != t)
        def _():
            here = target.at[half_of(j, s)]
            done(here, n.in_recv.at[which, j])
            remote(
                here, here, n.mate_send.at[which, j], n.mate_recv.at[which, j], mate
            ).start()

    def spread_wait(which, target, j):
        @pl.when(j != t)
        def _():
            done(target.at[half_of(j, s)], n.mate_recv.at[which, j])

    def spread_done(which):
        for other in range(CHUNKS):

            @pl.when(t != other)
            def _():
                done(bytes_of(part), n.in_send.at[which, other])
                done(bytes_of(part), n.mate_send.at[which, other])

    def pair_start(stage, ref, j):
        here = ref.at[half_of(j, s)]
        remote(here, here, n.pair_send.at[stage, j], n.pair_recv.at[stage, j], mate).start()

    def pair_wait(stage, j):
        done(bytes_of(part), n.pair_recv.at[stage, j])

    def sum_start(stage, j):
        b = stage % 2
        remote(
            n.PART.at[b, half_of(j, 1 - s)],
            n.RC.at[b, j],
            n.rs_send.at[stage, 0, j],
            n.rs_recv.at[stage, 0, j],
            mate,
        ).start()

    def sum_pass(stage, j):
        b = lax.rem(stage, 2)
        here = half_of(j, s)
        done(n.RC.at[b, j], n.rs_recv.at[stage, 0, j])
        n.PART[b, here, :] = (
            n.PART[b, here, :].astype(F32) + n.RC[b, j].astype(F32)
        ).astype(BF16)
        remote(
            n.PART.at[b, here],
            n.RX.at[b, j],
            n.rs_send.at[stage, 1, j],
            n.rs_recv.at[stage, 1, j],
            peer_x,
        ).start()
        done(n.RC.at[b, j], n.rs_send.at[stage, 0, j])

    def sum_wait(stage, j):
        b = stage % 2
        done(n.RX.at[b, j], n.rs_recv.at[stage, 1, j])
        total = n.PART[b, half_of(j, s), :].astype(F32) + n.RX[b, j].astype(F32)
        done(n.RX.at[b, j], n.rs_send.at[stage, 1, j])
        return total

    key_index = lax.broadcasted_iota(jnp.int32, (chunk, chunk), 0)
    query_index = lax.broadcasted_iota(jnp.int32, (chunk, chunk), 1)
    causal = key_index <= query_index

    def scores(l, st, i, j, diagonal):
        if l == 0:
            grown = st * st + 1.0
            inverse = lax.rsqrt(grown)
            magnitude = grown * inverse
            sign = st * inverse
        else:
            inverse, magnitude, sign = None, st, None
        if diagonal:
            magnitude = jnp.where(causal, magnitude, MASKED)
        else:
            apart = (j >= half) & (i < half)
            magnitude = magnitude + jnp.where(apart, n.bias[0:1, 0:chunk], 0.0)
        return inverse, magnitude, sign

    def norm_qkv(l, j):
        rows = rows_of(j)
        if l == 0:
            spread_wait(0, n.X0, j)
        else:
            pair_wait(PAIR_MIDDLE, j)
        source = n.X0 if l == 0 else n.Y0

        @pl.loop(0, 4)
        def _(i):
            some = pl.ds(pl.multiple_of(j * chunk + i * (chunk // 4), chunk // 4), chunk // 4)
            unit, _ = unit_rows(source[some, :].astype(F32))
            n.N1[l, some, :] = (unit * n.GAINS[2 * l : 2 * l + 1, :]).astype(BF16)

        kv = nn(n.N1[l, rows, :], n.W[l, 0, :, 0:q_columns])
        kv_low = kv.astype(BF16)
        turned = kv.T.astype(BF16)
        for h in range(heads):
            n.KV[l, h, rows, :] = kv_low[:, 2 * h * HEAD : 2 * (h + 1) * HEAD]
            n.KT[l, h, :, rows] = turned[2 * h * HEAD : (2 * h + 1) * HEAD]
            n.VT[h, :, rows] = turned[(2 * h + 1) * HEAD : (2 * h + 2) * HEAD]
        q = nn(n.N1[l, rows, :], n.W[l, 0, :, q_columns:o_columns]).astype(BF16)
        blank = jnp.zeros((chunk, HEAD), BF16)
        for h in range(heads):
            q_h = q[:, h * HEAD : (h + 1) * HEAD] * jnp.asarray(HEAD**-0.5, BF16)
            n.Q[l, h, rows, :] = jnp.concatenate([q_h, blank], axis=1)

    def attend(l, j, h):
        rows = rows_of(j)
        query = n.Q[l, h, rows, :]

        def block(i, carry, diagonal):
            top, total, out = carry
            keys = rows_of(i)
            st = nt(n.KV[l, h, keys, :], query)
            _, magnitude, sign = scores(l, st, i, j, diagonal)
            new_top = jnp.maximum(top, jnp.max(magnitude, axis=0, keepdims=True))
            weights = jnp.exp(magnitude - new_top)
            shrink = jnp.exp(top - new_top)
            total = total * shrink + jnp.sum(weights, axis=0, keepdims=True)
            signed = weights if l == 1 else sign * weights
            out = out * shrink + nn(n.VT[h, :, keys], signed.astype(BF16))
            return new_top, total, out

        carry = (
            jnp.full((1, chunk), MASKED, F32),
            jnp.zeros((1, chunk), F32),
            jnp.zeros((HEAD, chunk), F32),
        )
        carry = block(j, carry, True)
        top, total, out = lax.fori_loop(0, j, lambda i, c: block(i, c, False), carry)
        n.ATTT[l, h, :, rows] = out / total
        n.LSE[l, h, :, rows] = top + jnp.log(total)

    def out_product(l, j):
        rows = rows_of(j)
        joined = jnp.concatenate(
            [jnp.zeros((HEAD, chunk), F32)] + [n.ATTT[l, h, :, rows] for h in range(heads)],
            axis=0,
        )
        n.ATT[l, rows, :] = joined.T.astype(BF16)
        for i in range(tiles):
            here = slice(i * TILE, (i + 1) * TILE)
            n.PART[0, rows, here] = nt(
                n.ATT[l, rows, :], n.W[l, 0, here, o_columns - HEAD : width]
            ).astype(BF16)
        sum_start(SUM_ATTN[l], j)

    def attn_sum(l, j):
        source = n.X0 if l == 0 else n.Y0
        own = half_of(j, s)
        middle = source[own, :].astype(F32) + sum_wait(SUM_ATTN[l], j)
        n.MID[l, own_of(j), :] = middle
        unit, _ = unit_rows(middle)
        n.N2[l, own, :] = (unit * n.GAINS[2 * l + 1 : 2 * l + 2, :]).astype(BF16)
        pair_start(PAIR_N2[l], n.N2.at[l], j)

    def up_product(l, j):
        rows = rows_of(j)
        pair_wait(PAIR_N2[l], j)
        for i in range(tiles):
            here = slice(i * TILE, (i + 1) * TILE)
            pre = nn(n.N2[l, rows, :], n.W[l, 1, :, here])
            n.PRE[l, rows, here] = pre.astype(BF16)
            n.HID[rows, here] = gelu_parts(pre)[0].astype(BF16)

    def down_product(l, j):
        rows = rows_of(j)
        for i in range(tiles):
            here = slice(i * TILE, (i + 1) * TILE)
            n.PART[1, rows, here] = nt(n.HID[rows, :], n.W[l, 2, here, :]).astype(BF16)
        sum_start(SUM_MLP[l], j)

    def mlp_sum(l, j):
        result = n.MID[l, own_of(j), :] + sum_wait(SUM_MLP[l], j)
        if l == 0:
            n.Y0[half_of(j, s), :] = result.astype(BF16)
            pair_start(PAIR_MIDDLE, n.Y0, j)
        else:
            n.PART[1, half_of(j, s), :] = result.astype(BF16)
            last_out(0, 1, n.acts, j)

    def last_out(which, section, out, j):
        here = n.PART.at[1, half_of(j, s)]
        target = out.at[y, half_of(0, s)]

        @pl.when((s == section) & (t == j))
        def _():
            copy = pltpu.make_async_copy(here, target, n.out_send.at[which, j])
            copy.start()
            copy.wait()

        @pl.when((lax.rem(j, 2) == x) & ((s != section) | (t != j)))
        def _():
            remote(
                here,
                target,
                n.out_send.at[which, j],
                n.out_recv.at[which, y, s],
                (section, j, z),
            ).start()

    def last_out_sent(which, section, j):
        @pl.when((lax.rem(j, 2) == x) & ((s != section) | (t != j)))
        def _():
            done(bytes_of(part), n.out_send.at[which, j])

    def last_out_done(which, section, out):
        @pl.when(s == section)
        def _():
            for m in range(2):
                for c in range(2):

                    @pl.when((y != m) | (s != c))
                    def _():
                        done(bytes_of(part), n.out_recv.at[which, m, c])

    def full_out(which, section, ref, out):
        @pl.when(s == section)
        def _():
            pltpu.make_async_copy(
                ref.at[rows_of(t)], out.at[y], n.full_recv.at[which, y]
            ).start()
            remote(
                ref.at[rows_of(t_y)],
                out.at[y],
                n.full_send.at[which],
                n.full_recv.at[which, y],
                peer_y,
            ).start()

    def full_out_done(which, section):
        @pl.when(s == section)
        def _():
            done(bytes_of(chunk), n.full_recv.at[which, 0])
            done(bytes_of(chunk), n.full_recv.at[which, 1])
            done(bytes_of(chunk), n.full_send.at[which])

    def hidden_back(l, j):
        rows = rows_of(j)
        if l == 1:
            spread_wait(1, n.CT, j)
        else:
            pair_wait(PAIR_DR, j)
        source = n.CT if l == 1 else n.DR
        for i in range(tiles):
            here = slice(i * TILE, (i + 1) * TILE)
            back = nn(source[rows, :], n.W[l, 2, :, here])
            hidden, slope = gelu_parts(n.PRE[l, rows, here].astype(F32))
            n.HID[rows, here] = hidden.astype(BF16)
            n.DPRE[rows, here] = (slope * back).astype(BF16)

    def up_back(l, j):
        rows = rows_of(j)
        for i in range(tiles):
            here = slice(i * TILE, (i + 1) * TILE)
            n.PART[0, rows, here] = nt(n.DPRE[rows, :], n.W[l, 1, here, :]).astype(BF16)
        sum_start(SUM_DMLP[l], j)

    def mlp_back_sum(l, j):
        total = sum_wait(SUM_DMLP[l], j)
        source = n.CT if l == 1 else n.DR
        own = half_of(j, s)
        unit, scale = unit_rows(n.MID[l, own_of(j), :])
        n.GACC[l, 1:2, :] += jnp.sum(total * unit, axis=0, keepdims=True)
        gain = n.GAINS[2 * l + 1 : 2 * l + 2, :]
        grad = source[own, :].astype(F32) + norm_back(unit, scale, gain, total)
        n.DMID[own_of(j), :] = grad
        n.DA[l, own, :] = grad.astype(BF16)
        pair_start(PAIR_DA[l], n.DA.at[l], j)

    def attn_grad(l, j):
        rows = rows_of(j)
        pair_wait(PAIR_DA[l], j)

        @pl.when(j == CHUNKS - 1)
        def _():
            n.DKV[...] = jnp.zeros_like(n.DKV)

        back = nn(n.DA[l, rows, :], n.W[l, 0, :, o_columns - HEAD : width])
        low = back.astype(BF16)
        turned = low.astype(F32).T
        blank = jnp.zeros((chunk, HEAD), BF16)
        for h in range(heads):
            here = slice((h + 1) * HEAD, (h + 2) * HEAD)
            n.GRAD[h] = jnp.concatenate([blank, low[:, here]], axis=1)
            inner = jnp.sum(turned[here] * n.ATTT[l, h, :, rows], axis=0, keepdims=True)
            n.GRADT[h] = inner

    def attend_back(l, j, h):
        rows = rows_of(j)
        query = n.Q[l, h, rows, :]
        grad = n.GRAD[h]
        inner = n.GRADT[h]
        log_total = n.LSE[l, h, :, rows]

        def block(i, query_grad, diagonal):
            keys = rows_of(i)
            kv = n.KV[l, h, keys, :]
            st = nt(kv, query)
            dp = nt(kv, grad)
            inverse, magnitude, sign = scores(l, st, i, j, diagonal)
            weights = jnp.exp(magnitude - log_total)
            if l == 0:
                signed = sign * weights
                ds = weights * (sign * (sign * dp - inner) + dp * (inverse * inverse * inverse))
            else:
                signed = weights
                ds = weights * (dp - inner)
            ds = ds.astype(BF16)
            n.DKV[h, keys, :] += nn(ds, query) + nn(signed.astype(BF16), grad)
            return query_grad + nn(n.KT[l, h, :, keys], ds)

        query_grad = block(j, jnp.zeros((HEAD, chunk), F32), True)
        query_grad = lax.fori_loop(0, j, lambda i, c: block(i, c, False), query_grad)
        n.DQT[h] = query_grad * HEAD**-0.5

    def qkv_back(l, j):
        rows = rows_of(j)
        turned = jnp.concatenate([n.DQT[h] for h in range(heads)], axis=0).T
        for h in range(heads):
            n.DQKV[rows, 2 * h * HEAD : 2 * (h + 1) * HEAD] = n.DKV[h, rows, :].astype(BF16)
        n.DQKV[rows, q_columns:] = turned.astype(BF16)
        if l == 1:
            last_out_sent(0, 1, j)
        for i in range(tiles):
            here = slice(i * TILE, (i + 1) * TILE)
            n.PART[1, rows, here] = nt(n.DQKV[rows, :], n.W[l, 0, here, 0:o_columns]).astype(
                BF16
            )
        sum_start(SUM_DATTN[l], j)

    def attn_back_sum(l, j):
        total = sum_wait(SUM_DATTN[l], j)
        source = n.X0 if l == 0 else n.Y0
        own = half_of(j, s)
        unit, scale = unit_rows(source[own, :].astype(F32))
        n.GACC[l, 0:1, :] += jnp.sum(total * unit, axis=0, keepdims=True)
        gain = n.GAINS[2 * l : 2 * l + 1, :]
        result = n.DMID[own_of(j), :] + norm_back(unit, scale, gain, total)
        if l == 1:
            n.DR[own, :] = result.astype(BF16)
            pair_start(PAIR_DR, n.DR, j)
        else:
            n.PART[1, own, :] = result.astype(BF16)
            last_out(1, 0, n.igr, j)

    long = width // 2
    grad_order = ((1, 2), (1, 1), (1, 0), (0, 2), (0, 1), (0, 0))
    grad_to = 2 * s + x

    def kept_here(l):
        return hub & (s == l)

    def grad_sent(l, p, i):
        if not inside:
            done(n.STG.at[i], n.stg_send.at[l, p, i])
            return

        @pl.when(jnp.logical_not(kept_here(l)))
        def _():
            done(n.STG.at[i], n.stg_send.at[l, p, i])

    def weight_grad(l, p, i):
        at = grad_order.index((l, p))
        if at > 0:
            grad_sent(*grad_order[at - 1], i)
        rows = pl.ds(pl.multiple_of(i * long, long), long)
        if p == 0:
            left = n.N1[l, :, rows]
            n.STG[i, :, 0:256] = tn(left, n.DQKV[:, 0:256]).astype(BF16)
            n.STG[i, :, 256:512] = tn(left, n.DQKV[:, 256:512]).astype(BF16)
            last = tn(left, n.DQKV[:, 512:o_columns])
            out_part = tn(n.DA[l, :, rows], n.ATT[l])
            n.STG[i, :, 512:width] = jnp.concatenate([last, out_part[:, HEAD:]], axis=1).astype(
                BF16
            )
        else:
            if p == 1:
                left, right = n.N2[l, :, rows], n.DPRE
            else:
                left, right = (n.CT if l == 1 else n.DR)[:, rows], n.HID
            for k in range(tiles):
                here = slice(k * TILE, (k + 1) * TILE)
                n.STG[i, :, here] = tn(left, right[:, here]).astype(BF16)
        if not inside:
            pltpu.make_async_copy(
                n.STG.at[i], n.grads.at[l, p, rows], n.stg_send.at[l, p, i]
            ).start()
            return

        @pl.when(kept_here(l))
        def _():
            n.GR[0, p, rows, :] = n.STG[i]

        @pl.when(jnp.logical_not(kept_here(l)))
        def _():
            way = jnp.where(hub, 0, 1)
            remote(
                n.STG.at[i],
                n.GR.at[way, p, rows],
                n.stg_send.at[l, p, i],
                n.gr_recv.at[way, p, i],
                (l, grad_to, z),
            ).start()

    def slot_of(source, target):
        return jnp.where(source > target, source - 1, source)

    def grad_pass(l, p, i):
        if not inside:
            return

        @pl.when(s == l)
        def _():
            rows = pl.ds(pl.multiple_of(i * long, long), long)

            @pl.when(jnp.logical_not(hub))
            def _():
                done(n.GR.at[0, p, rows], n.gr_recv.at[0, p, i])

            done(n.GR.at[1, p, rows], n.gr_recv.at[1, p, i])
            for k in range(depth // 2):
                far = i * (depth // 2) + k

                @pl.when(z != far)
                def _():
                    here = slab_of(far)
                    n.GR[0, p, here, :] = (
                        n.GR[0, p, here, :].astype(F32) + n.GR[1, p, here, :].astype(F32)
                    ).astype(BF16)
                    slot = slot_of(z, far)
                    remote(
                        n.GR.at[0, p, here],
                        n.ZR.at[slot, p],
                        n.z_send.at[p, far],
                        n.z_recv.at[p, slot],
                        (s, t, far),
                    ).start()

    def grad_final(l, p):
        if not inside:
            return

        @pl.when(s == l)
        def _():
            here = slab_of(z)
            total = n.GR[0, p, here, :].astype(F32) + n.GR[1, p, here, :].astype(F32)
            for slot in range(depth - 1):
                done(n.ZR.at[slot, p], n.z_recv.at[p, slot])
                total = total + n.ZR[slot, p].astype(F32)
            n.FIN[p] = total
            pltpu.make_async_copy(n.FIN.at[p], n.gsum.at[p], n.fin_send.at[p]).start()

    def grads_done():
        if not inside:
            grad_sent(*grad_order[-1], 0)
            grad_sent(*grad_order[-1], 1)
            return
        grad_sent(*grad_order[-1], 0)
        grad_sent(*grad_order[-1], 1)
        for p in range(PARTS):
            for far in range(depth):

                @pl.when(z != far)
                def _():
                    done(n.ZR.at[0, p], n.z_send.at[p, far])

            done(n.FIN.at[p], n.fin_send.at[p])

    def gains_send():
        if not inside:
            n.GAINS[...] = n.gain_rows[...]
            return
        n.GIN[s, z] = n.gain_rows[...]
        for c in range(2):
            for far in range(depth):

                @pl.when((s != c) | (z != far))
                def _():
                    remote(
                        n.gain_rows,
                        n.GIN.at[s, z],
                        n.gin_send.at[c, far],
                        n.gin_recv.at[s, z],
                        (c, t, far),
                    ).start()

    def gains_wait():
        if not inside:
            return
        for c in range(2):
            for far in range(depth):

                @pl.when((s != c) | (z != far))
                def _():
                    done(n.gain_rows, n.gin_recv.at[c, far])
                    done(n.gain_rows, n.gin_send.at[c, far])

                for k in range(2):
                    n.GAINS[2 * c + k : 2 * c + k + 1, far * slab : (far + 1) * slab] = n.GIN[
                        c, far, k : k + 1, 0:slab
                    ]

    def gain_grads():
        if not inside:
            n.gain_out[...] = jnp.concatenate([n.GACC[0, 0:2], n.GACC[1, 0:2], n.GACC[0, 4:8]])
            return
        remote(n.GACC.at[1 - s], n.GC, n.gg_send.at[0], n.gg_recv.at[0], mate).start()
        done(n.GC, n.gg_recv.at[0])
        n.GACC[s] += n.GC[...]
        remote(n.GACC.at[s], n.GY, n.gg_send.at[1], n.gg_recv.at[1], peer_y).start()
        done(n.GY, n.gg_recv.at[1])
        n.GC[...] = n.GACC[s] + n.GY[...]
        for far in range(depth):

            @pl.when(z != far)
            def _():
                slot = slot_of(z, far)
                remote(
                    n.GC, n.GZ.at[slot], n.gg_send.at[2 + far], n.gg_recv.at[2 + slot], (s, t, far)
                ).start()

    def gain_grads_done():
        if not inside:
            return
        total = n.GC[...]
        for slot in range(depth - 1):
            done(n.GZ.at[slot], n.gg_recv.at[2 + slot])
            total = total + n.GZ[slot]
        n.gain_out[...] = total
        done(n.GC, n.gg_send.at[0])
        done(n.GC, n.gg_send.at[1])
        for far in range(depth):

            @pl.when(z != far)
            def _():
                done(n.GC, n.gg_send.at[2 + far])

    tasks = {"none": lambda h, j: None}
    for l in range(2):
        tasks[f"nq{l}"] = lambda h, j, l=l: norm_qkv(l, j)
        tasks[f"at{l}"] = lambda h, j, l=l: attend(l, j, h)
        tasks[f"op{l}"] = lambda h, j, l=l: out_product(l, j)
        tasks[f"sa{l}"] = lambda h, j, l=l: attn_sum(l, j)
        tasks[f"up{l}"] = lambda h, j, l=l: up_product(l, j)
        tasks[f"dn{l}"] = lambda h, j, l=l: down_product(l, j)
        tasks[f"sm{l}"] = lambda h, j, l=l: mlp_sum(l, j)
        tasks[f"hb{l}"] = lambda h, j, l=l: hidden_back(l, j)
        tasks[f"ub{l}"] = lambda h, j, l=l: up_back(l, j)
        tasks[f"sd{l}"] = lambda h, j, l=l: mlp_back_sum(l, j)
        tasks[f"ag{l}"] = lambda h, j, l=l: attn_grad(l, j)
        tasks[f"ab{l}"] = lambda h, j, l=l: attend_back(l, j, h)
        tasks[f"qb{l}"] = lambda h, j, l=l: qkv_back(l, j)
        tasks[f"sb{l}"] = lambda h, j, l=l: attn_back_sum(l, j)
        for p in range(PARTS):
            tasks[f"wg{l}{p}"] = lambda h, j, l=l, p=p: weight_grad(l, p, j)
    for p in range(PARTS):
        tasks[f"ws{p}"] = lambda h, j, p=p: weights_send(1, p)
    tasks["r"] = lambda h, j: sum_pass(h, j)
    tasks["x0"] = lambda h, j: spread_pass(0, n.X0, j)
    tasks["x1"] = lambda h, j: spread_pass(1, n.CT, j)
    tasks["wr"] = lambda h, j: weights_relay(h, j)
    tasks["ww"] = lambda h, j: weights_wait(h, j)
    tasks["gp"] = lambda h, j: grad_pass(lax.div(j, 2), h, lax.rem(j, 2))
    tasks["gf"] = lambda h, j: grad_final(j, h)
    tasks["fy"] = lambda h, j: full_out(0, 0, n.Y0, n.acts)
    tasks["fd"] = lambda h, j: full_out(1, 1, n.DR, n.igr)
    tasks["gw"] = lambda h, j: gains_wait()
    tasks["cs"] = lambda h, j: spread(1, n.cot, n.CT)
    order = list(tasks)
    run = [tasks[name] for name in order]

    weights_send(0, 0)
    gains_send()
    spread(0, n.inp, n.X0)
    weights_send(0, 1)
    weights_send(0, 2)
    n.GACC[...] = jnp.zeros_like(n.GACC)

    group = 12
    codes = [order.index(name) * 32 + h * 4 + j for name, h, j in steps]
    codes += [0] * (-len(codes) % group)
    pairs = [codes[i] + 4096 * codes[i + 1] for i in range(0, len(codes), 2)]
    per_group = group // 2
    groups = len(pairs) // per_group

    def pick(index, values):
        value = values[0]
        for at in range(1, len(values)):
            value = jnp.where(index == at, values[at], value)
        return value

    def dispatch(low, high, op, h, j):
        if high - low == 1:
            run[low](h, j)
            return
        middle = (low + high) // 2
        lax.cond(
            op < middle,
            lambda: dispatch(low, middle, op, h, j),
            lambda: dispatch(middle, high, op, h, j),
        )

    @pl.loop(0, groups)
    def _(g):
        words = [
            pick(g, [pairs[q * per_group + w] for q in range(groups)]) for w in range(per_group)
        ]

        @pl.loop(0, group)
        def _(i):
            word = pick(lax.div(i, 2), words)
            code = jnp.where(lax.rem(i, 2) == 0, lax.rem(word, 4096), lax.div(word, 4096))
            dispatch(
                0, len(run), lax.div(code, 32), lax.rem(lax.div(code, 4), 8), lax.rem(code, 4)
            )

    gain_grads()

    if inside:
        for p in range(PARTS):
            weights_sent(p)
            for l in range(2):

                @pl.when(hub)
                def _():
                    for far in range(depth):
                        done(n.W.at[l, p, slab_of(far)], n.relay_send.at[l, p, far])

    spread_done(0)
    spread_done(1)

    @pl.loop(0, CHUNKS)
    def _(j):
        for stage in range(6):
            done(bytes_of(part), n.pair_send.at[stage, j])
        last_out_sent(1, 0, j)

    full_out_done(0, 0)
    full_out_done(1, 1)
    last_out_done(0, 1, n.acts)
    last_out_done(1, 0, n.igr)
    grads_done()
    gain_grads_done()


STEPS = (
    ("x0", 0, 3), ("gw", 0, 0), ("cs", 0, 0), ("x0", 0, 0), ("x0", 0, 1), ("x0", 0, 2),
    ("wr", 0, 0), ("ww", 0, 0), ("ws0", 0, 0), ("nq0", 0, 0), ("at0", 0, 0), ("at0", 2, 0),
    ("at0", 1, 0), ("nq0", 0, 3), ("nq0", 0, 1), ("wr", 0, 1), ("op0", 0, 0), ("at0", 2, 1),
    ("at0", 1, 1), ("nq0", 0, 2), ("x1", 0, 3), ("at0", 0, 1), ("at0", 0, 2), ("r", 0, 0),
    ("wr", 0, 2), ("op0", 0, 1), ("at0", 2, 2), ("ws1", 0, 0), ("at0", 1, 2), ("r", 0, 1),
    ("at0", 1, 3), ("at0", 0, 3), ("ww", 0, 1), ("op0", 0, 2), ("sa0", 0, 0), ("x1", 0, 0),
    ("sa0", 0, 1), ("r", 0, 2), ("up0", 0, 0), ("wr", 1, 0), ("up0", 0, 1), ("ww", 0, 2),
    ("dn0", 0, 0), ("r", 1, 0), ("dn0", 0, 1), ("ws2", 0, 0), ("r", 1, 1), ("at0", 2, 3),
    ("sa0", 0, 2), ("op0", 0, 3), ("up0", 0, 2), ("r", 0, 3), ("dn0", 0, 2), ("sm0", 0, 0),
    ("wr", 1, 1), ("x1", 0, 1), ("ww", 1, 0), ("sm0", 0, 1), ("nq1", 0, 0), ("r", 1, 2),
    ("sa0", 0, 3), ("at1", 0, 0), ("at1", 1, 0), ("up0", 0, 3), ("at1", 2, 0), ("dn0", 0, 3),
    ("nq1", 0, 1), ("at1", 0, 1), ("r", 1, 3), ("sm0", 0, 2), ("op1", 0, 0), ("at1", 1, 1),
    ("at1", 2, 1), ("nq1", 0, 2), ("op1", 0, 1), ("r", 2, 0), ("at1", 0, 2), ("at1", 2, 2),
    ("sm0", 0, 3), ("wr", 1, 2), ("x1", 0, 2), ("at1", 1, 2), ("r", 2, 1), ("op1", 0, 2),
    ("ww", 1, 1), ("nq1", 0, 3), ("at1", 2, 3), ("sa1", 0, 0), ("r", 2, 2), ("at1", 1, 3),
    ("at1", 0, 3), ("op1", 0, 3), ("sa1", 0, 1), ("up1", 0, 0), ("r", 2, 3), ("sa1", 0, 2),
    ("ww", 1, 2), ("dn1", 0, 0), ("r", 3, 0), ("up1", 0, 1), ("sa1", 0, 3), ("dn1", 0, 1),
    ("fy", 0, 0), ("r", 3, 1), ("up1", 0, 2), ("dn1", 0, 2), ("up1", 0, 3), ("hb1", 0, 2),
    ("hb1", 0, 0), ("dn1", 0, 3), ("sm1", 0, 0), ("r", 3, 3), ("hb1", 0, 3), ("ub1", 0, 3),
    ("hb1", 0, 1), ("wg12", 0, 1), ("r", 3, 2), ("ub1", 0, 1), ("sm1", 0, 3), ("r", 4, 3),
    ("ub1", 0, 2), ("sm1", 0, 2), ("sm1", 0, 1), ("ub1", 0, 0), ("r", 4, 2), ("wg11", 0, 1),
    ("sd1", 0, 3), ("r", 4, 0), ("wg12", 0, 0), ("ag1", 0, 3), ("ab1", 1, 3), ("ab1", 2, 3),
    ("sd1", 0, 2), ("r", 4, 1), ("ab1", 0, 3), ("qb1", 0, 3), ("ag1", 0, 2), ("sd1", 0, 0),
    ("ab1", 0, 2), ("ab1", 1, 2), ("r", 5, 3), ("sd1", 0, 1), ("ab1", 2, 2), ("qb1", 0, 2),
    ("ag1", 0, 1), ("ab1", 2, 1), ("r", 5, 2), ("wg11", 0, 0), ("gp", 1, 3), ("ab1", 0, 1),
    ("gp", 2, 2), ("ab1", 1, 1), ("qb1", 0, 1), ("ag1", 0, 0), ("ab1", 1, 0), ("ab1", 0, 0),
    ("r", 5, 1), ("ab1", 2, 0), ("sb1", 0, 3), ("qb1", 0, 0), ("wg10", 0, 0), ("sb1", 0, 2),
    ("hb0", 0, 3), ("r", 5, 0), ("gp", 1, 2), ("ub0", 0, 3), ("sb1", 0, 1), ("r", 6, 3),
    ("hb0", 0, 2), ("ub0", 0, 2), ("wg10", 0, 1), ("hb0", 0, 1), ("ub0", 0, 1), ("r", 6, 2),
    ("gp", 2, 3), ("sb1", 0, 0), ("sd0", 0, 3), ("r", 6, 1), ("hb0", 0, 0), ("wg02", 0, 0),
    ("ag0", 0, 3), ("gp", 0, 3), ("sd0", 0, 2), ("wg02", 0, 1), ("gp", 0, 2), ("ab0", 1, 3),
    ("ab0", 0, 3), ("gf", 2, 1), ("ab0", 2, 3), ("qb0", 0, 3), ("ag0", 0, 2), ("sd0", 0, 1),
    ("ub0", 0, 0), ("ab0", 0, 2), ("wg01", 0, 0), ("gp", 2, 0), ("r", 6, 0), ("ab0", 2, 2),
    ("ab0", 1, 2), ("qb0", 0, 2), ("ag0", 0, 1), ("gp", 2, 1), ("wg01", 0, 1), ("ab0", 1, 1),
    ("ab0", 2, 1), ("ab0", 0, 1), ("qb0", 0, 1), ("gp", 1, 0), ("sd0", 0, 0), ("ag0", 0, 0),
    ("r", 7, 1), ("gf", 0, 1), ("ab0", 0, 0), ("ab0", 2, 0), ("ab0", 1, 0), ("qb0", 0, 0),
    ("r", 7, 2), ("wg00", 0, 0), ("r", 7, 3), ("r", 7, 0), ("gp", 1, 1), ("sb0", 0, 1),
    ("gf", 1, 1), ("wg00", 0, 1), ("gp", 0, 0), ("sb0", 0, 3), ("gp", 0, 1), ("sb0", 0, 2),
    ("gf", 1, 0), ("fd", 0, 0), ("gf", 2, 0), ("sb0", 0, 0), ("gf", 0, 0),
)


def run_blocks(inputs, cotangent, weights, gain_rows, bias, depth, inside):
    buckets, chunk, width = inputs.shape
    rows = CHUNKS * chunk
    part = chunk // 2
    heads = width // 4 // HEAD
    vmem, dma = pltpu.VMEM, pltpu.SemaphoreType.DMA
    scratch = dict(
        W=vmem((2, PARTS, width, width), BF16),
        X0=vmem((rows, width), BF16),
        Y0=vmem((rows, width), BF16),
        CT=vmem((rows, width), BF16),
        DR=vmem((rows, width), BF16),
        N1=vmem((2, rows, width), BF16),
        N2=vmem((2, rows, width), BF16),
        Q=vmem((2, heads, rows, 2 * HEAD), BF16),
        KV=vmem((2, heads, rows, 2 * HEAD), BF16),
        KT=vmem((2, heads, HEAD, rows), BF16),
        VT=vmem((heads, HEAD, rows), BF16),
        ATT=vmem((2, rows, (heads + 1) * HEAD), BF16),
        ATTT=vmem((2, heads, HEAD, rows), F32),
        LSE=vmem((2, heads, 1, rows), F32),
        PRE=vmem((2, rows, width), BF16),
        HID=vmem((rows, width), BF16),
        DPRE=vmem((rows, width), BF16),
        DQKV=vmem((rows, 3 * heads * HEAD), BF16),
        DA=vmem((2, rows, width), BF16),
        DKV=vmem((heads, rows, 2 * HEAD), F32),
        GRAD=vmem((heads, chunk, 2 * HEAD), BF16),
        GRADT=vmem((heads, 1, chunk), F32),
        DQT=vmem((heads, HEAD, chunk), F32),
        MID=vmem((2, CHUNKS * part, width), F32),
        DMID=vmem((CHUNKS * part, width), F32),
        PART=vmem((2, rows, width), BF16),
        RC=vmem((2, CHUNKS, part, width), BF16),
        RX=vmem((2, CHUNKS, part, width), BF16),
        STG=vmem((2, width // 2, width), BF16),
        GAINS=vmem((8, width), F32),
        GACC=vmem((2, 8, width), F32),
        in_send=dma((2, CHUNKS)),
        in_recv=dma((2, CHUNKS)),
        mate_send=dma((2, CHUNKS)),
        mate_recv=dma((2, CHUNKS)),
        pair_send=dma((6, CHUNKS)),
        pair_recv=dma((6, CHUNKS)),
        rs_send=dma((8, 2, CHUNKS)),
        rs_recv=dma((8, 2, CHUNKS)),
        w_recv=dma((2, PARTS, depth if inside else 1)),
        stg_send=dma((2, PARTS, 2)),
        out_send=dma((2, CHUNKS)),
        out_recv=dma((2, 2, 2)),
        full_send=dma((2,)),
        full_recv=dma((2, 2)),
    )
    outs = dict(
        acts=jax.ShapeDtypeStruct(inputs.shape, BF16), igr=jax.ShapeDtypeStruct(inputs.shape, BF16)
    )
    if inside:
        slab = width // depth
        scratch.update(
            GR=vmem((2, PARTS, width, width), BF16),
            ZR=vmem((depth - 1, PARTS, slab, width), BF16),
            FIN=vmem((PARTS, slab, width), F32),
            GIN=vmem((2, depth) + gain_rows.shape, F32),
            GC=vmem((8, width), F32),
            GY=vmem((8, width), F32),
            GZ=vmem((depth - 1, 8, width), F32),
            w_send=dma((PARTS, depth)),
            relay_send=dma((2, PARTS, depth)),
            gr_recv=dma((2, PARTS, 2)),
            z_send=dma((PARTS, depth)),
            z_recv=dma((PARTS, depth - 1)),
            fin_send=dma((PARTS,)),
            gin_send=dma((2, depth)),
            gin_recv=dma((2, depth)),
            gg_send=dma((2 + depth,)),
            gg_recv=dma((1 + depth,)),
        )
        own = dict(own_a=weights[0], own_b=weights[1], own_c=weights[2])
        outs["gsum"] = jax.ShapeDtypeStruct((PARTS, slab, width), F32)
    else:
        own = dict(w_whole=weights)
        outs["grads"] = jax.ShapeDtypeStruct(weights.shape, BF16)
    outs["gain_out"] = jax.ShapeDtypeStruct((8, width), F32)
    given = dict(inp=inputs, cot=cotangent, **own, gain_rows=gain_rows, bias=bias)
    hbm = pl.BlockSpec(memory_space=pl.ANY)
    in_vmem = pl.BlockSpec(memory_space=pltpu.VMEM)
    small = ("gain_rows", "bias", "gain_out")
    return pl.pallas_call(
        functools.partial(
            block_kernel, inside, STEPS, list(given) + list(outs) + list(scratch)
        ),
        out_shape=tuple(outs.values()),
        in_specs=[in_vmem if name in small else hbm for name in given],
        out_specs=tuple(in_vmem if name in small else hbm for name in outs),
        scratch_shapes=list(scratch.values()),
        compiler_params=pltpu.CompilerParams(
            collective_id=0, has_side_effects=True, vmem_limit_bytes=VMEM_LIMIT
        ),
        cost_estimate=pl.CostEstimate(
            flops=27_000_000_000, bytes_accessed=40_000_000, transcendentals=20_000_000
        ),
        name="blocks",
    )(*given.values())


def shards(inputs, lengths, gains, w_qkv, w_out, w_up, w_down, cotangent):
    local_rows, width = inputs.shape[1:]
    slab = w_up.shape[1]
    heads = w_qkv.shape[3] // HEAD
    depth = lax.axis_size("dp")
    y = lax.div(lax.axis_index("tensor"), 2)
    section = lax.axis_index("section")
    inside = slab % 16 == 0 and depth % 2 == 0
    split = (slab, heads, HEAD)
    kv = jnp.stack([w_qkv[0, :, 1].reshape(split), w_qkv[0, :, 2].reshape(split)], axis=2)
    own = (
        jnp.concatenate([kv.reshape(slab, -1), w_qkv[0, :, 0], w_out[0].T], axis=1),
        w_up[0],
        w_down[0].T,
    )
    bias = jnp.where(lengths[y] == CHUNKS * local_rows, 0.0, MASKED).astype(F32)
    bias = jnp.broadcast_to(bias, (8, local_rows))
    axes = ("section", "tensor")
    if inside:
        gain_rows = jnp.pad(gains[0].astype(F32), ((0, 6), (0, -slab % 128)))
        acts, input_grads, total, gain_part = run_blocks(
            inputs, cotangent, own, gain_rows, bias, depth, inside
        )
        gain_part = gain_part[None, :2]
        at = lax.axis_index("tensor") * depth + lax.axis_index("dp")
        share = width // (depth * lax.axis_size("tensor"))
        gain_grads = lax.dynamic_slice_in_dim(gain_part, at * share, share, 2)
    else:
        whole = lax.all_gather(jnp.stack(own), "dp", axis=1, tiled=True)
        weights = []
        for l in range(2):
            parts = []
            for to_y in range(2):
                pairs = [
                    (4 * l + 2 * c + x, 4 * c + 2 * to_y + x) for c in range(2) for x in range(2)
                ]
                parts.append(lax.ppermute(whole, axes, pairs))
            weights.append(jnp.where(y == 0, parts[0], parts[1]))
        weights = jnp.stack(weights)
        gain_rows = lax.all_gather(gains, "dp", axis=2, tiled=True)
        gain_rows = lax.all_gather(gain_rows, "section", axis=0, tiled=True)
        gain_rows = jnp.pad(gain_rows.reshape(4, width).astype(F32), ((0, 4), (0, 0)))
        acts, input_grads, partial, gain_part = run_blocks(
            inputs, cotangent, weights, gain_rows, bias, depth, inside
        )
        total = jnp.zeros(partial.shape[1:], F32)
        for l in range(2):
            for from_y in range(2):
                pairs = [
                    (4 * c + 2 * from_y + x, 4 * l + 2 * c + x) for c in range(2) for x in range(2)
                ]
                total = total + lax.ppermute(partial[l], axes, pairs).astype(F32)
        total = lax.psum_scatter(total.astype(BF16), "dp", scatter_dimension=1, tiled=True)
        total = total.astype(F32)
        gain_part = lax.psum(gain_part[:4].reshape(2, 2, width), "section")
        gain_part = lax.dynamic_slice_in_dim(gain_part, section, 1, 0)
        gain_grads = 0.5 * lax.psum_scatter(
            gain_part, ("tensor", "dp"), scatter_dimension=2, tiled=True
        )
    columns = heads * HEAD
    kv = total[0, :, : 2 * columns].reshape(slab, heads, 2, HEAD)
    q = total[0, :, 2 * columns : 3 * columns]
    qkv_grads = jnp.stack([q, kv[:, :, 0].reshape(q.shape), kv[:, :, 1].reshape(q.shape)], axis=1)
    return (
        acts[None],
        input_grads[None],
        gain_grads,
        qkv_grads[None],
        total[0, :, 3 * columns :].T[None],
        total[1][None],
        total[2].T[None],
    )


def solution(mesh):
    in_specs = (
        P("dp", "tensor", None),
        P("dp"),
        P("section", None, "dp"),
        P("section", "dp", None, "tensor"),
        P("section", "tensor", "dp"),
        P("section", "dp", "tensor"),
        P("section", "tensor", "dp"),
        P("dp", "tensor", None),
    )
    out_specs = (
        P("section", "dp", "tensor", None),
        P("section", "dp", "tensor", None),
        P("section", None, ("tensor", "dp")),
        P("section", "dp", None, "tensor"),
        P("section", "tensor", "dp"),
        P("section", "dp", "tensor"),
        P("section", "tensor", "dp"),
    )
    return jax.shard_map(shards, mesh=mesh, in_specs=in_specs, out_specs=out_specs, check_vma=False)
```

```python
import functools

import jax
import jax.numpy as jnp
from jax import lax
from jax.experimental import pallas as pl
from jax.experimental.pallas import tpu as pltpu
from jax.sharding import PartitionSpec as P

HEAD = 64
EPSILON = 1e-05
MASKED = -1e30
CHUNKS = 4
PARTS = 3
VMEM_LIMIT = 63 << 20
TILE = 256
BF16 = jnp.bfloat16
F32 = jnp.float32
MESH = pl.DeviceIdType.MESH

SUM_ATTN = (0, 2)
SUM_MLP = (1, 3)
SUM_DMLP = (6, 4)
SUM_DATTN = (7, 5)
PAIR_N2 = (0, 1)
PAIR_N1 = (6, 2)
PAIR_DA = (4, 3)
PAIR_DR = 5


def nn(left, right):
    return lax.dot_general(left, right, (((1,), (0,)), ((), ())), preferred_element_type=F32)


def nt(left, right):
    return lax.dot_general(left, right, (((1,), (1,)), ((), ())), preferred_element_type=F32)


def tn(left, right):
    return lax.dot_general(left, right, (((0,), (0,)), ((), ())), preferred_element_type=F32)


def unit_rows(rows):
    centre = rows - jnp.mean(rows, axis=-1, keepdims=True)
    spread = jnp.mean(centre * centre, axis=-1, keepdims=True)
    scale = lax.rsqrt(spread + EPSILON)
    return centre * scale, scale


def norm_back(unit, scale, gain, grad):
    wide = grad * gain
    inner = jnp.mean(wide * unit, axis=-1, keepdims=True)
    return scale * (wide - jnp.mean(wide, axis=-1, keepdims=True) - unit * inner)


def gelu_parts(x):
    root = 0.7978845608028654
    square = x * x
    bend = jnp.tanh(root * x * (1.0 + 0.044715 * square))
    half = 0.5 + 0.5 * bend
    slope = half + 0.5 * x * (1.0 - bend * bend) * (root * (1.0 + 0.134145 * square))
    return x * half, slope


class Names:
    pass


def block_kernel(inside, steps, names, *refs):
    n = Names()
    for name, ref in zip(names, refs, strict=True):
        setattr(n, name, ref)
    s = lax.axis_index("section")
    t = lax.axis_index("tensor")
    z = lax.axis_index("dp")
    x = lax.rem(t, 2)
    y = lax.div(t, 2)
    t_y = 2 * (1 - y) + x
    mate = (1 - s, t, z)
    peer_x = (s, 2 * y + 1 - x, z)
    peer_y = (s, t_y, z)
    hub = s == y
    rows_all, width = n.CT.shape
    chunk = rows_all // CHUNKS
    part = chunk // 2
    half = CHUNKS // 2
    heads = n.KT.shape[1]
    tiles = width // TILE
    depth = lax.axis_size("dp")
    slab = width // depth
    q_columns = 2 * heads * HEAD
    o_columns = 3 * heads * HEAD

    def remote(src, dst, send_sem, recv_sem, device):
        return pltpu.make_async_remote_copy(
            src_ref=src,
            dst_ref=dst,
            send_sem=send_sem,
            recv_sem=recv_sem,
            device_id=device,
            device_id_type=MESH,
        )

    def done(ref, sem):
        pltpu.make_async_copy(ref, ref, sem).wait()

    def rows_of(j):
        return pl.ds(pl.multiple_of(j * chunk, chunk), chunk)

    def half_of(j, c):
        return pl.ds(pl.multiple_of(j * chunk + c * part, part), part)

    def own_of(j):
        return pl.ds(pl.multiple_of(j * part, part), part)

    def slab_of(i):
        return pl.ds(pl.multiple_of(i * slab, slab), slab)

    def bytes_of(count):
        return n.PART.at[0, 0:count]

    barrier = pltpu.get_barrier_semaphore()
    greeted = 0
    for other_s in range(2):
        for other in range(CHUNKS):
            greeted += 1

            @pl.when((s != other_s) | (t != other))
            def _():
                pl.semaphore_signal(
                    barrier, inc=1, device_id=(other_s, other, z), device_id_type=MESH
                )

        if inside:
            for other in range(depth):
                greeted += 1

                @pl.when(z != other)
                def _():
                    pl.semaphore_signal(
                        barrier, inc=1, device_id=(other_s, t, other), device_id_type=MESH
                    )

    pl.semaphore_wait(barrier, greeted - 1 - (2 if inside else 0))

    def pick(index, values):
        value = values[0]
        for at in range(1, len(values)):
            value = jnp.where(index == at, values[at], value)
        return value

    def weights_send(l, p):
        if not inside:
            pltpu.make_async_copy(n.w_whole.at[l, p], n.W.at[l, p], n.w_recv.at[l, p, 0]).start()
            return
        own = (n.own_a, n.own_b, n.own_c)[p]

        @pl.when(s == l)
        def _():
            for far in range(depth):
                @pl.when(hub & (z == far))
                def _():
                    pltpu.make_async_copy(
                        own, n.W.at[l, p, slab_of(z)], n.w_recv.at[l, p, z]
                    ).start()

                @pl.when(jnp.logical_not(hub & (z == far)))
                def _():
                    remote(
                        own,
                        n.W.at[l, p, slab_of(z)],
                        n.w_send.at[p, far],
                        n.w_recv.at[l, p, z],
                        (y, t, far),
                    ).start()

    def weights_sent(p):
        own = (n.own_a, n.own_b, n.own_c)[p]
        for far in range(depth):

            @pl.when(jnp.logical_not(hub & (z == far)))
            def _():
                done(own, n.w_send.at[p, far])

    def weights_relay(l, p, step):
        if not inside:
            return

        @pl.when(hub)
        def _():
            beside = z + 1 - 2 * lax.rem(z, 2)
            far = pick(step, [z, beside, lax.rem(z + 2, depth), lax.rem(beside + 2, depth)])
            here = n.W.at[l, p, slab_of(far)]
            done(here, n.w_recv.at[l, p, far])
            remote(
                here, here, n.relay_send.at[l, p, far], n.w_recv.at[l, p, far], peer_y
            ).start()

    def weights_wait(l, p):
        if not inside:
            done(n.W.at[l, p], n.w_recv.at[l, p, 0])
            return

        @pl.when(jnp.logical_not(hub))
        def _():
            for far in range(depth):
                done(n.W.at[l, p, slab_of(far)], n.w_recv.at[l, p, far])

    def spread(which, source, target):
        own = target.at[own_of(t)] if which == 0 else target.at[half_of(t, s)]
        pltpu.make_async_copy(
            source.at[y, half_of(0, s)], own, n.in_recv.at[which, t]
        ).start()
        for other in range(CHUNKS):

            @pl.when(t != other)
            def _():
                remote(
                    source.at[other // 2, half_of(0, s)],
                    own,
                    n.in_send.at[which, other],
                    n.in_recv.at[which, t],
                    (s, other, z),
                ).start()

    def inputs_pass(j):
        done(bytes_of(part), n.in_recv.at[0, j])
        norm_first(0, n.X0[own_of(j), :].astype(F32), j)

    def cotangent_pass(j):
        here = n.CT.at[half_of(j, s)]
        done(here, n.in_recv.at[1, j])
        remote(here, here, n.mate_send.at[j], n.mate_recv.at[j], mate).start()

    def cotangent_wait(j):
        done(bytes_of(part), n.mate_recv.at[j])

    def spread_done(which):
        for other in range(CHUNKS):

            @pl.when(t != other)
            def _():
                done(bytes_of(part), n.in_send.at[which, other])

            if which == 1:
                done(bytes_of(part), n.mate_send.at[other])

    def pair_start(stage, ref, j):
        here = ref.at[half_of(j, s)]
        remote(here, here, n.pair_send.at[stage, j], n.pair_recv.at[stage, j], mate).start()

    def pair_wait(stage, j):
        done(bytes_of(part), n.pair_recv.at[stage, j])

    def sum_start(stage, j):
        b = stage % 2
        remote(
            n.PART.at[b, half_of(j, 1 - s)],
            n.RC.at[b, j],
            n.rs_send.at[stage, 0, j],
            n.rs_recv.at[stage, 0, j],
            mate,
        ).start()

    def sum_pass(stage, j):
        b = lax.rem(stage, 2)
        here = half_of(j, s)
        done(n.RC.at[b, j], n.rs_recv.at[stage, 0, j])
        n.PART[b, here, :] = (
            n.PART[b, here, :].astype(F32) + n.RC[b, j].astype(F32)
        ).astype(BF16)
        arriving = jnp.where(stage == SUM_DMLP[1], 2, b)
        one_way = (stage == SUM_MLP[1]) | (stage == SUM_DATTN[0])

        @pl.when(jnp.logical_not(one_way) | (lax.rem(j, 2) != x))
        def _():
            remote(
                n.PART.at[b, here],
                n.RX.at[arriving, j],
                n.rs_send.at[stage, 1, j],
                n.rs_recv.at[stage, 1, j],
                peer_x,
            ).start()

        done(n.RC.at[b, j], n.rs_send.at[stage, 0, j])

    def sum_sent(stage, j):
        done(n.RX.at[stage % 2, j], n.rs_send.at[stage, 1, j])

    def sum_wait(stage, j):
        b = stage % 2
        arriving = 2 if stage == SUM_DMLP[1] else b
        done(n.RX.at[arriving, j], n.rs_recv.at[stage, 1, j])
        total = n.PART[b, half_of(j, s), :].astype(F32) + n.RX[arriving, j].astype(F32)
        if stage not in (SUM_MLP[1], SUM_DATTN[0]):
            sum_sent(stage, j)
        return total

    key_index = lax.broadcasted_iota(jnp.int32, (chunk, chunk), 0)
    query_index = lax.broadcasted_iota(jnp.int32, (chunk, chunk), 1)
    causal = key_index <= query_index

    def scores(l, st, i, j, diagonal):
        if l == 0:
            grown = st * st + 1.0
            inverse = lax.rsqrt(grown)
            magnitude = grown * inverse
            sign = st * inverse
        else:
            inverse, magnitude, sign = None, st, None
        if diagonal:
            magnitude = jnp.where(causal, magnitude, MASKED)
        else:
            apart = (j >= half) & (i < half)
            magnitude = magnitude + jnp.where(apart, n.bias[0:1, 0:chunk], 0.0)
        return inverse, magnitude, sign

    def norm_first(l, own_rows, j):
        unit, _ = unit_rows(own_rows)
        n.N1[l, half_of(j, s), :] = (unit * n.GAINS[2 * l : 2 * l + 1, :]).astype(BF16)
        pair_start(PAIR_N1[l], n.N1.at[l], j)

    def qkv_product(l, j):
        rows = rows_of(j)
        pair_wait(PAIR_N1[l], j)
        kv = nn(n.N1[l, rows, :], n.W[l, 0, :, 0:q_columns])
        kv_low = kv.astype(BF16)
        turned = kv.T.astype(BF16)
        for h in range(heads):
            n.KV[l, h, rows, :] = kv_low[:, 2 * h * HEAD : 2 * (h + 1) * HEAD]
            n.KT[l, h, :, rows] = turned[2 * h * HEAD : (2 * h + 1) * HEAD]
            n.VT[h, :, rows] = turned[(2 * h + 1) * HEAD : (2 * h + 2) * HEAD]
        q = nn(n.N1[l, rows, :], n.W[l, 0, :, q_columns:o_columns]).astype(BF16)
        blank = jnp.zeros((chunk, HEAD), BF16)
        for h in range(heads):
            q_h = q[:, h * HEAD : (h + 1) * HEAD] * jnp.asarray(HEAD**-0.5, BF16)
            n.Q[l, h, rows, :] = jnp.concatenate([q_h, blank], axis=1)

    def heads_loop(task, l, j, h):
        @pl.loop(jnp.where(h == heads, 0, h), jnp.where(h == heads, heads, h + 1))
        def _(one):
            task(l, j, one)

    def attend(l, j, h):
        rows = rows_of(j)
        query = n.Q[l, h, rows, :]

        def block(i, carry, diagonal):
            top, total, out = carry
            keys = rows_of(i)
            st = nt(n.KV[l, h, keys, :], query)
            _, magnitude, sign = scores(l, st, i, j, diagonal)
            new_top = jnp.maximum(top, jnp.max(magnitude, axis=0, keepdims=True))
            weights = jnp.exp(magnitude - new_top)
            shrink = jnp.exp(top - new_top)
            total = total * shrink + jnp.sum(weights, axis=0, keepdims=True)
            signed = weights if l == 1 else sign * weights
            out = out * shrink + nn(n.VT[h, :, keys], signed.astype(BF16))
            return new_top, total, out

        carry = (
            jnp.full((1, chunk), MASKED, F32),
            jnp.zeros((1, chunk), F32),
            jnp.zeros((HEAD, chunk), F32),
        )
        carry = block(j, carry, True)
        top, total, out = lax.fori_loop(0, j, lambda i, c: block(i, c, False), carry)
        n.ATTT[l, h, :, rows] = out / total
        n.LSE[l, h, :, rows] = top + jnp.log(total)

    def out_product(l, j):
        rows = rows_of(j)
        joined = jnp.concatenate(
            [jnp.zeros((HEAD, chunk), F32)] + [n.ATTT[l, h, :, rows] for h in range(heads)],
            axis=0,
        )
        n.ATT[l, rows, :] = joined.T.astype(BF16)
        for i in range(tiles):
            here = slice(i * TILE, (i + 1) * TILE)
            n.PART[0, rows, here] = nt(
                n.ATT[l, rows, :], n.W[l, 0, here, o_columns - HEAD : width]
            ).astype(BF16)
        sum_start(SUM_ATTN[l], j)

    def attn_sum(l, j):
        source = n.X0 if l == 0 else n.Y0
        own = half_of(j, s)
        middle = source[own_of(j), :].astype(F32) + sum_wait(SUM_ATTN[l], j)
        n.MID[l, own_of(j), :] = middle
        unit, _ = unit_rows(middle)
        n.N2[l, own, :] = (unit * n.GAINS[2 * l + 1 : 2 * l + 2, :]).astype(BF16)
        pair_start(PAIR_N2[l], n.N2.at[l], j)

    def up_product(l, j):
        rows = rows_of(j)
        pair_wait(PAIR_N2[l], j)
        for i in range(tiles):
            here = slice(i * TILE, (i + 1) * TILE)
            pre = nn(n.N2[l, rows, :], n.W[l, 1, :, here])
            n.PRE[l, rows, here] = pre.astype(BF16)
            n.HID[rows, here] = gelu_parts(pre)[0].astype(BF16)
        for i in range(tiles):
            here = slice(i * TILE, (i + 1) * TILE)
            n.PART[1, rows, here] = nt(n.HID[rows, :], n.W[l, 2, here, :]).astype(BF16)
        sum_start(SUM_MLP[l], j)

    def mlp_sum(l, j):
        if l == 0:
            result = (n.MID[l, own_of(j), :] + sum_wait(SUM_MLP[l], j)).astype(BF16)
            n.Y0[own_of(j), :] = result
            norm_first(1, result.astype(F32), j)
            give_out(2, 0, n.Y0.at[own_of(j)], n.acts, j)
        else:

            @pl.when(lax.rem(j, 2) == x)
            def _():
                result = n.MID[l, own_of(j), :] + sum_wait(SUM_MLP[l], j)
                n.PART[1, half_of(j, s), :] = result.astype(BF16)
                give_out(0, 1, n.PART.at[1, half_of(j, s)], n.acts, j)

            @pl.when(lax.rem(j, 2) != x)
            def _():
                sum_sent(SUM_MLP[l], j)

    def give_out(which, section, here, out, j):
        target = out.at[y, half_of(0, s)]

        @pl.when((s == section) & (t == j))
        def _():
            copy = pltpu.make_async_copy(here, target, n.out_send.at[which, j])
            copy.start()
            copy.wait()

        @pl.when((lax.rem(j, 2) == x) & ((s != section) | (t != j)))
        def _():
            remote(
                here,
                target,
                n.out_send.at[which, j],
                n.out_recv.at[which, y, s],
                (section, j, z),
            ).start()

    def given_out(which, section, j):
        @pl.when((lax.rem(j, 2) == x) & ((s != section) | (t != j)))
        def _():
            done(bytes_of(part), n.out_send.at[which, j])

    def got_out(which, section):
        @pl.when(s == section)
        def _():
            for m in range(2):
                for c in range(2):

                    @pl.when((y != m) | (s != c))
                    def _():
                        done(bytes_of(part), n.out_recv.at[which, m, c])

    def hidden_back(l, j):
        rows = rows_of(j)
        if l == 1:
            cotangent_wait(j)
        else:
            pair_wait(PAIR_DR, j)
        source = n.CT if l == 1 else n.DR
        for i in range(tiles):
            here = slice(i * TILE, (i + 1) * TILE)
            back = nn(source[rows, :], n.W[l, 2, :, here])
            hidden, slope = gelu_parts(n.PRE[l, rows, here].astype(F32))
            n.HID[rows, here] = hidden.astype(BF16)
            n.DPRE[rows, here] = (slope * back).astype(BF16)
        for i in range(tiles):
            here = slice(i * TILE, (i + 1) * TILE)
            n.PART[0, rows, here] = nt(n.DPRE[rows, :], n.W[l, 1, here, :]).astype(BF16)
        sum_start(SUM_DMLP[l], j)

    def mlp_back_sum(l, j):
        total = sum_wait(SUM_DMLP[l], j)
        source = n.CT if l == 1 else n.DR
        own = half_of(j, s)
        unit, scale = unit_rows(n.MID[l, own_of(j), :])
        n.GACC[l, 1:2, :] += jnp.sum(total * unit, axis=0, keepdims=True)
        gain = n.GAINS[2 * l + 1 : 2 * l + 2, :]
        grad = source[own, :].astype(F32) + norm_back(unit, scale, gain, total)
        n.DMID[own_of(j), :] = grad
        n.DA[l, own, :] = grad.astype(BF16)
        pair_start(PAIR_DA[l], n.DA.at[l], j)

    def attn_grad(l, j):
        rows = rows_of(j)
        pair_wait(PAIR_DA[l], j)

        @pl.when(j == CHUNKS - 1)
        def _():
            n.DKV[...] = jnp.zeros_like(n.DKV)

        back = nn(n.DA[l, rows, :], n.W[l, 0, :, o_columns - HEAD : width])
        low = back.astype(BF16)
        turned = low.astype(F32).T
        blank = jnp.zeros((chunk, HEAD), BF16)
        for h in range(heads):
            here = slice((h + 1) * HEAD, (h + 2) * HEAD)
            n.GRAD[h] = jnp.concatenate([blank, low[:, here]], axis=1)
            inner = jnp.sum(turned[here] * n.ATTT[l, h, :, rows], axis=0, keepdims=True)
            n.GRADT[h] = inner

    def attend_back(l, j, h):
        rows = rows_of(j)
        query = n.Q[l, h, rows, :]
        grad = n.GRAD[h]
        inner = n.GRADT[h]
        log_total = n.LSE[l, h, :, rows]

        def block(i, query_grad, diagonal):
            keys = rows_of(i)
            kv = n.KV[l, h, keys, :]
            st = nt(kv, query)
            dp = nt(kv, grad)
            inverse, magnitude, sign = scores(l, st, i, j, diagonal)
            weights = jnp.exp(magnitude - log_total)
            if l == 0:
                signed = sign * weights
                ds = weights * (sign * (sign * dp - inner) + dp * (inverse * inverse * inverse))
            else:
                signed = weights
                ds = weights * (dp - inner)
            ds = ds.astype(BF16)
            n.DKV[h, keys, :] += nn(ds, query) + nn(signed.astype(BF16), grad)
            return query_grad + nn(n.KT[l, h, :, keys], ds)

        query_grad = block(j, jnp.zeros((HEAD, chunk), F32), True)
        query_grad = lax.fori_loop(0, j, lambda i, c: block(i, c, False), query_grad)
        n.DQT[h] = query_grad * HEAD**-0.5

    def qkv_back(l, j):
        rows = rows_of(j)
        turned = jnp.concatenate([n.DQT[h] for h in range(heads)], axis=0).T
        for h in range(heads):
            n.DQKV[rows, 2 * h * HEAD : 2 * (h + 1) * HEAD] = n.DKV[h, rows, :].astype(BF16)
        n.DQKV[rows, q_columns:] = turned.astype(BF16)
        if l == 1:
            given_out(0, 1, j)
        for i in range(tiles):
            here = slice(i * TILE, (i + 1) * TILE)
            n.PART[1, rows, here] = nt(n.DQKV[rows, :], n.W[l, 0, here, 0:o_columns]).astype(
                BF16
            )
        sum_start(SUM_DATTN[l], j)

    def attn_back_result(l, j):
        total = sum_wait(SUM_DATTN[l], j)
        source = n.X0 if l == 0 else n.Y0
        unit, scale = unit_rows(source[own_of(j), :].astype(F32))
        n.GACC[l, 0:1, :] += jnp.sum(total * unit, axis=0, keepdims=True)
        gain = n.GAINS[2 * l : 2 * l + 1, :]
        return n.DMID[own_of(j), :] + norm_back(unit, scale, gain, total)

    def attn_back_sum(l, j):
        own = half_of(j, s)
        if l == 1:
            n.DR[own, :] = attn_back_result(l, j).astype(BF16)
            pair_start(PAIR_DR, n.DR, j)
            give_out(3, 1, n.DR.at[own], n.igr, j)
        else:

            @pl.when(lax.rem(j, 2) == x)
            def _():
                n.PART[1, own, :] = attn_back_result(l, j).astype(BF16)
                give_out(1, 0, n.PART.at[1, own], n.igr, j)

            @pl.when(lax.rem(j, 2) != x)
            def _():
                sum_sent(SUM_DATTN[l], j)

    long = width // 2
    grad_order = ((1, 2), (1, 1), (1, 0), (0, 2), (0, 1), (0, 0))
    grad_to = 2 * s + x

    def kept_here(l):
        return hub & (s == l)

    def grad_sent(l, p, i):
        if not inside:
            done(n.STG.at[i], n.stg_send.at[l, p, i])
            return

        @pl.when(jnp.logical_not(kept_here(l)))
        def _():
            done(n.STG.at[i], n.stg_send.at[l, p, i])

    def weight_grad(l, p, i):
        at = grad_order.index((l, p))
        if at > 0:
            grad_sent(*grad_order[at - 1], i)
        rows = pl.ds(pl.multiple_of(i * long, long), long)
        if p == 0:
            left = n.N1[l, :, rows]
            n.STG[i, :, 0:256] = tn(left, n.DQKV[:, 0:256]).astype(BF16)
            n.STG[i, :, 256:512] = tn(left, n.DQKV[:, 256:512]).astype(BF16)
            last = tn(left, n.DQKV[:, 512:o_columns])
            out_part = tn(n.DA[l, :, rows], n.ATT[l])
            n.STG[i, :, 512:width] = jnp.concatenate([last, out_part[:, HEAD:]], axis=1).astype(
                BF16
            )
        else:
            if p == 1:
                left, right = n.N2[l, :, rows], n.DPRE
            else:
                left, right = (n.CT if l == 1 else n.DR)[:, rows], n.HID
            for k in range(tiles):
                here = slice(k * TILE, (k + 1) * TILE)
                n.STG[i, :, here] = tn(left, right[:, here]).astype(BF16)
        if not inside:
            pltpu.make_async_copy(
                n.STG.at[i], n.grads.at[l, p, rows], n.stg_send.at[l, p, i]
            ).start()
            return

        @pl.when(kept_here(l))
        def _():
            n.GR[0, p, rows, :] = n.STG[i]

        @pl.when(jnp.logical_not(kept_here(l)))
        def _():
            way = jnp.where(hub, 0, 1)
            remote(
                n.STG.at[i],
                n.GR.at[way, p, rows],
                n.stg_send.at[l, p, i],
                n.gr_recv.at[way, p, i],
                (l, grad_to, z),
            ).start()

    def slot_of(source, target):
        return jnp.where(source > target, source - 1, source)

    def grad_pass(l, p, i):
        if not inside:
            return

        @pl.when(s == l)
        def _():
            rows = pl.ds(pl.multiple_of(i * long, long), long)

            @pl.when(jnp.logical_not(hub))
            def _():
                done(n.GR.at[0, p, rows], n.gr_recv.at[0, p, i])

            done(n.GR.at[1, p, rows], n.gr_recv.at[1, p, i])
            for k in range(depth // 2):
                far = i * (depth // 2) + k

                @pl.when(z != far)
                def _():
                    here = slab_of(far)
                    n.GR[0, p, here, :] = (
                        n.GR[0, p, here, :].astype(F32) + n.GR[1, p, here, :].astype(F32)
                    ).astype(BF16)
                    slot = slot_of(z, far)
                    remote(
                        n.GR.at[0, p, here],
                        n.ZR.at[slot, p],
                        n.z_send.at[p, far],
                        n.z_recv.at[p, slot],
                        (s, t, far),
                    ).start()

    def grad_final(l, p):
        if not inside:
            return

        @pl.when(s == l)
        def _():
            here = slab_of(z)
            total = n.GR[0, p, here, :].astype(F32) + n.GR[1, p, here, :].astype(F32)
            for slot in range(depth - 1):
                done(n.ZR.at[slot, p], n.z_recv.at[p, slot])
                total = total + n.ZR[slot, p].astype(F32)
            n.FIN[p] = total
            pltpu.make_async_copy(n.FIN.at[p], n.gsum.at[p], n.fin_send.at[p]).start()

    def grads_done():
        if not inside:
            grad_sent(*grad_order[-1], 0)
            grad_sent(*grad_order[-1], 1)
            return
        grad_sent(*grad_order[-1], 0)
        grad_sent(*grad_order[-1], 1)
        for p in range(PARTS):
            for far in range(depth):

                @pl.when(z != far)
                def _():
                    done(n.ZR.at[0, p], n.z_send.at[p, far])

            done(n.FIN.at[p], n.fin_send.at[p])

    def gains_send():
        if not inside:
            n.GAINS[...] = n.gain_rows[...]
            return
        n.GIN[s, z] = n.gain_rows[...]
        for c in range(2):
            for far in range(depth):

                @pl.when((s != c) | (z != far))
                def _():
                    remote(
                        n.gain_rows,
                        n.GIN.at[s, z],
                        n.gin_send.at[c, far],
                        n.gin_recv.at[s, z],
                        (c, t, far),
                    ).start()

    def gains_wait():
        if not inside:
            return
        for c in range(2):
            for far in range(depth):

                @pl.when((s != c) | (z != far))
                def _():
                    done(n.gain_rows, n.gin_recv.at[c, far])
                    done(n.gain_rows, n.gin_send.at[c, far])

                for k in range(2):
                    n.GAINS[2 * c + k : 2 * c + k + 1, far * slab : (far + 1) * slab] = n.GIN[
                        c, far, k : k + 1, 0:slab
                    ]

    def gain_grads(step):
        if not inside:
            return
        if step == 0:
            remote(n.GACC.at[1 - s], n.GC, n.gg_send.at[0], n.gg_recv.at[0], mate).start()
        elif step == 1:
            done(n.GC, n.gg_recv.at[0])
            n.GACC[s] += n.GC[...]
            remote(n.GACC.at[s], n.GX, n.gg_send.at[6], n.gg_recv.at[4], peer_x).start()
        elif step == 2:
            done(n.GX, n.gg_recv.at[4])
            done(n.GX, n.gg_send.at[6])
            row = lax.broadcasted_iota(jnp.int32, n.GX.shape, 0)
            n.GACC[s] += jnp.where((row == 0) & (s == 0), n.GX[...], 0.0)
            remote(n.GACC.at[s], n.GY, n.gg_send.at[1], n.gg_recv.at[1], peer_y).start()
        else:
            done(n.GY, n.gg_recv.at[1])
            n.GC[...] = n.GACC[s] + n.GY[...]
            for far in range(depth):

                @pl.when(z != far)
                def _():
                    slot = slot_of(z, far)
                    remote(
                        n.GC,
                        n.GZ.at[slot],
                        n.gg_send.at[2 + far],
                        n.gg_recv.at[5 + slot],
                        (s, t, far),
                    ).start()

    def gain_grads_done():
        if not inside:
            n.gain_out[...] = jnp.concatenate([n.GACC[0, 0:2], n.GACC[1, 0:2], n.GACC[0, 4:8]])
            return
        total = n.GC[...]
        for slot in range(depth - 1):
            done(n.GZ.at[slot], n.gg_recv.at[5 + slot])
            total = total + n.GZ[slot]
        n.gain_out[...] = total
        done(n.GC, n.gg_send.at[0])
        done(n.GC, n.gg_send.at[1])
        for far in range(depth):

            @pl.when(z != far)
            def _():
                done(n.GC, n.gg_send.at[2 + far])

    tasks = {"none": lambda h, j: None}
    for l in range(2):
        tasks[f"nq{l}"] = lambda h, j, l=l: qkv_product(l, j)
        tasks[f"at{l}"] = lambda h, j, l=l: heads_loop(attend, l, j, h)
        tasks[f"op{l}"] = lambda h, j, l=l: out_product(l, j)
        tasks[f"sa{l}"] = lambda h, j, l=l: attn_sum(l, j)
        tasks[f"ud{l}"] = lambda h, j, l=l: up_product(l, j)
        tasks[f"sm{l}"] = lambda h, j, l=l: mlp_sum(l, j)
        tasks[f"hu{l}"] = lambda h, j, l=l: hidden_back(l, j)
        tasks[f"sd{l}"] = lambda h, j, l=l: mlp_back_sum(l, j)
        tasks[f"ag{l}"] = lambda h, j, l=l: attn_grad(l, j)
        tasks[f"ab{l}"] = lambda h, j, l=l: heads_loop(attend_back, l, j, h)
        tasks[f"qb{l}"] = lambda h, j, l=l: qkv_back(l, j)
        tasks[f"sb{l}"] = lambda h, j, l=l: attn_back_sum(l, j)
        for p in range(PARTS):
            tasks[f"wg{l}{p}"] = lambda h, j, l=l, p=p: weight_grad(l, p, j)
    for p in range(PARTS):
        tasks[f"ws{p}"] = lambda h, j, p=p: weights_send(1, p)
        tasks[f"wt{p}"] = lambda h, j, p=p: weights_send(0, p)
    tasks["r"] = lambda h, j: sum_pass(h, j)
    tasks["x0"] = lambda h, j: inputs_pass(j)
    tasks["x1"] = lambda h, j: cotangent_pass(j)
    tasks["wr"] = lambda h, j: weights_relay(lax.div(h, PARTS), lax.rem(h, PARTS), j)
    tasks["ww"] = lambda h, j: weights_wait(h, j)
    tasks["gp"] = lambda h, j: grad_pass(lax.div(j, 2), h, lax.rem(j, 2))
    tasks["gf"] = lambda h, j: grad_final(j, h)
    for step in range(4):
        tasks[f"gg{step}"] = lambda h, j, step=step: gain_grads(step)
    tasks["gw"] = lambda h, j: gains_wait()
    tasks["cs"] = lambda h, j: spread(1, n.cot, n.CT)
    used = {"none"} | {name for name, _, _ in steps}
    order = [name for name in tasks if name in used]
    run = [tasks[name] for name in order]

    weights_send(0, 0)
    gains_send()
    spread(0, n.inp, n.X0)
    n.GACC[...] = jnp.zeros_like(n.GACC)

    group = 12
    codes = [order.index(name) * 32 + h * 4 + j for name, h, j in steps]
    codes += [0] * (-len(codes) % group)
    pairs = [codes[i] + 4096 * codes[i + 1] for i in range(0, len(codes), 2)]
    per_group = group // 2
    groups = len(pairs) // per_group

    def dispatch(low, high, op, h, j):
        if high - low == 1:
            run[low](h, j)
            return
        middle = (low + high) // 2
        lax.cond(
            op < middle,
            lambda: dispatch(low, middle, op, h, j),
            lambda: dispatch(middle, high, op, h, j),
        )

    @pl.loop(0, groups)
    def _(g):
        words = [
            pick(g, [pairs[q * per_group + w] for q in range(groups)]) for w in range(per_group)
        ]

        @pl.loop(0, group)
        def _(i):
            word = pick(lax.div(i, 2), words)
            code = jnp.where(lax.rem(i, 2) == 0, lax.rem(word, 4096), lax.div(word, 4096))
            dispatch(
                0, len(run), lax.div(code, 32), lax.rem(lax.div(code, 4), 8), lax.rem(code, 4)
            )

    if inside:
        for p in range(PARTS):
            weights_sent(p)
            for l in range(2):

                @pl.when(hub)
                def _():
                    for far in range(depth):
                        done(n.W.at[l, p, slab_of(far)], n.relay_send.at[l, p, far])

    spread_done(0)
    spread_done(1)

    @pl.loop(0, CHUNKS)
    def _(j):
        for stage in range(7):
            done(bytes_of(part), n.pair_send.at[stage, j])
        for which, section in ((1, 0), (2, 0), (3, 1)):
            given_out(which, section, j)

    for which, section in ((0, 1), (1, 0), (2, 0), (3, 1)):
        got_out(which, section)
    grads_done()
    gain_grads_done()


STEPS = (
    ("cs", 0, 0), ("wt1", 0, 0), ("wr", 0, 1), ("wt2", 0, 0), ("wr", 0, 3), ("wr", 0, 0),
    ("wr", 0, 2), ("gw", 0, 0), ("wr", 1, 0), ("wr", 1, 1), ("x0", 0, 2), ("ww", 0, 0),
    ("x0", 0, 1), ("x0", 0, 0), ("x0", 0, 3), ("nq0", 0, 2), ("nq0", 0, 0), ("nq0", 0, 1),
    ("wr", 2, 0), ("nq0", 0, 3), ("at0", 0, 2), ("ws0", 0, 0), ("at0", 3, 1), ("wr", 2, 2),
    ("op0", 0, 1), ("at0", 1, 2), ("at0", 2, 2), ("wr", 1, 3), ("at0", 0, 3), ("r", 0, 1),
    ("wr", 2, 1), ("at0", 3, 0), ("at0", 1, 3), ("op0", 0, 2), ("wr", 2, 3), ("wr", 1, 2),
    ("ws2", 0, 0), ("op0", 0, 0), ("ws1", 0, 0), ("at0", 2, 3), ("r", 0, 0), ("ww", 0, 1),
    ("r", 0, 2), ("op0", 0, 3), ("sa0", 0, 1), ("wr", 3, 0), ("sa0", 0, 0), ("ww", 0, 2),
    ("wr", 3, 2), ("r", 0, 3), ("wr", 4, 0), ("x1", 0, 3), ("ud0", 0, 1), ("sa0", 0, 2),
    ("wr", 3, 3), ("r", 1, 1), ("ud0", 0, 0), ("sa0", 0, 3), ("r", 1, 0), ("wr", 3, 1),
    ("wr", 5, 2), ("ud0", 0, 3), ("sm0", 0, 1), ("ud0", 0, 2), ("wr", 5, 0), ("r", 1, 2),
    ("x1", 0, 2), ("ww", 1, 0), ("sm0", 0, 0), ("nq1", 0, 1), ("nq1", 0, 0), ("sm0", 0, 2),
    ("x1", 0, 1), ("r", 1, 3), ("at1", 3, 0), ("op1", 0, 0), ("wr", 4, 1), ("wr", 5, 1),
    ("at1", 3, 1), ("nq1", 0, 2), ("r", 2, 0), ("at1", 1, 2), ("at1", 0, 2), ("wr", 5, 3),
    ("op1", 0, 1), ("sm0", 0, 3), ("at1", 2, 2), ("op1", 0, 2), ("wr", 4, 2), ("r", 2, 1),
    ("nq1", 0, 3), ("r", 2, 2), ("x1", 0, 0), ("at1", 2, 3), ("wr", 4, 3), ("at1", 0, 3),
    ("at1", 1, 3), ("sa1", 0, 0), ("sa1", 0, 1), ("op1", 0, 3), ("r", 2, 3), ("ww", 1, 2),
    ("ww", 1, 1), ("ud1", 0, 1), ("sa1", 0, 2), ("r", 3, 1), ("ud1", 0, 2), ("ud1", 0, 0),
    ("sa1", 0, 3), ("r", 3, 2), ("hu1", 0, 0), ("ud1", 0, 3), ("hu1", 0, 2), ("r", 3, 3),
    ("sm1", 0, 2), ("hu1", 0, 3), ("sm1", 0, 3), ("r", 4, 3), ("r", 3, 0), ("hu1", 0, 1),
    ("wg12", 0, 1), ("sm1", 0, 1), ("r", 4, 2), ("r", 4, 1), ("wg12", 0, 0), ("sd1", 0, 3),
    ("ag1", 0, 3), ("ab1", 2, 3), ("ab1", 1, 3), ("ab1", 0, 3), ("sd1", 0, 2), ("qb1", 0, 3),
    ("wg11", 0, 1), ("ag1", 0, 2), ("r", 5, 3), ("wg11", 0, 0), ("ab1", 2, 2), ("gp", 2, 2),
    ("ab1", 1, 2), ("ab1", 0, 2), ("sm1", 0, 0), ("r", 4, 0), ("qb1", 0, 2), ("sb1", 0, 3),
    ("r", 5, 2), ("gp", 2, 3), ("hu0", 0, 3), ("gp", 1, 3), ("sd1", 0, 1), ("r", 6, 3),
    ("sd1", 0, 0), ("ag1", 0, 1), ("ab1", 3, 1), ("qb1", 0, 1), ("ag1", 0, 0), ("ab1", 3, 0),
    ("qb1", 0, 0), ("gp", 1, 2), ("wg10", 0, 0), ("r", 5, 1), ("sd0", 0, 3), ("sb1", 0, 2),
    ("wg10", 0, 1), ("ag0", 0, 3), ("r", 5, 0), ("ab0", 0, 3), ("hu0", 0, 2), ("sb1", 0, 1),
    ("ab0", 1, 3), ("r", 6, 2), ("sb1", 0, 0), ("gp", 0, 2), ("ab0", 2, 3), ("hu0", 0, 0),
    ("sd0", 0, 2), ("hu0", 0, 1), ("wg02", 0, 0), ("qb0", 0, 3), ("gp", 0, 3), ("wg02", 0, 1),
    ("r", 6, 1), ("wg01", 0, 0), ("ag0", 0, 2), ("r", 7, 3), ("ab0", 0, 2), ("sd0", 0, 1),
    ("r", 6, 0), ("ab0", 1, 2), ("ab0", 2, 2), ("gp", 2, 0), ("qb0", 0, 2), ("wg01", 0, 1),
    ("ag0", 0, 1), ("sd0", 0, 0), ("gp", 2, 1), ("ab0", 3, 1), ("qb0", 0, 1), ("r", 7, 1),
    ("ag0", 0, 0), ("gf", 1, 1), ("ab0", 3, 0), ("sb0", 0, 3), ("qb0", 0, 0), ("r", 7, 0),
    ("wg00", 0, 0), ("gp", 1, 0), ("wg00", 0, 1), ("gf", 2, 0), ("r", 7, 2), ("sb0", 0, 1),
    ("gf", 2, 1), ("gp", 1, 1), ("gp", 0, 0), ("sb0", 0, 0), ("sb0", 0, 2), ("gg0", 0, 0),
    ("gg1", 0, 0), ("gg2", 0, 0), ("gp", 0, 1), ("gf", 1, 0), ("gf", 0, 1), ("gg3", 0, 0),
    ("gf", 0, 0),
)


def run_blocks(inputs, cotangent, weights, gain_rows, bias, depth, inside):
    buckets, chunk, width = inputs.shape
    rows = CHUNKS * chunk
    part = chunk // 2
    heads = width // 4 // HEAD
    vmem, dma = pltpu.VMEM, pltpu.SemaphoreType.DMA
    scratch = dict(
        W=vmem((2, PARTS, width, width), BF16),
        X0=vmem((CHUNKS * part, width), BF16),
        Y0=vmem((CHUNKS * part, width), BF16),
        CT=vmem((rows, width), BF16),
        DR=vmem((rows, width), BF16),
        N1=vmem((2, rows, width), BF16),
        N2=vmem((2, rows, width), BF16),
        Q=vmem((2, heads, rows, 2 * HEAD), BF16),
        KV=vmem((2, heads, rows, 2 * HEAD), BF16),
        KT=vmem((2, heads, HEAD, rows), BF16),
        VT=vmem((heads, HEAD, rows), BF16),
        ATT=vmem((2, rows, (heads + 1) * HEAD), BF16),
        ATTT=vmem((2, heads, HEAD, rows), F32),
        LSE=vmem((2, heads, 1, rows), F32),
        PRE=vmem((2, rows, width), BF16),
        HID=vmem((rows, width), BF16),
        DPRE=vmem((rows, width), BF16),
        DQKV=vmem((rows, 3 * heads * HEAD), BF16),
        DA=vmem((2, rows, width), BF16),
        DKV=vmem((heads, rows, 2 * HEAD), F32),
        GRAD=vmem((heads, chunk, 2 * HEAD), BF16),
        GRADT=vmem((heads, 1, chunk), F32),
        DQT=vmem((heads, HEAD, chunk), F32),
        MID=vmem((2, CHUNKS * part, width), F32),
        DMID=vmem((CHUNKS * part, width), F32),
        PART=vmem((2, rows, width), BF16),
        RC=vmem((2, CHUNKS, part, width), BF16),
        RX=vmem((3, CHUNKS, part, width), BF16),
        STG=vmem((2, width // 2, width), BF16),
        GAINS=vmem((8, width), F32),
        GACC=vmem((2, 8, width), F32),
        in_send=dma((2, CHUNKS)),
        in_recv=dma((2, CHUNKS)),
        mate_send=dma((CHUNKS,)),
        mate_recv=dma((CHUNKS,)),
        pair_send=dma((7, CHUNKS)),
        pair_recv=dma((7, CHUNKS)),
        rs_send=dma((8, 2, CHUNKS)),
        rs_recv=dma((8, 2, CHUNKS)),
        w_recv=dma((2, PARTS, depth if inside else 1)),
        stg_send=dma((2, PARTS, 2)),
        out_send=dma((4, CHUNKS)),
        out_recv=dma((4, 2, 2)),
    )
    outs = dict(
        acts=jax.ShapeDtypeStruct(inputs.shape, BF16), igr=jax.ShapeDtypeStruct(inputs.shape, BF16)
    )
    if inside:
        slab = width // depth
        scratch.update(
            GR=vmem((2, PARTS, width, width), BF16),
            ZR=vmem((depth - 1, PARTS, slab, width), BF16),
            FIN=vmem((PARTS, slab, width), F32),
            GIN=vmem((2, depth) + gain_rows.shape, F32),
            GC=vmem((8, width), F32),
            GX=vmem((8, width), F32),
            GY=vmem((8, width), F32),
            GZ=vmem((depth - 1, 8, width), F32),
            w_send=dma((PARTS, depth)),
            relay_send=dma((2, PARTS, depth)),
            gr_recv=dma((2, PARTS, 2)),
            z_send=dma((PARTS, depth)),
            z_recv=dma((PARTS, depth - 1)),
            fin_send=dma((PARTS,)),
            gin_send=dma((2, depth)),
            gin_recv=dma((2, depth)),
            gg_send=dma((3 + depth,)),
            gg_recv=dma((4 + depth,)),
        )
        own = dict(own_a=weights[0], own_b=weights[1], own_c=weights[2])
        outs["gsum"] = jax.ShapeDtypeStruct((PARTS, slab, width), F32)
    else:
        own = dict(w_whole=weights)
        outs["grads"] = jax.ShapeDtypeStruct(weights.shape, BF16)
    outs["gain_out"] = jax.ShapeDtypeStruct((8, width), F32)
    given = dict(inp=inputs, cot=cotangent, **own, gain_rows=gain_rows, bias=bias)
    hbm = pl.BlockSpec(memory_space=pl.ANY)
    in_vmem = pl.BlockSpec(memory_space=pltpu.VMEM)
    small = ("gain_rows", "bias", "gain_out")
    return pl.pallas_call(
        functools.partial(
            block_kernel, inside, STEPS, list(given) + list(outs) + list(scratch)
        ),
        out_shape=tuple(outs.values()),
        in_specs=[in_vmem if name in small else hbm for name in given],
        out_specs=tuple(in_vmem if name in small else hbm for name in outs),
        scratch_shapes=list(scratch.values()),
        compiler_params=pltpu.CompilerParams(
            collective_id=0, has_side_effects=True, vmem_limit_bytes=VMEM_LIMIT
        ),
        cost_estimate=pl.CostEstimate(
            flops=27_000_000_000, bytes_accessed=40_000_000, transcendentals=20_000_000
        ),
        name="blocks",
    )(*given.values())


def shards(inputs, lengths, gains, w_qkv, w_out, w_up, w_down, cotangent):
    local_rows, width = inputs.shape[1:]
    slab = w_up.shape[1]
    heads = w_qkv.shape[3] // HEAD
    depth = lax.axis_size("dp")
    y = lax.div(lax.axis_index("tensor"), 2)
    section = lax.axis_index("section")
    inside = slab % 16 == 0 and depth == 4
    split = (slab, heads, HEAD)
    kv = jnp.stack([w_qkv[0, :, 1].reshape(split), w_qkv[0, :, 2].reshape(split)], axis=2)
    own = (
        jnp.concatenate([kv.reshape(slab, -1), w_qkv[0, :, 0], w_out[0].T], axis=1),
        w_up[0],
        w_down[0].T,
    )
    bias = jnp.where(lengths[y] == CHUNKS * local_rows, 0.0, MASKED).astype(F32)
    bias = jnp.broadcast_to(bias, (8, local_rows))
    axes = ("section", "tensor")
    if inside:
        gain_rows = jnp.pad(gains[0].astype(F32), ((0, 6), (0, -slab % 128)))
        acts, input_grads, total, gain_part = run_blocks(
            inputs, cotangent, own, gain_rows, bias, depth, inside
        )
        gain_part = gain_part[None, :2]
        at = lax.axis_index("tensor") * depth + lax.axis_index("dp")
        share = width // (depth * lax.axis_size("tensor"))
        gain_grads = lax.dynamic_slice_in_dim(gain_part, at * share, share, 2)
    else:
        whole = lax.all_gather(jnp.stack(own), "dp", axis=1, tiled=True)
        weights = []
        for l in range(2):
            parts = []
            for to_y in range(2):
                pairs = [
                    (4 * l + 2 * c + x, 4 * c + 2 * to_y + x) for c in range(2) for x in range(2)
                ]
                parts.append(lax.ppermute(whole, axes, pairs))
            weights.append(jnp.where(y == 0, parts[0], parts[1]))
        weights = jnp.stack(weights)
        gain_rows = lax.all_gather(gains, "dp", axis=2, tiled=True)
        gain_rows = lax.all_gather(gain_rows, "section", axis=0, tiled=True)
        gain_rows = jnp.pad(gain_rows.reshape(4, width).astype(F32), ((0, 4), (0, 0)))
        acts, input_grads, partial, gain_part = run_blocks(
            inputs, cotangent, weights, gain_rows, bias, depth, inside
        )
        total = jnp.zeros(partial.shape[1:], F32)
        for l in range(2):
            for from_y in range(2):
                pairs = [
                    (4 * c + 2 * from_y + x, 4 * l + 2 * c + x) for c in range(2) for x in range(2)
                ]
                total = total + lax.ppermute(partial[l], axes, pairs).astype(F32)
        total = lax.psum_scatter(total.astype(BF16), "dp", scatter_dimension=1, tiled=True)
        total = total.astype(F32)
        gain_part = lax.psum(gain_part[:4].reshape(2, 2, width), "section")
        gain_part = lax.dynamic_slice_in_dim(gain_part, section, 1, 0)
        first = (section == 0) & (jnp.arange(2) == 0)
        gain_part = gain_part * jnp.where(first, 1.0, 0.5)[None, :, None]
        gain_grads = lax.psum_scatter(
            gain_part, ("tensor", "dp"), scatter_dimension=2, tiled=True
        )
    columns = heads * HEAD
    kv = total[0, :, : 2 * columns].reshape(slab, heads, 2, HEAD)
    q = total[0, :, 2 * columns : 3 * columns]
    qkv_grads = jnp.stack([q, kv[:, :, 0].reshape(q.shape), kv[:, :, 1].reshape(q.shape)], axis=1)
    return (
        acts[None],
        input_grads[None],
        gain_grads,
        qkv_grads[None],
        total[0, :, 3 * columns :].T[None],
        total[1][None],
        total[2].T[None],
    )


def solution(mesh):
    in_specs = (
        P("dp", "tensor", None),
        P("dp"),
        P("section", None, "dp"),
        P("section", "dp", None, "tensor"),
        P("section", "tensor", "dp"),
        P("section", "dp", "tensor"),
        P("section", "tensor", "dp"),
        P("dp", "tensor", None),
    )
    out_specs = (
        P("section", "dp", "tensor", None),
        P("section", "dp", "tensor", None),
        P("section", None, ("tensor", "dp")),
        P("section", "dp", None, "tensor"),
        P("section", "tensor", "dp"),
        P("section", "dp", "tensor"),
        P("section", "tensor", "dp"),
    )
    return jax.shard_map(shards, mesh=mesh, in_specs=in_specs, out_specs=out_specs, check_vma=False)
```

```python
import functools

import jax
import jax.numpy as jnp
from jax import lax
from jax.experimental import pallas as pl
from jax.experimental.pallas import tpu as pltpu
from jax.sharding import PartitionSpec as P

HEAD = 64
EPSILON = 1e-05
MASKED = -1e30
CHUNKS = 4
PARTS = 3
VMEM_LIMIT = 63 << 20
TILE = 256
BF16 = jnp.bfloat16
F32 = jnp.float32
MESH = pl.DeviceIdType.MESH

SUM_ATTN = (0, 2)
SUM_MLP = (1, 3)
SUM_DMLP = (6, 4)
SUM_DATTN = (7, 5)
PAIR_N2 = (0, 1)
PAIR_N1 = (6, 2)
PAIR_DA = (4, 3)
PAIR_DR = 5


def nn(left, right):
    return lax.dot_general(left, right, (((1,), (0,)), ((), ())), preferred_element_type=F32)


def nt(left, right):
    return lax.dot_general(left, right, (((1,), (1,)), ((), ())), preferred_element_type=F32)


def tn(left, right):
    return lax.dot_general(left, right, (((0,), (0,)), ((), ())), preferred_element_type=F32)


def unit_rows(rows):
    centre = rows - jnp.mean(rows, axis=-1, keepdims=True)
    spread = jnp.mean(centre * centre, axis=-1, keepdims=True)
    scale = lax.rsqrt(spread + EPSILON)
    return centre * scale, scale


def norm_back(unit, scale, gain, grad):
    wide = grad * gain
    inner = jnp.mean(wide * unit, axis=-1, keepdims=True)
    return scale * (wide - jnp.mean(wide, axis=-1, keepdims=True) - unit * inner)


def gelu_parts(x):
    root = 0.7978845608028654
    square = x * x
    bend = jnp.tanh(root * x * (1.0 + 0.044715 * square))
    half = 0.5 + 0.5 * bend
    slope = half + 0.5 * x * (1.0 - bend * bend) * (root * (1.0 + 0.134145 * square))
    return x * half, slope


class Names:
    pass


def block_kernel(inside, steps, names, *refs):
    n = Names()
    for name, ref in zip(names, refs, strict=True):
        setattr(n, name, ref)
    s = lax.axis_index("section")
    t = lax.axis_index("tensor")
    z = lax.axis_index("dp")
    x = lax.rem(t, 2)
    y = lax.div(t, 2)
    t_y = 2 * (1 - y) + x
    mate = (1 - s, t, z)
    peer_x = (s, 2 * y + 1 - x, z)
    peer_y = (s, t_y, z)
    hub = s == y
    rows_all, width = n.CT.shape
    chunk = rows_all // CHUNKS
    part = chunk // 2
    half = CHUNKS // 2
    heads = n.KT.shape[1]
    tiles = width // TILE
    depth = lax.axis_size("dp")
    slab = width // depth
    q_columns = 2 * heads * HEAD
    o_columns = 3 * heads * HEAD

    def remote(src, dst, send_sem, recv_sem, device):
        return pltpu.make_async_remote_copy(
            src_ref=src,
            dst_ref=dst,
            send_sem=send_sem,
            recv_sem=recv_sem,
            device_id=device,
            device_id_type=MESH,
        )

    def done(ref, sem):
        pltpu.make_async_copy(ref, ref, sem).wait()

    def rows_of(j):
        return pl.ds(pl.multiple_of(j * chunk, chunk), chunk)

    def half_of(j, c):
        return pl.ds(pl.multiple_of(j * chunk + c * part, part), part)

    def own_of(j):
        return pl.ds(pl.multiple_of(j * part, part), part)

    def slab_of(i):
        return pl.ds(pl.multiple_of(i * slab, slab), slab)

    def bytes_of(count):
        return n.PART.at[0, 0:count]

    barrier = pltpu.get_barrier_semaphore()
    greeted = 0
    for other_s in range(2):
        for other in range(CHUNKS):
            greeted += 1

            @pl.when((s != other_s) | (t != other))
            def _():
                pl.semaphore_signal(
                    barrier, inc=1, device_id=(other_s, other, z), device_id_type=MESH
                )

        if inside:
            for other in range(depth):
                greeted += 1

                @pl.when(z != other)
                def _():
                    pl.semaphore_signal(
                        barrier, inc=1, device_id=(other_s, t, other), device_id_type=MESH
                    )

    pl.semaphore_wait(barrier, greeted - 1 - (2 if inside else 0))

    def pick(index, values):
        value = values[0]
        for at in range(1, len(values)):
            value = jnp.where(index == at, values[at], value)
        return value

    def not_far(end):
        if end == 0:
            return z < depth // 2
        if end == depth - 1:
            return z >= depth // 2
        return z >= 0

    def weights_send(l, p):
        if not inside:
            pltpu.make_async_copy(n.w_whole.at[l, p], n.W.at[l, p], n.w_recv.at[l, p, 0]).start()
            return
        own = (n.own_a, n.own_b, n.own_c)[p]

        @pl.when(s == l)
        def _():
            for far in range(depth):
                @pl.when(hub & (z == far))
                def _():
                    pltpu.make_async_copy(
                        own, n.W.at[l, p, slab_of(z)], n.w_recv.at[l, p, z]
                    ).start()

                @pl.when(jnp.logical_not(hub & (z == far)) & not_far(far))
                def _():
                    remote(
                        own,
                        n.W.at[l, p, slab_of(z)],
                        n.w_send.at[p, far],
                        n.w_recv.at[l, p, z],
                        (y, t, far),
                    ).start()

    def weights_sent(p):
        own = (n.own_a, n.own_b, n.own_c)[p]
        for far in range(depth):

            @pl.when(jnp.logical_not(hub & (z == far)) & not_far(far))
            def _():
                done(own, n.w_send.at[p, far])

    def weights_relay(l, p, step):
        if not inside:
            return

        @pl.when(hub)
        def _():
            beside = z + 1 - 2 * lax.rem(z, 2)
            low = z < 2
            far = pick(step, [z, beside, jnp.where(low, 2, 1), jnp.where(low, 3, 0)])
            here = n.W.at[l, p, slab_of(far)]
            done(here, n.w_recv.at[l, p, far])
            remote(
                here, here, n.relay_send.at[l, p, far], n.w_recv.at[l, p, far], peer_y
            ).start()
            for place, end in ((1, 0), (2, 3)):

                @pl.when((z == place) & (far >= 2 if place == 1 else far < 2))
                def _():
                    remote(
                        here,
                        here,
                        n.onward_send.at[l, p, far],
                        n.w_recv.at[l, p, far],
                        (s, t, end),
                    ).start()

    def weights_wait(l, p):
        if not inside:
            done(n.W.at[l, p], n.w_recv.at[l, p, 0])
            return

        @pl.when(jnp.logical_not(hub))
        def _():
            for far in range(depth):
                done(n.W.at[l, p, slab_of(far)], n.w_recv.at[l, p, far])

    t_x = 2 * y + 1 - x
    t_far = 2 * (1 - y) + 1 - x

    def landing(which, target, source_t):
        return target.at[own_of(source_t)] if which == 0 else target.at[half_of(source_t, s)]

    def spread(which, source, target):
        here = source.at[y, half_of(0, s)]
        own = landing(which, target, t)
        remote(
            source.at[1 - y, half_of(0, s)],
            own,
            n.in_send.at[which, 0],
            n.in_recv.at[which, t],
            peer_y,
        ).start()
        remote(here, own, n.in_send.at[which, 1], n.in_recv.at[which, t], peer_x).start()
        pltpu.make_async_copy(here, own, n.in_recv.at[which, t]).start()

    def spread_pass(which, target):
        near = landing(which, target, t_y)
        done(near, n.in_recv.at[which, t_y])
        remote(near, near, n.in_send.at[which, 2], n.in_recv.at[which, t_y], peer_x).start()

    def spread_wait(which, j):
        @pl.when(j != t_y)
        def _():
            done(bytes_of(part), n.in_recv.at[which, j])

    def inputs_pass(j):
        spread_wait(0, j)
        norm_first(0, n.X0[own_of(j), :].astype(F32), j)

    def cotangent_pass(j):
        here = n.CT.at[half_of(j, s)]
        spread_wait(1, j)
        remote(here, here, n.mate_send.at[j], n.mate_recv.at[j], mate).start()

    def cotangent_wait(j):
        done(bytes_of(part), n.mate_recv.at[j])

    def spread_done(which):
        for way in range(3):
            done(bytes_of(part), n.in_send.at[which, way])
        if which == 1:
            for j in range(CHUNKS):
                done(bytes_of(part), n.mate_send.at[j])

    def pair_start(stage, ref, j):
        here = ref.at[half_of(j, s)]
        remote(here, here, n.pair_send.at[stage, j], n.pair_recv.at[stage, j], mate).start()

    def pair_wait(stage, j):
        done(bytes_of(part), n.pair_recv.at[stage, j])

    def sum_start(stage, j):
        b = stage % 2
        remote(
            n.PART.at[b, half_of(j, 1 - s)],
            n.RC.at[b, j],
            n.rs_send.at[stage, 0, j],
            n.rs_recv.at[stage, 0, j],
            mate,
        ).start()

    def sum_pass(stage, j):
        b = lax.rem(stage, 2)
        here = half_of(j, s)
        done(n.RC.at[b, j], n.rs_recv.at[stage, 0, j])
        n.PART[b, here, :] = (
            n.PART[b, here, :].astype(F32) + n.RC[b, j].astype(F32)
        ).astype(BF16)
        arriving = jnp.where(stage == SUM_DMLP[1], 2, b)
        one_way = (stage == SUM_MLP[1]) | (stage == SUM_DATTN[0])

        @pl.when(jnp.logical_not(one_way) | (lax.rem(j, 2) != x))
        def _():
            remote(
                n.PART.at[b, here],
                n.RX.at[arriving, j],
                n.rs_send.at[stage, 1, j],
                n.rs_recv.at[stage, 1, j],
                peer_x,
            ).start()

        done(n.RC.at[b, j], n.rs_send.at[stage, 0, j])

    def sum_sent(stage, j):
        done(n.RX.at[stage % 2, j], n.rs_send.at[stage, 1, j])

    def sum_wait(stage, j):
        b = stage % 2
        arriving = 2 if stage == SUM_DMLP[1] else b
        done(n.RX.at[arriving, j], n.rs_recv.at[stage, 1, j])
        total = n.PART[b, half_of(j, s), :].astype(F32) + n.RX[arriving, j].astype(F32)
        if stage not in (SUM_MLP[1], SUM_DATTN[0]):
            sum_sent(stage, j)
        return total

    first_index = lax.broadcasted_iota(jnp.int32, (chunk, chunk), 0)
    second_index = lax.broadcasted_iota(jnp.int32, (chunk, chunk), 1)

    def scores(l, st, i, j, diagonal, keys_first):
        if l == 0:
            grown = st * st + 1.0
            inverse = lax.rsqrt(grown)
            magnitude = grown * inverse
            sign = st * inverse
        else:
            inverse, magnitude, sign = None, st, None
        if diagonal:
            seen = first_index <= second_index if keys_first else second_index <= first_index
            magnitude = jnp.where(seen, magnitude, MASKED)
        else:
            apart = (j >= half) & (i < half)
            magnitude = magnitude + jnp.where(apart, n.BIAS[0:1, :], 0.0)
        return inverse, magnitude, sign

    def norm_first(l, own_rows, j):
        unit, _ = unit_rows(own_rows)
        n.N1[l, half_of(j, s), :] = (unit * n.GAINS[2 * l : 2 * l + 1, :]).astype(BF16)
        pair_start(PAIR_N1[l], n.N1.at[l], j)

    def qkv_product(l, j):
        rows = rows_of(j)
        pair_wait(PAIR_N1[l], j)
        kv = nn(n.N1[l, rows, :], n.W[l, 0, :, 0:q_columns])
        kv_low = kv.astype(BF16)
        turned = kv.T.astype(BF16)
        for h in range(heads):
            n.KV[l, h, rows, :] = kv_low[:, 2 * h * HEAD : 2 * (h + 1) * HEAD]
            n.KT[l, h, :, rows] = turned[2 * h * HEAD : (2 * h + 1) * HEAD]
        q = nn(n.N1[l, rows, :], n.W[l, 0, :, q_columns:o_columns]).astype(BF16)
        blank = jnp.zeros((chunk, HEAD), BF16)
        for h in range(heads):
            q_h = q[:, h * HEAD : (h + 1) * HEAD] * jnp.asarray(HEAD**-0.5, BF16)
            n.Q[l, h, rows, :] = jnp.concatenate([q_h, blank], axis=1)

    def attend(l, j):
        rows = rows_of(j)

        def block(i, carry, diagonal):
            keys = rows_of(i)
            new = []
            for h in range(heads):
                top, total, out = carry[h]
                kv = n.KV[l, h, keys, :]
                st = nt(n.Q[l, h, rows, :], kv)
                _, magnitude, sign = scores(l, st, i, j, diagonal, False)
                new_top = jnp.maximum(top, jnp.max(magnitude, axis=1, keepdims=True))
                weights = jnp.exp(magnitude - new_top)
                shrink = jnp.exp(top - new_top)
                total = total * shrink + jnp.sum(weights, axis=1, keepdims=True)
                signed = weights if l == 1 else sign * weights
                out = out * shrink + nn(signed.astype(BF16), kv)
                new.append((new_top, total, out))
            return tuple(new)

        carry = (
            jnp.full((chunk, 1), MASKED, F32),
            jnp.zeros((chunk, 1), F32),
            jnp.zeros((chunk, 2 * HEAD), F32),
        )
        carry = block(j, (carry,) * heads, True)
        carry = lax.fori_loop(0, j, lambda i, c: block(i, c, False), carry)
        lane = lax.broadcasted_iota(jnp.int32, (chunk, 128), 1)
        logs = jnp.zeros((chunk, 128), F32)
        outs = [jnp.zeros((chunk, HEAD), BF16)]
        for h in range(heads):
            top, total, out = carry[h]
            outs.append((out / total)[:, HEAD:].astype(BF16))
            logs = jnp.where(lane == h, top + jnp.log(total), logs)
        n.ATT[l, rows, :] = jnp.concatenate(outs, axis=1)
        n.LSE[l, :, rows] = logs.T[0:8]

    def out_product(l, j):
        rows = rows_of(j)
        for i in range(tiles):
            here = slice(i * TILE, (i + 1) * TILE)
            n.PART[0, rows, here] = nt(
                n.ATT[l, rows, :], n.W[l, 0, here, o_columns - HEAD : width]
            ).astype(BF16)
        sum_start(SUM_ATTN[l], j)

    def attn_sum(l, j):
        source = n.X0 if l == 0 else n.Y0
        own = half_of(j, s)
        middle = source[own_of(j), :].astype(F32) + sum_wait(SUM_ATTN[l], j)
        n.MID[l, own_of(j), :] = middle
        unit, _ = unit_rows(middle)
        n.N2[l, own, :] = (unit * n.GAINS[2 * l + 1 : 2 * l + 2, :]).astype(BF16)
        pair_start(PAIR_N2[l], n.N2.at[l], j)

    def up_product(l, j):
        rows = rows_of(j)
        pair_wait(PAIR_N2[l], j)
        for i in range(tiles):
            here = slice(i * TILE, (i + 1) * TILE)
            pre = nn(n.N2[l, rows, :], n.W[l, 1, :, here])
            n.PRE[l, rows, here] = pre.astype(BF16)
            n.HID[rows, here] = gelu_parts(pre)[0].astype(BF16)
        for i in range(tiles):
            here = slice(i * TILE, (i + 1) * TILE)
            n.PART[1, rows, here] = nt(n.HID[rows, :], n.W[l, 2, here, :]).astype(BF16)
        sum_start(SUM_MLP[l], j)

    def mlp_sum(l, j):
        if l == 0:
            result = (n.MID[l, own_of(j), :] + sum_wait(SUM_MLP[l], j)).astype(BF16)
            n.Y0[own_of(j), :] = result
            norm_first(1, result.astype(F32), j)
            give_out(2, 0, n.Y0.at[own_of(j)], n.acts, j)
        else:

            @pl.when(lax.rem(j, 2) == x)
            def _():
                result = n.MID[l, own_of(j), :] + sum_wait(SUM_MLP[l], j)
                n.PART[1, half_of(j, s), :] = result.astype(BF16)
                give_out(0, 1, n.PART.at[1, half_of(j, s)], n.acts, j)

            @pl.when(lax.rem(j, 2) != x)
            def _():
                sum_sent(SUM_MLP[l], j)

    def give_out(which, section, here, out, j):
        target = out.at[y, half_of(0, s)]

        @pl.when((s == section) & (t == j))
        def _():
            copy = pltpu.make_async_copy(here, target, n.out_send.at[which, j])
            copy.start()
            copy.wait()

        @pl.when((lax.rem(j, 2) == x) & ((s != section) | (t != j)))
        def _():
            remote(
                here,
                target,
                n.out_send.at[which, j],
                n.out_recv.at[which, y, s],
                (section, j, z),
            ).start()

    def given_out(which, section, j):
        @pl.when((lax.rem(j, 2) == x) & ((s != section) | (t != j)))
        def _():
            done(bytes_of(part), n.out_send.at[which, j])

    def got_out(which, section):
        @pl.when(s == section)
        def _():
            for m in range(2):
                for c in range(2):

                    @pl.when((y != m) | (s != c))
                    def _():
                        done(bytes_of(part), n.out_recv.at[which, m, c])

    def hidden_back(l, j):
        rows = rows_of(j)
        if l == 1:
            cotangent_wait(j)
        else:
            pair_wait(PAIR_DR, j)
        source = n.CT if l == 1 else n.DR
        for i in range(tiles):
            here = slice(i * TILE, (i + 1) * TILE)
            back = nn(source[rows, :], n.W[l, 2, :, here])
            hidden, slope = gelu_parts(n.PRE[l, rows, here].astype(F32))
            n.HID[rows, here] = hidden.astype(BF16)
            n.DPRE[rows, here] = (slope * back).astype(BF16)
        for i in range(tiles):
            here = slice(i * TILE, (i + 1) * TILE)
            n.PART[0, rows, here] = nt(n.DPRE[rows, :], n.W[l, 1, here, :]).astype(BF16)
        sum_start(SUM_DMLP[l], j)

    def mlp_back_sum(l, j):
        total = sum_wait(SUM_DMLP[l], j)
        source = n.CT if l == 1 else n.DR
        own = half_of(j, s)
        unit, scale = unit_rows(n.MID[l, own_of(j), :])
        n.GACC[l, 1:2, :] += jnp.sum(total * unit, axis=0, keepdims=True)
        gain = n.GAINS[2 * l + 1 : 2 * l + 2, :]
        grad = source[own, :].astype(F32) + norm_back(unit, scale, gain, total)
        n.DMID[own_of(j), :] = grad
        n.DA[l, own, :] = grad.astype(BF16)
        pair_start(PAIR_DA[l], n.DA.at[l], j)

    def attn_grad(l, j):
        rows = rows_of(j)
        pair_wait(PAIR_DA[l], j)

        @pl.when(j == CHUNKS - 1)
        def _():
            n.DKV[...] = jnp.zeros_like(n.DKV)

        low = nn(n.DA[l, rows, :], n.W[l, 0, :, o_columns - HEAD : width]).astype(BF16)
        product = low.astype(F32) * n.ATT[l, rows, :].astype(F32)
        blank = jnp.zeros((chunk, HEAD), BF16)
        lane = lax.broadcasted_iota(jnp.int32, (chunk, 128), 1)
        inner = jnp.zeros((chunk, 128), F32)
        for h in range(heads):
            here = slice((h + 1) * HEAD, (h + 2) * HEAD)
            n.GRAD[h] = jnp.concatenate([blank, low[:, here]], axis=1)
            inner = jnp.where(
                lane == h, jnp.sum(product[:, here], axis=1, keepdims=True), inner
            )
        n.GRADT[...] = inner.T[0:8]

    def attend_back(l, j):
        rows = rows_of(j)

        def block(i, carry, diagonal):
            keys = rows_of(i)
            new = []
            for h in range(heads):
                kv = n.KV[l, h, keys, :]
                st = nt(kv, n.Q[l, h, rows, :])
                dp = nt(kv, n.GRAD[h])
                inverse, magnitude, sign = scores(l, st, i, j, diagonal, True)
                weights = jnp.exp(magnitude - n.LSE[l, h : h + 1, rows])
                inner = n.GRADT[h : h + 1, :]
                if l == 0:
                    signed = sign * weights
                    ds = weights * (
                        sign * (sign * dp - inner) + dp * (inverse * inverse * inverse)
                    )
                else:
                    signed = weights
                    ds = weights * (dp - inner)
                ds = ds.astype(BF16)
                n.DKV[h, keys, :] += nn(ds, n.Q[l, h, rows, :]) + nn(
                    signed.astype(BF16), n.GRAD[h]
                )
                new.append(carry[h] + nn(n.KT[l, h, :, keys], ds))
            return tuple(new)

        blank = jnp.zeros((HEAD, chunk), F32)
        query_grad = block(j, (blank,) * heads, True)
        query_grad = lax.fori_loop(0, j, lambda i, c: block(i, c, False), query_grad)
        for h in range(heads):
            n.DQT[h] = query_grad[h] * HEAD**-0.5

    def qkv_back(l, j):
        rows = rows_of(j)
        turned = jnp.concatenate([n.DQT[h] for h in range(heads)], axis=0).T
        for h in range(heads):
            n.DQKV[rows, 2 * h * HEAD : 2 * (h + 1) * HEAD] = n.DKV[h, rows, :].astype(BF16)
        n.DQKV[rows, q_columns:] = turned.astype(BF16)
        if l == 1:
            given_out(0, 1, j)
        for i in range(tiles):
            here = slice(i * TILE, (i + 1) * TILE)
            n.PART[1, rows, here] = nt(n.DQKV[rows, :], n.W[l, 0, here, 0:o_columns]).astype(
                BF16
            )
        sum_start(SUM_DATTN[l], j)

    def attn_back_result(l, j):
        total = sum_wait(SUM_DATTN[l], j)
        source = n.X0 if l == 0 else n.Y0
        unit, scale = unit_rows(source[own_of(j), :].astype(F32))
        n.GACC[l, 0:1, :] += jnp.sum(total * unit, axis=0, keepdims=True)
        gain = n.GAINS[2 * l : 2 * l + 1, :]
        return n.DMID[own_of(j), :] + norm_back(unit, scale, gain, total)

    def attn_back_sum(l, j):
        own = half_of(j, s)
        if l == 1:
            n.DR[own, :] = attn_back_result(l, j).astype(BF16)
            pair_start(PAIR_DR, n.DR, j)
            give_out(3, 1, n.DR.at[own], n.igr, j)
        else:

            @pl.when(lax.rem(j, 2) == x)
            def _():
                n.PART[1, own, :] = attn_back_result(l, j).astype(BF16)
                give_out(1, 0, n.PART.at[1, own], n.igr, j)

            @pl.when(lax.rem(j, 2) != x)
            def _():
                sum_sent(SUM_DATTN[l], j)

    long = width // 2
    grad_order = ((1, 2), (1, 1), (1, 0), (0, 2), (0, 1), (0, 0))
    grad_to = 2 * s + x

    def kept_here(l):
        return hub & (s == l)

    def grad_sent(l, p, i):
        if not inside:
            done(n.STG.at[0], n.stg_send.at[l, p, i])
            return

        @pl.when(jnp.logical_not(kept_here(l)))
        def _():
            for k in range(2):
                done(n.STG.at[0, 0:slab], n.stg_send.at[l, p, 2 * i + k])

    def weight_grad(l, p, i):
        at = grad_order.index((l, p))
        slot = 2 * (at % 2) + i
        if at > 1:
            grad_sent(*grad_order[at - 2], i)
        rows = pl.ds(pl.multiple_of(i * long, long), long)
        if p == 0:
            left = n.N1[l, :, rows]
            n.STG[slot, :, 0:256] = tn(left, n.DQKV[:, 0:256]).astype(BF16)
            n.STG[slot, :, 256:512] = tn(left, n.DQKV[:, 256:512]).astype(BF16)
            last = tn(left, n.DQKV[:, 512:o_columns])
            out_part = tn(n.DA[l, :, rows], n.ATT[l])
            n.STG[slot, :, 512:width] = jnp.concatenate([last, out_part[:, HEAD:]], axis=1).astype(
                BF16
            )
        else:
            if p == 1:
                left, right = n.N2[l, :, rows], n.DPRE
            else:
                left, right = (n.CT if l == 1 else n.DR)[:, rows], n.HID
            for k in range(tiles):
                here = slice(k * TILE, (k + 1) * TILE)
                n.STG[slot, :, here] = tn(left, right[:, here]).astype(BF16)
        if not inside:
            pltpu.make_async_copy(
                n.STG.at[slot], n.grads.at[l, p, rows], n.stg_send.at[l, p, i]
            ).start()
            return

        @pl.when(kept_here(l))
        def _():
            n.GR[0, p, rows, :] = n.STG[slot]

        @pl.when(jnp.logical_not(kept_here(l)))
        def _():
            way = jnp.where(hub, 0, 1)
            for k in range(2):
                k_at = jnp.where(i == 0, k, 1 - k)
                at_slab = 2 * i + k_at
                remote(
                    n.STG.at[slot, slab_of(k_at)],
                    n.GR.at[way, p, slab_of(at_slab)],
                    n.stg_send.at[l, p, at_slab],
                    n.gr_recv.at[way, p, at_slab],
                    (l, grad_to, z),
                ).start()

    def slot_of(source, target):
        return jnp.where(source > target, source - 1, source)

    def grad_pass(l, p, far):
        if not inside:
            return

        @pl.when(s == l)
        def _():
            here = slab_of(far)

            @pl.when(jnp.logical_not(hub))
            def _():
                done(n.GR.at[0, p, here], n.gr_recv.at[0, p, far])

            done(n.GR.at[1, p, here], n.gr_recv.at[1, p, far])

            @pl.when(z != far)
            def _():
                n.GR[0, p, here, :] = (
                    n.GR[0, p, here, :].astype(F32) + n.GR[1, p, here, :].astype(F32)
                ).astype(BF16)
                slot = slot_of(z, far)
                remote(
                    n.GR.at[0, p, here],
                    n.ZR.at[slot, p],
                    n.z_send.at[p, far],
                    n.z_recv.at[p, slot],
                    (s, t, far),
                ).start()

    def grad_final(l, p):
        if not inside:
            return

        @pl.when(s == l)
        def _():
            here = slab_of(z)
            total = n.GR[0, p, here, :].astype(F32) + n.GR[1, p, here, :].astype(F32)
            for slot in range(depth - 1):
                done(n.ZR.at[slot, p], n.z_recv.at[p, slot])
                total = total + n.ZR[slot, p].astype(F32)
            slot = lax.rem(p, 2)

            @pl.when(p == 0)
            def _():
                done(n.FIN.at[0], n.fin_send.at[2])

            n.FIN[slot] = total
            pltpu.make_async_copy(n.FIN.at[slot], n.gsum.at[p], n.fin_send.at[p]).start()

    def grads_done():
        if not inside:
            for late in grad_order[-2:]:
                grad_sent(*late, 0)
                grad_sent(*late, 1)
            return
        for late in grad_order[-2:]:
            grad_sent(*late, 0)
            grad_sent(*late, 1)
        for p in range(PARTS):
            for far in range(depth):

                @pl.when(z != far)
                def _():
                    done(n.ZR.at[0, p], n.z_send.at[p, far])

        done(n.FIN.at[0], n.fin_send.at[0])
        done(n.FIN.at[1], n.fin_send.at[1])

    def gains_send():
        if not inside:
            n.GAINS[...] = n.gain_rows[...]
            return
        n.GIN[s, z] = n.gain_rows[...]
        for c in range(2):
            for far in range(depth):

                @pl.when((s != c) | (z != far))
                def _():
                    remote(
                        n.gain_rows,
                        n.GIN.at[s, z],
                        n.gin_send.at[c, far],
                        n.gin_recv.at[s, z],
                        (c, t, far),
                    ).start()

    def gains_wait():
        if not inside:
            return
        for c in range(2):
            for far in range(depth):

                @pl.when((s != c) | (z != far))
                def _():
                    done(n.gain_rows, n.gin_recv.at[c, far])
                    done(n.gain_rows, n.gin_send.at[c, far])

                for k in range(2):
                    n.GAINS[2 * c + k : 2 * c + k + 1, far * slab : (far + 1) * slab] = n.GIN[
                        c, far, k : k + 1, 0:slab
                    ]

    def gain_grads(step):
        if not inside:
            return
        if step == 0:
            remote(n.GACC.at[1 - s], n.GC, n.gg_send.at[0], n.gg_recv.at[0], mate).start()
        elif step == 1:
            done(n.GC, n.gg_recv.at[0])
            n.GACC[s] += n.GC[...]
            remote(n.GACC.at[s], n.GX, n.gg_send.at[6], n.gg_recv.at[4], peer_x).start()
        elif step == 2:
            done(n.GX, n.gg_recv.at[4])
            done(n.GX, n.gg_send.at[6])
            row = lax.broadcasted_iota(jnp.int32, n.GX.shape, 0)
            n.GACC[s] += jnp.where((row == 0) & (s == 0), n.GX[...], 0.0)
            remote(n.GACC.at[s], n.GY, n.gg_send.at[1], n.gg_recv.at[1], peer_y).start()
        else:
            done(n.GY, n.gg_recv.at[1])
            n.GC[...] = n.GACC[s] + n.GY[...]
            for far in range(depth):

                @pl.when(z != far)
                def _():
                    slot = slot_of(z, far)
                    remote(
                        n.GC,
                        n.GZ.at[slot],
                        n.gg_send.at[2 + far],
                        n.gg_recv.at[5 + slot],
                        (s, t, far),
                    ).start()

    def gain_grads_done():
        if not inside:
            n.gain_out[...] = jnp.concatenate([n.GACC[0, 0:2], n.GACC[1, 0:2], n.GACC[0, 4:8]])
            return
        total = n.GC[...]
        for slot in range(depth - 1):
            done(n.GZ.at[slot], n.gg_recv.at[5 + slot])
            total = total + n.GZ[slot]
        n.gain_out[...] = total
        done(n.GC, n.gg_send.at[0])
        done(n.GC, n.gg_send.at[1])
        for far in range(depth):

            @pl.when(z != far)
            def _():
                done(n.GC, n.gg_send.at[2 + far])

    tasks = {"none": lambda h, j: None}
    for l in range(2):
        tasks[f"nq{l}"] = lambda h, j, l=l: qkv_product(l, j)
        tasks[f"at{l}"] = lambda h, j, l=l: attend(l, j)
        tasks[f"op{l}"] = lambda h, j, l=l: out_product(l, j)
        tasks[f"sa{l}"] = lambda h, j, l=l: attn_sum(l, j)
        tasks[f"ud{l}"] = lambda h, j, l=l: up_product(l, j)
        tasks[f"sm{l}"] = lambda h, j, l=l: mlp_sum(l, j)
        tasks[f"hu{l}"] = lambda h, j, l=l: hidden_back(l, j)
        tasks[f"sd{l}"] = lambda h, j, l=l: mlp_back_sum(l, j)
        tasks[f"ag{l}"] = lambda h, j, l=l: attn_grad(l, j)
        tasks[f"ab{l}"] = lambda h, j, l=l: attend_back(l, j)
        tasks[f"qb{l}"] = lambda h, j, l=l: qkv_back(l, j)
        tasks[f"sb{l}"] = lambda h, j, l=l: attn_back_sum(l, j)
        for p in range(PARTS):
            tasks[f"wg{l}{p}"] = lambda h, j, l=l, p=p: weight_grad(l, p, j)
    for p in range(PARTS):
        tasks[f"ws{p}"] = lambda h, j, p=p: weights_send(1, p)
        tasks[f"wt{p}"] = lambda h, j, p=p: weights_send(0, p)
    tasks["r"] = lambda h, j: sum_pass(h, j)
    tasks["x0"] = lambda h, j: inputs_pass(j)
    tasks["x1"] = lambda h, j: cotangent_pass(j)
    tasks["wr"] = lambda h, j: weights_relay(lax.div(h, PARTS), lax.rem(h, PARTS), j)
    tasks["ww"] = lambda h, j: weights_wait(h, j)
    for l in range(2):
        tasks[f"gp{l}"] = lambda h, j, l=l: grad_pass(l, h, j)
    tasks["gf"] = lambda h, j: grad_final(j, h)
    for step in range(4):
        tasks[f"gg{step}"] = lambda h, j, step=step: gain_grads(step)
    tasks["gw"] = lambda h, j: gains_wait()
    tasks["xp"] = lambda h, j: spread_pass(0, n.X0)
    tasks["cp"] = lambda h, j: spread_pass(1, n.CT)
    tasks["cs"] = lambda h, j: spread(1, n.cot, n.CT)
    used = {"none"} | {name for name, _, _ in steps}
    order = [name for name in tasks if name in used]
    run = [tasks[name] for name in order]

    weights_send(0, 0)
    gains_send()
    spread(0, n.inp, n.X0)
    n.GACC[...] = jnp.zeros_like(n.GACC)
    n.BIAS[...] = jnp.where(n.lengths[y] == rows_all, 0.0, MASKED) + jnp.zeros_like(n.BIAS)

    group = 12
    codes = [order.index(name) * 32 + h * 4 + j for name, h, j in steps]
    codes += [0] * (-len(codes) % group)
    pairs = [codes[i] + 4096 * codes[i + 1] for i in range(0, len(codes), 2)]
    per_group = group // 2
    groups = len(pairs) // per_group

    def dispatch(low, high, op, h, j):
        if high - low == 1:
            run[low](h, j)
            return
        middle = (low + high) // 2
        lax.cond(
            op < middle,
            lambda: dispatch(low, middle, op, h, j),
            lambda: dispatch(middle, high, op, h, j),
        )

    @pl.loop(0, groups)
    def _(g):
        words = [
            pick(g, [pairs[q * per_group + w] for q in range(groups)]) for w in range(per_group)
        ]

        @pl.loop(0, group)
        def _(i):
            word = pick(lax.shift_right_logical(i, 1), words)
            code = jnp.where((i & 1) == 0, word & 4095, lax.shift_right_logical(word, 12))
            dispatch(
                0,
                len(run),
                lax.shift_right_logical(code, 5),
                lax.shift_right_logical(code, 2) & 7,
                code & 3,
            )

    if inside:
        for p in range(PARTS):
            weights_sent(p)
            for l in range(2):

                @pl.when(hub)
                def _():
                    for far in range(depth):
                        done(n.W.at[l, p, slab_of(far)], n.relay_send.at[l, p, far])

                        @pl.when((z == 1) if far >= 2 else (z == 2))
                        def _():
                            done(n.W.at[l, p, slab_of(far)], n.onward_send.at[l, p, far])

    spread_done(0)
    spread_done(1)

    @pl.loop(0, CHUNKS)
    def _(j):
        for stage in range(7):
            done(bytes_of(part), n.pair_send.at[stage, j])
        for which, section in ((1, 0), (2, 0), (3, 1)):
            given_out(which, section, j)

    for which, section in ((0, 1), (1, 0), (2, 0), (3, 1)):
        got_out(which, section)
    grads_done()
    gain_grads_done()


STEPS = (
    ("wr", 0, 0), ("wt1", 0, 0), ("xp", 0, 0), ("wr", 1, 0), ("gw", 0, 0), ("wt2", 0, 0),
    ("wr", 0, 1), ("x0", 0, 0), ("wr", 0, 3), ("wr", 0, 2), ("x0", 0, 1), ("x0", 0, 3),
    ("ww", 0, 0), ("nq0", 0, 1), ("cs", 0, 0), ("nq0", 0, 0), ("x0", 0, 2), ("wr", 1, 3),
    ("at0", 3, 1), ("wr", 2, 0), ("op0", 0, 1), ("ws1", 0, 0), ("ws0", 0, 0), ("wr", 1, 2),
    ("wr", 2, 2), ("wr", 1, 1), ("cp", 0, 0), ("nq0", 0, 2), ("ws2", 0, 0), ("nq0", 0, 3),
    ("wr", 2, 1), ("r", 0, 1), ("at0", 3, 3), ("op0", 0, 3), ("at0", 3, 0), ("at0", 3, 2),
    ("r", 0, 3), ("op0", 0, 0), ("wr", 2, 3), ("sa0", 0, 3), ("wr", 5, 0), ("wr", 3, 2),
    ("r", 0, 0), ("wr", 3, 0), ("ww", 0, 1), ("wr", 3, 1), ("wr", 3, 3), ("op0", 0, 2),
    ("sa0", 0, 1), ("wr", 4, 1), ("r", 0, 2), ("wr", 4, 2), ("x1", 0, 3), ("wr", 4, 0),
    ("x1", 0, 0), ("ww", 0, 2), ("x1", 0, 2), ("ud0", 0, 1), ("r", 1, 1), ("sa0", 0, 0),
    ("ud0", 0, 0), ("r", 1, 0), ("sa0", 0, 2), ("ud0", 0, 2), ("wr", 5, 3), ("sm0", 0, 1),
    ("r", 1, 2), ("ud0", 0, 3), ("ww", 1, 0), ("r", 1, 3), ("sm0", 0, 0), ("wr", 5, 2),
    ("nq1", 0, 0), ("at1", 3, 0), ("wr", 5, 1), ("nq1", 0, 1), ("x1", 0, 1), ("at1", 3, 1),
    ("sm0", 0, 2), ("op1", 0, 0), ("wr", 4, 3), ("nq1", 0, 2), ("sm0", 0, 3), ("r", 2, 0),
    ("at1", 3, 2), ("op1", 0, 2), ("nq1", 0, 3), ("r", 2, 2), ("at1", 3, 3), ("op1", 0, 3),
    ("r", 2, 3), ("sa1", 0, 2), ("op1", 0, 1), ("sa1", 0, 0), ("ww", 1, 2), ("r", 2, 1),
    ("sa1", 0, 3), ("ww", 1, 1), ("ud1", 0, 2), ("ud1", 0, 3), ("ud1", 0, 0), ("sa1", 0, 1),
    ("r", 3, 3), ("hu1", 0, 2), ("ud1", 0, 1), ("hu1", 0, 3), ("r", 3, 2), ("hu1", 0, 0),
    ("sm1", 0, 3), ("r", 4, 3), ("hu1", 0, 1), ("wg12", 0, 0), ("r", 3, 0), ("r", 3, 1),
    ("sm1", 0, 2), ("wg12", 0, 1), ("r", 4, 2), ("sd1", 0, 3), ("ag1", 0, 3), ("ab1", 3, 3),
    ("sm1", 0, 1), ("wg11", 0, 0), ("r", 4, 1), ("wg11", 0, 1), ("qb1", 0, 3), ("sd1", 0, 2),
    ("gp1", 2, 1), ("sm1", 0, 0), ("r", 4, 0), ("ag1", 0, 2), ("ab1", 3, 2), ("sd1", 0, 1),
    ("gp1", 2, 3), ("qb1", 0, 2), ("r", 5, 3), ("ag1", 0, 1), ("ab1", 3, 1), ("gp1", 1, 0),
    ("sd1", 0, 0), ("gp1", 2, 0), ("qb1", 0, 1), ("ag1", 0, 0), ("r", 5, 1), ("ab1", 3, 0),
    ("sb1", 0, 3), ("gp1", 2, 2), ("r", 5, 2), ("qb1", 0, 0), ("gp1", 1, 3), ("wg10", 0, 0),
    ("hu0", 0, 3), ("r", 5, 0), ("gp1", 1, 2), ("sb1", 0, 1), ("wg10", 0, 1), ("r", 6, 3),
    ("sb1", 0, 2), ("hu0", 0, 2), ("gp1", 0, 1), ("hu0", 0, 1), ("sb1", 0, 0), ("gp1", 0, 0),
    ("r", 6, 2), ("hu0", 0, 0), ("wg02", 0, 1), ("sd0", 0, 3), ("gf", 2, 1), ("r", 6, 1),
    ("gp1", 0, 3), ("ag0", 0, 3), ("wg02", 0, 0), ("ab0", 3, 3), ("gp1", 1, 1), ("gp1", 0, 2),
    ("qb0", 0, 3), ("gp0", 2, 2), ("gp0", 2, 3), ("sd0", 0, 2), ("wg01", 0, 1), ("r", 6, 0),
    ("r", 7, 3), ("gp0", 2, 0), ("ag0", 0, 2), ("ab0", 3, 2), ("wg01", 0, 0), ("sd0", 0, 0),
    ("qb0", 0, 2), ("gp0", 2, 1), ("sd0", 0, 1), ("ag0", 0, 1), ("ab0", 3, 1), ("qb0", 0, 1),
    ("ag0", 0, 0), ("ab0", 3, 0), ("qb0", 0, 0), ("r", 7, 2), ("wg00", 0, 1), ("gp0", 1, 2),
    ("gp0", 1, 0), ("r", 7, 1), ("gp0", 1, 1), ("r", 7, 0), ("sb0", 0, 3), ("gf", 0, 1),
    ("gp0", 1, 3), ("wg00", 0, 0), ("sb0", 0, 0), ("gp0", 0, 2), ("sb0", 0, 1), ("sb0", 0, 2),
    ("gg0", 0, 0), ("gg1", 0, 0), ("gf", 1, 1), ("gp0", 0, 0), ("gf", 1, 0), ("gf", 2, 0),
    ("gp0", 0, 1), ("gp0", 0, 3), ("gg2", 0, 0), ("gg3", 0, 0), ("gf", 0, 0),
)


def run_blocks(inputs, cotangent, weights, gain_rows, lengths, depth, inside):
    buckets, chunk, width = inputs.shape
    rows = CHUNKS * chunk
    part = chunk // 2
    heads = width // 4 // HEAD
    vmem, dma = pltpu.VMEM, pltpu.SemaphoreType.DMA
    scratch = dict(
        W=vmem((2, PARTS, width, width), BF16),
        X0=vmem((CHUNKS * part, width), BF16),
        Y0=vmem((CHUNKS * part, width), BF16),
        CT=vmem((rows, width), BF16),
        DR=vmem((rows, width), BF16),
        N1=vmem((2, rows, width), BF16),
        N2=vmem((2, rows, width), BF16),
        Q=vmem((2, heads, rows, 2 * HEAD), BF16),
        KV=vmem((2, heads, rows, 2 * HEAD), BF16),
        KT=vmem((2, heads, HEAD, rows), BF16),
        ATT=vmem((2, rows, (heads + 1) * HEAD), BF16),
        LSE=vmem((2, 8, rows), F32),
        PRE=vmem((2, rows, width), BF16),
        HID=vmem((rows, width), BF16),
        DPRE=vmem((rows, width), BF16),
        DQKV=vmem((rows, 3 * heads * HEAD), BF16),
        DA=vmem((2, rows, width), BF16),
        DKV=vmem((heads, rows, 2 * HEAD), F32),
        GRAD=vmem((heads, chunk, 2 * HEAD), BF16),
        GRADT=vmem((8, chunk), F32),
        DQT=vmem((heads, HEAD, chunk), F32),
        MID=vmem((2, CHUNKS * part, width), F32),
        DMID=vmem((CHUNKS * part, width), F32),
        PART=vmem((2, rows, width), BF16),
        RC=vmem((2, CHUNKS, part, width), BF16),
        RX=vmem((3, CHUNKS, part, width), BF16),
        STG=vmem((4, width // 2, width), BF16),
        GAINS=vmem((8, width), F32),
        BIAS=vmem((8, chunk), F32),
        GACC=vmem((2, 8, width), F32),
        in_send=dma((2, 3)),
        in_recv=dma((2, CHUNKS)),
        mate_send=dma((CHUNKS,)),
        mate_recv=dma((CHUNKS,)),
        pair_send=dma((7, CHUNKS)),
        pair_recv=dma((7, CHUNKS)),
        rs_send=dma((8, 2, CHUNKS)),
        rs_recv=dma((8, 2, CHUNKS)),
        w_recv=dma((2, PARTS, depth if inside else 1)),
        stg_send=dma((2, PARTS, 4)),
        out_send=dma((4, CHUNKS)),
        out_recv=dma((4, 2, 2)),
    )
    outs = dict(
        acts=jax.ShapeDtypeStruct(inputs.shape, BF16), igr=jax.ShapeDtypeStruct(inputs.shape, BF16)
    )
    if inside:
        slab = width // depth
        scratch.update(
            GR=vmem((2, PARTS, width, width), BF16),
            ZR=vmem((depth - 1, PARTS, slab, width), BF16),
            FIN=vmem((2, slab, width), F32),
            GIN=vmem((2, depth) + gain_rows.shape, F32),
            GC=vmem((8, width), F32),
            GX=vmem((8, width), F32),
            GY=vmem((8, width), F32),
            GZ=vmem((depth - 1, 8, width), F32),
            w_send=dma((PARTS, depth)),
            relay_send=dma((2, PARTS, depth)),
            onward_send=dma((2, PARTS, depth)),
            gr_recv=dma((2, PARTS, 4)),
            z_send=dma((PARTS, depth)),
            z_recv=dma((PARTS, depth - 1)),
            fin_send=dma((PARTS,)),
            gin_send=dma((2, depth)),
            gin_recv=dma((2, depth)),
            gg_send=dma((3 + depth,)),
            gg_recv=dma((4 + depth,)),
        )
        own = dict(own_a=weights[0], own_b=weights[1], own_c=weights[2])
        outs["gsum"] = jax.ShapeDtypeStruct((PARTS, slab, width), F32)
    else:
        own = dict(w_whole=weights)
        outs["grads"] = jax.ShapeDtypeStruct(weights.shape, BF16)
    outs["gain_out"] = jax.ShapeDtypeStruct((8, width), F32)
    given = dict(inp=inputs, cot=cotangent, **own, gain_rows=gain_rows, lengths=lengths)
    hbm = pl.BlockSpec(memory_space=pl.ANY)
    in_vmem = pl.BlockSpec(memory_space=pltpu.VMEM)
    small = ("gain_rows", "gain_out")
    in_smem = pl.BlockSpec(memory_space=pltpu.SMEM)
    return pl.pallas_call(
        functools.partial(
            block_kernel, inside, STEPS, list(given) + list(outs) + list(scratch)
        ),
        out_shape=tuple(outs.values()),
        in_specs=[
            in_vmem if name in small else in_smem if name == "lengths" else hbm for name in given
        ],
        out_specs=tuple(in_vmem if name in small else hbm for name in outs),
        scratch_shapes=list(scratch.values()),
        compiler_params=pltpu.CompilerParams(
            collective_id=0, has_side_effects=True, vmem_limit_bytes=VMEM_LIMIT
        ),
        cost_estimate=pl.CostEstimate(
            flops=27_000_000_000, bytes_accessed=40_000_000, transcendentals=20_000_000
        ),
        name="blocks",
    )(*given.values())


def shards(inputs, lengths, gains, w_qkv, w_out, w_up, w_down, cotangent):
    local_rows, width = inputs.shape[1:]
    slab = w_up.shape[1]
    heads = w_qkv.shape[3] // HEAD
    depth = lax.axis_size("dp")
    y = lax.div(lax.axis_index("tensor"), 2)
    section = lax.axis_index("section")
    inside = slab % 16 == 0 and depth == 4
    split = (slab, heads, HEAD)
    kv = jnp.stack([w_qkv[0, :, 1].reshape(split), w_qkv[0, :, 2].reshape(split)], axis=2)
    own = (
        jnp.concatenate([kv.reshape(slab, -1), w_qkv[0, :, 0], w_out[0].T], axis=1),
        w_up[0],
        w_down[0].T,
    )
    axes = ("section", "tensor")
    if inside:
        gain_rows = jnp.pad(gains[0].astype(F32), ((0, 6), (0, -slab % 128)))
        acts, input_grads, total, gain_part = run_blocks(
            inputs, cotangent, own, gain_rows, lengths, depth, inside
        )
        gain_part = gain_part[None, :2]
        at = lax.axis_index("tensor") * depth + lax.axis_index("dp")
        share = width // (depth * lax.axis_size("tensor"))
        gain_grads = lax.dynamic_slice_in_dim(gain_part, at * share, share, 2)
    else:
        whole = lax.all_gather(jnp.stack(own), "dp", axis=1, tiled=True)
        weights = []
        for l in range(2):
            parts = []
            for to_y in range(2):
                pairs = [
                    (4 * l + 2 * c + x, 4 * c + 2 * to_y + x) for c in range(2) for x in range(2)
                ]
                parts.append(lax.ppermute(whole, axes, pairs))
            weights.append(jnp.where(y == 0, parts[0], parts[1]))
        weights = jnp.stack(weights)
        gain_rows = lax.all_gather(gains, "dp", axis=2, tiled=True)
        gain_rows = lax.all_gather(gain_rows, "section", axis=0, tiled=True)
        gain_rows = jnp.pad(gain_rows.reshape(4, width).astype(F32), ((0, 4), (0, 0)))
        acts, input_grads, partial, gain_part = run_blocks(
            inputs, cotangent, weights, gain_rows, lengths, depth, inside
        )
        total = jnp.zeros(partial.shape[1:], F32)
        for l in range(2):
            for from_y in range(2):
                pairs = [
                    (4 * c + 2 * from_y + x, 4 * l + 2 * c + x) for c in range(2) for x in range(2)
                ]
                total = total + lax.ppermute(partial[l], axes, pairs).astype(F32)
        total = lax.psum_scatter(total.astype(BF16), "dp", scatter_dimension=1, tiled=True)
        total = total.astype(F32)
        gain_part = lax.psum(gain_part[:4].reshape(2, 2, width), "section")
        gain_part = lax.dynamic_slice_in_dim(gain_part, section, 1, 0)
        first = (section == 0) & (jnp.arange(2) == 0)
        gain_part = gain_part * jnp.where(first, 1.0, 0.5)[None, :, None]
        gain_grads = lax.psum_scatter(
            gain_part, ("tensor", "dp"), scatter_dimension=2, tiled=True
        )
    columns = heads * HEAD
    kv = total[0, :, : 2 * columns].reshape(slab, heads, 2, HEAD)
    q = total[0, :, 2 * columns : 3 * columns]
    qkv_grads = jnp.stack([q, kv[:, :, 0].reshape(q.shape), kv[:, :, 1].reshape(q.shape)], axis=1)
    return (
        acts[None],
        input_grads[None],
        gain_grads,
        qkv_grads[None],
        total[0, :, 3 * columns :].T[None],
        total[1][None],
        total[2].T[None],
    )


def solution(mesh):
    in_specs = (
        P("dp", "tensor", None),
        P("dp"),
        P("section", None, "dp"),
        P("section", "dp", None, "tensor"),
        P("section", "tensor", "dp"),
        P("section", "dp", "tensor"),
        P("section", "tensor", "dp"),
        P("dp", "tensor", None),
    )
    out_specs = (
        P("section", "dp", "tensor", None),
        P("section", "dp", "tensor", None),
        P("section", None, ("tensor", "dp")),
        P("section", "dp", None, "tensor"),
        P("section", "tensor", "dp"),
        P("section", "dp", "tensor"),
        P("section", "tensor", "dp"),
    )
    return jax.shard_map(shards, mesh=mesh, in_specs=in_specs, out_specs=out_specs, check_vma=False)
```

```python
import functools

import jax
import jax.numpy as jnp
from jax import lax
from jax.experimental import pallas as pl
from jax.experimental.pallas import tpu as pltpu
from jax.sharding import PartitionSpec as P

HEAD = 64
EPSILON = 1e-05
MASKED = -1e30
CHUNKS = 4
PARTS = 3
VMEM_LIMIT = 63 << 20
TILE = 256
BF16 = jnp.bfloat16
F32 = jnp.float32
MESH = pl.DeviceIdType.MESH

SUM_ATTN = (0, 2)
SUM_MLP = (1, 3)
SUM_DMLP = (6, 4)
SUM_DATTN = (7, 5)
PAIR_N2 = (0, 1)
PAIR_N1 = (6, 2)
PAIR_DA = (4, 3)
PAIR_DR = 5


def nn(left, right):
    return lax.dot_general(left, right, (((1,), (0,)), ((), ())), preferred_element_type=F32)


def nt(left, right):
    return lax.dot_general(left, right, (((1,), (1,)), ((), ())), preferred_element_type=F32)


def tn(left, right):
    return lax.dot_general(left, right, (((0,), (0,)), ((), ())), preferred_element_type=F32)


def unit_rows(rows):
    centre = rows - jnp.mean(rows, axis=-1, keepdims=True)
    spread = jnp.mean(centre * centre, axis=-1, keepdims=True)
    scale = lax.rsqrt(spread + EPSILON)
    return centre * scale, scale


def norm_back(unit, scale, gain, grad):
    wide = grad * gain
    inner = jnp.mean(wide * unit, axis=-1, keepdims=True)
    return scale * (wide - jnp.mean(wide, axis=-1, keepdims=True) - unit * inner)


def gelu_parts(x):
    root = 0.7978845608028654
    square = x * x
    bend = jnp.tanh(root * x * (1.0 + 0.044715 * square))
    half = 0.5 + 0.5 * bend
    slope = half + 0.5 * x * (1.0 - bend * bend) * (root * (1.0 + 0.134145 * square))
    return x * half, slope


class Names:
    pass


def block_kernel(inside, steps, names, *refs):
    n = Names()
    for name, ref in zip(names, refs, strict=True):
        setattr(n, name, ref)
    s = lax.axis_index("section")
    t = lax.axis_index("tensor")
    z = lax.axis_index("dp")
    x = lax.rem(t, 2)
    y = lax.div(t, 2)
    t_y = 2 * (1 - y) + x
    mate = (1 - s, t, z)
    peer_x = (s, 2 * y + 1 - x, z)
    peer_y = (s, t_y, z)
    hub = s == y
    rows_all, width = n.CT.shape
    chunk = rows_all // CHUNKS
    part = chunk // 2
    half = CHUNKS // 2
    heads = n.KT.shape[1]
    tiles = width // TILE
    depth = lax.axis_size("dp")
    slab = width // depth
    q_columns = 2 * heads * HEAD
    o_columns = 3 * heads * HEAD

    def remote(src, dst, send_sem, recv_sem, device):
        return pltpu.make_async_remote_copy(
            src_ref=src,
            dst_ref=dst,
            send_sem=send_sem,
            recv_sem=recv_sem,
            device_id=device,
            device_id_type=MESH,
        )

    def done(ref, sem):
        pltpu.make_async_copy(ref, ref, sem).wait()

    def rows_of(j):
        return pl.ds(pl.multiple_of(j * chunk, chunk), chunk)

    def half_of(j, c):
        return pl.ds(pl.multiple_of(j * chunk + c * part, part), part)

    def own_of(j):
        return pl.ds(pl.multiple_of(j * part, part), part)

    def slab_of(i):
        return pl.ds(pl.multiple_of(i * slab, slab), slab)

    def bytes_of(count):
        return n.PART.at[0, 0:count]

    barrier = pltpu.get_barrier_semaphore()
    greeted = 0
    for other_s in range(2):
        for other in range(CHUNKS):
            greeted += 1

            @pl.when((s != other_s) | (t != other))
            def _():
                pl.semaphore_signal(
                    barrier, inc=1, device_id=(other_s, other, z), device_id_type=MESH
                )

        if inside:
            for other in range(depth):
                greeted += 1

                @pl.when(z != other)
                def _():
                    pl.semaphore_signal(
                        barrier, inc=1, device_id=(other_s, t, other), device_id_type=MESH
                    )

    pl.semaphore_wait(barrier, greeted - 1 - (2 if inside else 0))

    def pick(index, values):
        value = values[0]
        for at in range(1, len(values)):
            value = jnp.where(index == at, values[at], value)
        return value

    def not_far(end):
        if end == 0:
            return z < depth // 2
        if end == depth - 1:
            return z >= depth // 2
        return z >= 0

    def weights_send(l, p):
        if not inside:
            pltpu.make_async_copy(n.w_whole.at[l, p], n.W.at[l, p], n.w_recv.at[l, p, 0]).start()
            return
        own = (n.own_a, n.own_b, n.own_c)[p]

        @pl.when(s == l)
        def _():
            for far in range(depth):
                @pl.when(hub & (z == far))
                def _():
                    pltpu.make_async_copy(
                        own, n.W.at[l, p, slab_of(z)], n.w_recv.at[l, p, z]
                    ).start()

                @pl.when(jnp.logical_not(hub & (z == far)) & not_far(far))
                def _():
                    remote(
                        own,
                        n.W.at[l, p, slab_of(z)],
                        n.w_send.at[p, far],
                        n.w_recv.at[l, p, z],
                        (y, t, far),
                    ).start()

    def weights_sent(p):
        own = (n.own_a, n.own_b, n.own_c)[p]
        for far in range(depth):

            @pl.when(jnp.logical_not(hub & (z == far)) & not_far(far))
            def _():
                done(own, n.w_send.at[p, far])

    def weights_relay(l, p, step):
        if not inside:
            return

        @pl.when(hub)
        def _():
            beside = z + 1 - 2 * lax.rem(z, 2)
            low = z < 2
            far = pick(step, [z, beside, jnp.where(low, 2, 1), jnp.where(low, 3, 0)])
            here = n.W.at[l, p, slab_of(far)]
            done(here, n.w_recv.at[l, p, far])
            remote(
                here, here, n.relay_send.at[l, p, far], n.w_recv.at[l, p, far], peer_y
            ).start()
            for place, end in ((1, 0), (2, 3)):

                @pl.when((z == place) & (far >= 2 if place == 1 else far < 2))
                def _():
                    remote(
                        here,
                        here,
                        n.onward_send.at[l, p, far],
                        n.w_recv.at[l, p, far],
                        (s, t, end),
                    ).start()

    def weights_wait(l, p):
        if not inside:
            done(n.W.at[l, p], n.w_recv.at[l, p, 0])
            return

        @pl.when(jnp.logical_not(hub))
        def _():
            for far in range(depth):
                done(n.W.at[l, p, slab_of(far)], n.w_recv.at[l, p, far])

    t_x = 2 * y + 1 - x
    t_far = 2 * (1 - y) + 1 - x

    def landing(which, target, source_t):
        return target.at[own_of(source_t)] if which == 0 else target.at[half_of(source_t, s)]

    def spread(which, source, target):
        here = source.at[y, half_of(0, s)]
        own = landing(which, target, t)
        remote(
            source.at[1 - y, half_of(0, s)],
            own,
            n.in_send.at[which, 0],
            n.in_recv.at[which, t],
            peer_y,
        ).start()
        remote(here, own, n.in_send.at[which, 1], n.in_recv.at[which, t], peer_x).start()
        pltpu.make_async_copy(here, own, n.in_recv.at[which, t]).start()

    def spread_pass(which, target):
        near = landing(which, target, t_y)
        done(near, n.in_recv.at[which, t_y])
        remote(near, near, n.in_send.at[which, 2], n.in_recv.at[which, t_y], peer_x).start()

    def spread_wait(which, j):
        @pl.when(j != t_y)
        def _():
            done(bytes_of(part), n.in_recv.at[which, j])

    def inputs_pass(j):
        spread_wait(0, j)
        norm_first(0, n.X0[own_of(j), :].astype(F32), j)

    def cotangent_pass(j):
        here = n.CT.at[half_of(j, s)]
        spread_wait(1, j)
        remote(here, here, n.mate_send.at[j], n.mate_recv.at[j], mate).start()

    def cotangent_wait(j):
        done(bytes_of(part), n.mate_recv.at[j])

    def spread_done(which):
        for way in range(3):
            done(bytes_of(part), n.in_send.at[which, way])
        if which == 1:
            for j in range(CHUNKS):
                done(bytes_of(part), n.mate_send.at[j])

    def pair_start(stage, ref, j):
        here = ref.at[half_of(j, s)]
        remote(here, here, n.pair_send.at[stage, j], n.pair_recv.at[stage, j], mate).start()

    def pair_wait(stage, j):
        done(bytes_of(part), n.pair_recv.at[stage, j])

    def sum_start(stage, j):
        b = stage % 2
        remote(
            n.PART.at[b, half_of(j, 1 - s)],
            n.RC.at[b, j],
            n.rs_send.at[stage, 0, j],
            n.rs_recv.at[stage, 0, j],
            mate,
        ).start()

    def sum_pass(stage, j):
        b = lax.rem(stage, 2)
        here = half_of(j, s)
        done(n.RC.at[b, j], n.rs_recv.at[stage, 0, j])
        n.PART[b, here, :] = (
            n.PART[b, here, :].astype(F32) + n.RC[b, j].astype(F32)
        ).astype(BF16)
        arriving = jnp.where(stage == SUM_DMLP[1], 2, b)
        one_way = (stage == SUM_MLP[1]) | (stage == SUM_DATTN[0])

        @pl.when(jnp.logical_not(one_way) | (lax.rem(j, 2) != x))
        def _():
            remote(
                n.PART.at[b, here],
                n.RX.at[arriving, j],
                n.rs_send.at[stage, 1, j],
                n.rs_recv.at[stage, 1, j],
                peer_x,
            ).start()

        done(n.RC.at[b, j], n.rs_send.at[stage, 0, j])

    def sum_sent(stage, j):
        done(n.RX.at[stage % 2, j], n.rs_send.at[stage, 1, j])

    def sum_wait(stage, j):
        b = stage % 2
        arriving = 2 if stage == SUM_DMLP[1] else b
        done(n.RX.at[arriving, j], n.rs_recv.at[stage, 1, j])
        total = n.PART[b, half_of(j, s), :].astype(F32) + n.RX[arriving, j].astype(F32)
        if stage not in (SUM_MLP[1], SUM_DATTN[0]):
            sum_sent(stage, j)
        return total

    first_index = lax.broadcasted_iota(jnp.int32, (chunk, chunk), 0)
    second_index = lax.broadcasted_iota(jnp.int32, (chunk, chunk), 1)

    def scores(l, st, i, j, diagonal, keys_first):
        if l == 0:
            grown = st * st + 1.0
            inverse = lax.rsqrt(grown)
            magnitude = grown * inverse
            sign = st * inverse
        else:
            inverse, magnitude, sign = None, st, None
        if diagonal:
            seen = first_index <= second_index if keys_first else second_index <= first_index
            magnitude = jnp.where(seen, magnitude, MASKED)
        else:
            apart = (j >= half) & (i < half)
            magnitude = magnitude + jnp.where(apart, n.BIAS[0:1, :], 0.0)
        return inverse, magnitude, sign

    def norm_first(l, own_rows, j):
        unit, _ = unit_rows(own_rows)
        n.N1[l, half_of(j, s), :] = (unit * n.GAINS[2 * l : 2 * l + 1, :]).astype(BF16)
        pair_start(PAIR_N1[l], n.N1.at[l], j)

    def qkv_product(l, j):
        rows = rows_of(j)
        pair_wait(PAIR_N1[l], j)
        kv = nn(n.N1[l, rows, :], n.W[l, 0, :, 0:q_columns])
        kv_low = kv.astype(BF16)
        turned = kv.T.astype(BF16)
        for h in range(heads):
            n.KV[l, h, rows, :] = kv_low[:, 2 * h * HEAD : 2 * (h + 1) * HEAD]
            n.KT[l, h, :, rows] = turned[2 * h * HEAD : (2 * h + 1) * HEAD]
        q = nn(n.N1[l, rows, :], n.W[l, 0, :, q_columns:o_columns]).astype(BF16)
        blank = jnp.zeros((chunk, HEAD), BF16)
        for h in range(heads):
            q_h = q[:, h * HEAD : (h + 1) * HEAD] * jnp.asarray(HEAD**-0.5, BF16)
            n.Q[l, h, rows, :] = jnp.concatenate([q_h, blank], axis=1)

    def attend(l, j):
        rows = rows_of(j)

        def block(i, carry, diagonal):
            keys = rows_of(i)
            new = []
            for h in range(heads):
                top, total, out = carry[h]
                kv = n.KV[l, h, keys, :]
                st = nt(n.Q[l, h, rows, :], kv)
                _, magnitude, sign = scores(l, st, i, j, diagonal, False)
                new_top = jnp.maximum(top, jnp.max(magnitude, axis=1, keepdims=True))
                weights = jnp.exp(magnitude - new_top)
                shrink = jnp.exp(top - new_top)
                total = total * shrink + jnp.sum(weights, axis=1, keepdims=True)
                signed = weights if l == 1 else sign * weights
                out = out * shrink + nn(signed.astype(BF16), kv)
                new.append((new_top, total, out))
            return tuple(new)

        carry = (
            jnp.full((chunk, 1), MASKED, F32),
            jnp.zeros((chunk, 1), F32),
            jnp.zeros((chunk, 2 * HEAD), F32),
        )
        carry = block(j, (carry,) * heads, True)
        carry = lax.fori_loop(0, j, lambda i, c: block(i, c, False), carry)
        lane = lax.broadcasted_iota(jnp.int32, (chunk, 128), 1)
        logs = jnp.zeros((chunk, 128), F32)
        outs = [jnp.zeros((chunk, HEAD), BF16)]
        for h in range(heads):
            top, total, out = carry[h]
            outs.append((out / total)[:, HEAD:].astype(BF16))
            logs = jnp.where(lane == h, top + jnp.log(total), logs)
        n.ATT[l, rows, :] = jnp.concatenate(outs, axis=1)
        n.LSE[l, :, rows] = logs.T[0:8]

    def out_product(l, j):
        rows = rows_of(j)
        for i in range(tiles):
            here = slice(i * TILE, (i + 1) * TILE)
            n.PART[0, rows, here] = nt(
                n.ATT[l, rows, :], n.W[l, 0, here, o_columns - HEAD : width]
            ).astype(BF16)
        sum_start(SUM_ATTN[l], j)

    def attn_sum(l, j):
        source = n.X0 if l == 0 else n.Y0
        own = half_of(j, s)
        middle = source[own_of(j), :].astype(F32) + sum_wait(SUM_ATTN[l], j)
        n.MID[l, own_of(j), :] = middle
        unit, _ = unit_rows(middle)
        n.N2[l, own, :] = (unit * n.GAINS[2 * l + 1 : 2 * l + 2, :]).astype(BF16)
        pair_start(PAIR_N2[l], n.N2.at[l], j)

    def up_product(l, j):
        rows = rows_of(j)
        pair_wait(PAIR_N2[l], j)
        for i in range(tiles):
            here = slice(i * TILE, (i + 1) * TILE)
            pre = nn(n.N2[l, rows, :], n.W[l, 1, :, here])
            n.PRE[l, rows, here] = pre.astype(BF16)
            n.HID[rows, here] = gelu_parts(pre)[0].astype(BF16)
        for i in range(tiles):
            here = slice(i * TILE, (i + 1) * TILE)
            n.PART[1, rows, here] = nt(n.HID[rows, :], n.W[l, 2, here, :]).astype(BF16)
        sum_start(SUM_MLP[l], j)

    def mlp_sum(l, j):
        if l == 0:
            result = (n.MID[l, own_of(j), :] + sum_wait(SUM_MLP[l], j)).astype(BF16)
            n.Y0[own_of(j), :] = result
            norm_first(1, result.astype(F32), j)
            give_out(2, 0, n.Y0.at[own_of(j)], n.acts, j)
        else:

            @pl.when(lax.rem(j, 2) == x)
            def _():
                result = n.MID[l, own_of(j), :] + sum_wait(SUM_MLP[l], j)
                n.PART[1, half_of(j, s), :] = result.astype(BF16)
                give_out(0, 1, n.PART.at[1, half_of(j, s)], n.acts, j)

            @pl.when(lax.rem(j, 2) != x)
            def _():
                sum_sent(SUM_MLP[l], j)

    def give_out(which, section, here, out, j):
        target = out.at[y, half_of(0, s)]

        @pl.when((s == section) & (t == j))
        def _():
            copy = pltpu.make_async_copy(here, target, n.out_send.at[which, j])
            copy.start()
            copy.wait()

        @pl.when((lax.rem(j, 2) == x) & ((s != section) | (t != j)))
        def _():
            remote(
                here,
                target,
                n.out_send.at[which, j],
                n.out_recv.at[which, y, s],
                (section, j, z),
            ).start()

    def given_out(which, section, j):
        @pl.when((lax.rem(j, 2) == x) & ((s != section) | (t != j)))
        def _():
            done(bytes_of(part), n.out_send.at[which, j])

    def got_out(which, section):
        @pl.when(s == section)
        def _():
            for m in range(2):
                for c in range(2):

                    @pl.when((y != m) | (s != c))
                    def _():
                        done(bytes_of(part), n.out_recv.at[which, m, c])

    def hidden_back(l, j):
        rows = rows_of(j)
        if l == 1:
            cotangent_wait(j)
        else:
            pair_wait(PAIR_DR, j)
        source = n.CT if l == 1 else n.DR
        for i in range(tiles):
            here = slice(i * TILE, (i + 1) * TILE)
            back = nn(source[rows, :], n.W[l, 2, :, here])
            hidden, slope = gelu_parts(n.PRE[l, rows, here].astype(F32))
            n.HID[rows, here] = hidden.astype(BF16)
            n.DPRE[rows, here] = (slope * back).astype(BF16)
        for i in range(tiles):
            here = slice(i * TILE, (i + 1) * TILE)
            n.PART[0, rows, here] = nt(n.DPRE[rows, :], n.W[l, 1, here, :]).astype(BF16)
        sum_start(SUM_DMLP[l], j)

    def mlp_back_sum(l, j):
        total = sum_wait(SUM_DMLP[l], j)
        source = n.CT if l == 1 else n.DR
        own = half_of(j, s)
        unit, scale = unit_rows(n.MID[l, own_of(j), :])
        n.GACC[l, 1:2, :] += jnp.sum(total * unit, axis=0, keepdims=True)
        gain = n.GAINS[2 * l + 1 : 2 * l + 2, :]
        grad = source[own, :].astype(F32) + norm_back(unit, scale, gain, total)
        n.DMID[own_of(j), :] = grad
        n.DA[l, own, :] = grad.astype(BF16)
        pair_start(PAIR_DA[l], n.DA.at[l], j)

    def attn_grad(l, j):
        rows = rows_of(j)
        pair_wait(PAIR_DA[l], j)

        @pl.when(j == CHUNKS - 1)
        def _():
            n.DKV[...] = jnp.zeros_like(n.DKV)

        low = nn(n.DA[l, rows, :], n.W[l, 0, :, o_columns - HEAD : width]).astype(BF16)
        product = low.astype(F32) * n.ATT[l, rows, :].astype(F32)
        blank = jnp.zeros((chunk, HEAD), BF16)
        lane = lax.broadcasted_iota(jnp.int32, (chunk, 128), 1)
        inner = jnp.zeros((chunk, 128), F32)
        for h in range(heads):
            here = slice((h + 1) * HEAD, (h + 2) * HEAD)
            n.GRAD[h] = jnp.concatenate([blank, low[:, here]], axis=1)
            inner = jnp.where(
                lane == h, jnp.sum(product[:, here], axis=1, keepdims=True), inner
            )
        n.GRADT[...] = inner.T[0:8]

    def attend_back(l, j):
        rows = rows_of(j)

        def block(i, carry, diagonal):
            keys = rows_of(i)
            new = []
            for h in range(heads):
                kv = n.KV[l, h, keys, :]
                st = nt(kv, n.Q[l, h, rows, :])
                dp = nt(kv, n.GRAD[h])
                inverse, magnitude, sign = scores(l, st, i, j, diagonal, True)
                weights = jnp.exp(magnitude - n.LSE[l, h : h + 1, rows])
                inner = n.GRADT[h : h + 1, :]
                if l == 0:
                    signed = sign * weights
                    ds = weights * (
                        sign * (sign * dp - inner) + dp * (inverse * inverse * inverse)
                    )
                else:
                    signed = weights
                    ds = weights * (dp - inner)
                ds = ds.astype(BF16)
                n.DKV[h, keys, :] += nn(ds, n.Q[l, h, rows, :]) + nn(
                    signed.astype(BF16), n.GRAD[h]
                )
                new.append(carry[h] + nn(n.KT[l, h, :, keys], ds))
            return tuple(new)

        blank = jnp.zeros((HEAD, chunk), F32)
        query_grad = block(j, (blank,) * heads, True)
        query_grad = lax.fori_loop(0, j, lambda i, c: block(i, c, False), query_grad)
        for h in range(heads):
            n.DQT[h] = query_grad[h] * HEAD**-0.5

    def qkv_back(l, j):
        rows = rows_of(j)
        turned = jnp.concatenate([n.DQT[h] for h in range(heads)], axis=0).T
        for h in range(heads):
            n.DQKV[rows, 2 * h * HEAD : 2 * (h + 1) * HEAD] = n.DKV[h, rows, :].astype(BF16)
        n.DQKV[rows, q_columns:] = turned.astype(BF16)
        if l == 1:
            given_out(0, 1, j)
        for i in range(tiles):
            here = slice(i * TILE, (i + 1) * TILE)
            n.PART[1, rows, here] = nt(n.DQKV[rows, :], n.W[l, 0, here, 0:o_columns]).astype(
                BF16
            )
        sum_start(SUM_DATTN[l], j)

    def attn_back_result(l, j):
        total = sum_wait(SUM_DATTN[l], j)
        source = n.X0 if l == 0 else n.Y0
        unit, scale = unit_rows(source[own_of(j), :].astype(F32))
        n.GACC[l, 0:1, :] += jnp.sum(total * unit, axis=0, keepdims=True)
        gain = n.GAINS[2 * l : 2 * l + 1, :]
        return n.DMID[own_of(j), :] + norm_back(unit, scale, gain, total)

    def attn_back_sum(l, j):
        own = half_of(j, s)
        if l == 1:
            n.DR[own, :] = attn_back_result(l, j).astype(BF16)
            pair_start(PAIR_DR, n.DR, j)
            give_out(3, 1, n.DR.at[own], n.igr, j)
        else:

            @pl.when(lax.rem(j, 2) == x)
            def _():
                n.PART[1, own, :] = attn_back_result(l, j).astype(BF16)
                give_out(1, 0, n.PART.at[1, own], n.igr, j)

            @pl.when(lax.rem(j, 2) != x)
            def _():
                sum_sent(SUM_DATTN[l], j)

    long = width // 2
    grad_order = ((1, 2), (1, 1), (1, 0), (0, 2), (0, 1), (0, 0))
    grad_to = 2 * s + x

    def kept_here(l):
        return hub & (s == l)

    def grad_sent(l, p, i):
        if not inside:
            done(n.STG.at[0], n.stg_send.at[l, p, i])
            return

        @pl.when(jnp.logical_not(kept_here(l)))
        def _():
            for k in range(2):
                done(n.STG.at[0, 0:slab], n.stg_send.at[l, p, 2 * i + k])

    def weight_grad(l, p, i):
        at = grad_order.index((l, p))
        slot = 2 * (at % 2) + i
        if at > 1:
            grad_sent(*grad_order[at - 2], i)
        rows = pl.ds(pl.multiple_of(i * long, long), long)
        if p == 0:
            left = n.N1[l, :, rows]
            n.STG[slot, :, 0:256] = tn(left, n.DQKV[:, 0:256]).astype(BF16)
            n.STG[slot, :, 256:512] = tn(left, n.DQKV[:, 256:512]).astype(BF16)
            last = tn(left, n.DQKV[:, 512:o_columns])
            out_part = tn(n.DA[l, :, rows], n.ATT[l])
            n.STG[slot, :, 512:width] = jnp.concatenate([last, out_part[:, HEAD:]], axis=1).astype(
                BF16
            )
        else:
            if p == 1:
                left, right = n.N2[l, :, rows], n.DPRE
            else:
                left, right = (n.CT if l == 1 else n.DR)[:, rows], n.HID
            for k in range(tiles):
                here = slice(k * TILE, (k + 1) * TILE)
                n.STG[slot, :, here] = tn(left, right[:, here]).astype(BF16)
        if not inside:
            pltpu.make_async_copy(
                n.STG.at[slot], n.grads.at[l, p, rows], n.stg_send.at[l, p, i]
            ).start()
            return

        @pl.when(kept_here(l))
        def _():
            n.GR[0, p, rows, :] = n.STG[slot]

        @pl.when(jnp.logical_not(kept_here(l)))
        def _():
            way = jnp.where(hub, 0, 1)
            for k in range(2):
                k_at = jnp.where(i == 0, k, 1 - k)
                at_slab = 2 * i + k_at
                remote(
                    n.STG.at[slot, slab_of(k_at)],
                    n.GR.at[way, p, slab_of(at_slab)],
                    n.stg_send.at[l, p, at_slab],
                    n.gr_recv.at[way, p, at_slab],
                    (l, grad_to, z),
                ).start()

    def slot_of(source, target):
        return jnp.where(source > target, source - 1, source)

    def grad_pass(l, p, far):
        if not inside:
            return

        @pl.when(s == l)
        def _():
            here = slab_of(far)

            @pl.when(jnp.logical_not(hub))
            def _():
                done(n.GR.at[0, p, here], n.gr_recv.at[0, p, far])

            done(n.GR.at[1, p, here], n.gr_recv.at[1, p, far])

            @pl.when(z != far)
            def _():
                n.GR[0, p, here, :] = (
                    n.GR[0, p, here, :].astype(F32) + n.GR[1, p, here, :].astype(F32)
                ).astype(BF16)
                slot = slot_of(z, far)
                remote(
                    n.GR.at[0, p, here],
                    n.ZR.at[slot, p],
                    n.z_send.at[p, far],
                    n.z_recv.at[p, slot],
                    (s, t, far),
                ).start()

    def grad_final(l, p):
        if not inside:
            return

        @pl.when(s == l)
        def _():
            here = slab_of(z)
            total = n.GR[0, p, here, :].astype(F32) + n.GR[1, p, here, :].astype(F32)
            for slot in range(depth - 1):
                done(n.ZR.at[slot, p], n.z_recv.at[p, slot])
                total = total + n.ZR[slot, p].astype(F32)
            slot = lax.rem(p, 2)

            @pl.when(p == 0)
            def _():
                done(n.FIN.at[0], n.fin_send.at[2])

            n.FIN[slot] = total
            pltpu.make_async_copy(n.FIN.at[slot], n.gsum.at[p], n.fin_send.at[p]).start()

    def grads_done():
        if not inside:
            for late in grad_order[-2:]:
                grad_sent(*late, 0)
                grad_sent(*late, 1)
            return
        for late in grad_order[-2:]:
            grad_sent(*late, 0)
            grad_sent(*late, 1)
        for p in range(PARTS):
            for far in range(depth):

                @pl.when(z != far)
                def _():
                    done(n.ZR.at[0, p], n.z_send.at[p, far])

        done(n.FIN.at[0], n.fin_send.at[0])
        done(n.FIN.at[1], n.fin_send.at[1])

    def gains_send():
        if not inside:
            n.GAINS[...] = n.gain_rows[...]
            return
        n.GIN[s, z] = n.gain_rows[...]
        for c in range(2):
            for far in range(depth):

                @pl.when((s != c) | (z != far))
                def _():
                    remote(
                        n.gain_rows,
                        n.GIN.at[s, z],
                        n.gin_send.at[c, far],
                        n.gin_recv.at[s, z],
                        (c, t, far),
                    ).start()

    def gains_wait():
        if not inside:
            return
        for c in range(2):
            for far in range(depth):

                @pl.when((s != c) | (z != far))
                def _():
                    done(n.gain_rows, n.gin_recv.at[c, far])
                    done(n.gain_rows, n.gin_send.at[c, far])

                for k in range(2):
                    n.GAINS[2 * c + k : 2 * c + k + 1, far * slab : (far + 1) * slab] = n.GIN[
                        c, far, k : k + 1, 0:slab
                    ]

    def gain_grads(step):
        if not inside:
            return
        if step == 0:
            remote(n.GACC.at[1 - s], n.GC, n.gg_send.at[0], n.gg_recv.at[0], mate).start()
        elif step == 1:
            done(n.GC, n.gg_recv.at[0])
            n.GACC[s] += n.GC[...]
            remote(n.GACC.at[s], n.GX, n.gg_send.at[6], n.gg_recv.at[4], peer_x).start()
        elif step == 2:
            done(n.GX, n.gg_recv.at[4])
            done(n.GX, n.gg_send.at[6])
            row = lax.broadcasted_iota(jnp.int32, n.GX.shape, 0)
            n.GACC[s] += jnp.where((row == 0) & (s == 0), n.GX[...], 0.0)
            remote(n.GACC.at[s], n.GY, n.gg_send.at[1], n.gg_recv.at[1], peer_y).start()
        else:
            done(n.GY, n.gg_recv.at[1])
            n.GC[...] = n.GACC[s] + n.GY[...]
            for far in range(depth):

                @pl.when(z != far)
                def _():
                    slot = slot_of(z, far)
                    remote(
                        n.GC,
                        n.GZ.at[slot],
                        n.gg_send.at[2 + far],
                        n.gg_recv.at[5 + slot],
                        (s, t, far),
                    ).start()

    def gain_grads_done():
        if not inside:
            n.gain_out[...] = jnp.concatenate([n.GACC[0, 0:2], n.GACC[1, 0:2], n.GACC[0, 4:8]])
            return
        total = n.GC[...]
        for slot in range(depth - 1):
            done(n.GZ.at[slot], n.gg_recv.at[5 + slot])
            total = total + n.GZ[slot]
        n.gain_out[...] = total
        done(n.GC, n.gg_send.at[0])
        done(n.GC, n.gg_send.at[1])
        for far in range(depth):

            @pl.when(z != far)
            def _():
                done(n.GC, n.gg_send.at[2 + far])

    tasks = {"none": lambda h, j: None}
    for l in range(2):
        tasks[f"nq{l}"] = lambda h, j, l=l: qkv_product(l, j)
        tasks[f"at{l}"] = lambda h, j, l=l: attend(l, j)
        tasks[f"op{l}"] = lambda h, j, l=l: out_product(l, j)
        tasks[f"sa{l}"] = lambda h, j, l=l: attn_sum(l, j)
        tasks[f"ud{l}"] = lambda h, j, l=l: up_product(l, j)
        tasks[f"sm{l}"] = lambda h, j, l=l: mlp_sum(l, j)
        tasks[f"hu{l}"] = lambda h, j, l=l: hidden_back(l, j)
        tasks[f"sd{l}"] = lambda h, j, l=l: mlp_back_sum(l, j)
        tasks[f"ag{l}"] = lambda h, j, l=l: attn_grad(l, j)
        tasks[f"ab{l}"] = lambda h, j, l=l: attend_back(l, j)
        tasks[f"qb{l}"] = lambda h, j, l=l: qkv_back(l, j)
        tasks[f"sb{l}"] = lambda h, j, l=l: attn_back_sum(l, j)
        for p in range(PARTS):
            tasks[f"wg{l}{p}"] = lambda h, j, l=l, p=p: weight_grad(l, p, j)
    for p in range(PARTS):
        tasks[f"ws{p}"] = lambda h, j, p=p: weights_send(1, p)
        tasks[f"wt{p}"] = lambda h, j, p=p: weights_send(0, p)
    tasks["r"] = lambda h, j: sum_pass(h, j)
    tasks["x0"] = lambda h, j: inputs_pass(j)
    tasks["x1"] = lambda h, j: cotangent_pass(j)
    tasks["wr"] = lambda h, j: weights_relay(lax.div(h, PARTS), lax.rem(h, PARTS), j)
    tasks["ww"] = lambda h, j: weights_wait(h, j)
    for l in range(2):
        tasks[f"gp{l}"] = lambda h, j, l=l: grad_pass(l, h, j)
    tasks["gf"] = lambda h, j: grad_final(j, h)
    for step in range(4):
        tasks[f"gg{step}"] = lambda h, j, step=step: gain_grads(step)
    tasks["gw"] = lambda h, j: gains_wait()
    tasks["xp"] = lambda h, j: spread_pass(0, n.X0)
    tasks["cp"] = lambda h, j: spread_pass(1, n.CT)
    tasks["cs"] = lambda h, j: spread(1, n.cot, n.CT)
    used = {"none"} | {name for name, _, _ in steps}
    order = [name for name in tasks if name in used]
    run = [tasks[name] for name in order]

    weights_send(0, 0)
    gains_send()
    spread(0, n.inp, n.X0)
    n.GACC[...] = jnp.zeros_like(n.GACC)
    n.BIAS[...] = jnp.where(n.lengths[y] == rows_all, 0.0, MASKED) + jnp.zeros_like(n.BIAS)

    group = 12
    codes = [order.index(name) * 32 + h * 4 + j for name, h, j in steps]
    codes += [0] * (-len(codes) % group)
    pairs = [codes[i] + 4096 * codes[i + 1] for i in range(0, len(codes), 2)]
    per_group = group // 2
    groups = len(pairs) // per_group

    def dispatch(low, high, op, h, j):
        if high - low == 1:
            run[low](h, j)
            return
        middle = (low + high) // 2
        lax.cond(
            op < middle,
            lambda: dispatch(low, middle, op, h, j),
            lambda: dispatch(middle, high, op, h, j),
        )

    @pl.loop(0, groups)
    def _(g):
        words = [
            pick(g, [pairs[q * per_group + w] for q in range(groups)]) for w in range(per_group)
        ]

        @pl.loop(0, group)
        def _(i):
            word = pick(lax.shift_right_logical(i, 1), words)
            code = jnp.where((i & 1) == 0, word & 4095, lax.shift_right_logical(word, 12))
            dispatch(
                0,
                len(run),
                lax.shift_right_logical(code, 5),
                lax.shift_right_logical(code, 2) & 7,
                code & 3,
            )

    if inside:
        for p in range(PARTS):
            weights_sent(p)
            for l in range(2):

                @pl.when(hub)
                def _():
                    for far in range(depth):
                        done(n.W.at[l, p, slab_of(far)], n.relay_send.at[l, p, far])

                        @pl.when((z == 1) if far >= 2 else (z == 2))
                        def _():
                            done(n.W.at[l, p, slab_of(far)], n.onward_send.at[l, p, far])

    spread_done(0)
    spread_done(1)

    @pl.loop(0, CHUNKS)
    def _(j):
        for stage in range(7):
            done(bytes_of(part), n.pair_send.at[stage, j])
        for which, section in ((1, 0), (2, 0), (3, 1)):
            given_out(which, section, j)

    for which, section in ((0, 1), (1, 0), (2, 0), (3, 1)):
        got_out(which, section)
    grads_done()
    gain_grads_done()


STEPS = (
    ("cs", 0, 0), ("wt2", 0, 0), ("wt1", 0, 0), ("wr", 0, 0), ("xp", 0, 0), ("wr", 0, 1),
    ("wr", 0, 2), ("gw", 0, 0), ("wr", 0, 3), ("x0", 0, 0), ("x0", 0, 1), ("wr", 2, 2),
    ("x0", 0, 2), ("wr", 2, 0), ("cp", 0, 0), ("wr", 2, 1), ("ww", 0, 0), ("nq0", 0, 1),
    ("nq0", 0, 0), ("at0", 3, 1), ("nq0", 0, 2), ("op0", 0, 1), ("wr", 1, 2), ("x0", 0, 3),
    ("x1", 0, 3), ("at0", 3, 2), ("wr", 1, 0), ("wr", 1, 1), ("wr", 1, 3), ("op0", 0, 2),
    ("ws0", 0, 0), ("at0", 3, 0), ("op0", 0, 0), ("nq0", 0, 3), ("wr", 2, 3), ("r", 0, 1),
    ("r", 0, 2), ("r", 0, 0), ("at0", 3, 3), ("ws2", 0, 0), ("op0", 0, 3), ("wr", 3, 2),
    ("wr", 3, 0), ("ws1", 0, 0), ("sa0", 0, 1), ("sa0", 0, 0), ("x1", 0, 0), ("ww", 0, 1),
    ("wr", 3, 1), ("r", 0, 3), ("ww", 0, 2), ("ud0", 0, 0), ("wr", 3, 3), ("ud0", 0, 1),
    ("r", 1, 0), ("sa0", 0, 3), ("wr", 4, 2), ("ud0", 0, 3), ("r", 1, 1), ("wr", 5, 3),
    ("sa0", 0, 2), ("x1", 0, 1), ("ud0", 0, 2), ("r", 1, 2), ("sm0", 0, 1), ("sm0", 0, 0),
    ("ww", 1, 0), ("wr", 4, 0), ("nq1", 0, 0), ("wr", 4, 1), ("r", 1, 3), ("nq1", 0, 1),
    ("at1", 3, 1), ("at1", 3, 0), ("op1", 0, 1), ("sm0", 0, 2), ("op1", 0, 0), ("wr", 5, 2),
    ("nq1", 0, 2), ("r", 2, 1), ("sm0", 0, 3), ("at1", 3, 2), ("op1", 0, 2), ("x1", 0, 2),
    ("r", 2, 0), ("wr", 4, 3), ("nq1", 0, 3), ("at1", 3, 3), ("wr", 5, 1), ("op1", 0, 3),
    ("r", 2, 2), ("r", 2, 3), ("wr", 5, 0), ("sa1", 0, 0), ("ww", 1, 1), ("sa1", 0, 1),
    ("sa1", 0, 2), ("ww", 1, 2), ("ud1", 0, 1), ("ud1", 0, 2), ("sa1", 0, 3), ("hu1", 0, 1),
    ("r", 3, 1), ("ud1", 0, 3), ("hu1", 0, 2), ("r", 3, 2), ("r", 3, 3), ("ud1", 0, 0),
    ("hu1", 0, 3), ("hu1", 0, 0), ("wg12", 0, 1), ("sm1", 0, 3), ("r", 4, 3), ("r", 3, 0),
    ("wg12", 0, 0), ("sm1", 0, 1), ("wg11", 0, 1), ("r", 4, 1), ("sd1", 0, 3), ("gp1", 2, 2),
    ("sm1", 0, 2), ("sm1", 0, 0), ("r", 4, 2), ("ag1", 0, 3), ("gp1", 2, 3), ("ab1", 3, 3),
    ("gp1", 2, 0), ("qb1", 0, 3), ("sd1", 0, 2), ("r", 4, 0), ("wg11", 0, 0), ("gp1", 2, 1),
    ("sd1", 0, 1), ("r", 5, 3), ("ag1", 0, 2), ("ab1", 3, 2), ("gp1", 1, 3), ("qb1", 0, 2),
    ("ag1", 0, 1), ("sd1", 0, 0), ("ab1", 3, 1), ("r", 5, 2), ("qb1", 0, 1), ("sb1", 0, 3),
    ("ag1", 0, 0), ("ab1", 3, 0), ("gp1", 1, 2), ("qb1", 0, 0), ("r", 5, 1), ("wg10", 0, 1),
    ("gp1", 1, 0), ("hu0", 0, 3), ("wg10", 0, 0), ("gp1", 1, 1), ("sb1", 0, 2), ("r", 5, 0),
    ("r", 6, 3), ("sb1", 0, 1), ("hu0", 0, 2), ("gp1", 0, 3), ("sb1", 0, 0), ("hu0", 0, 1),
    ("gp1", 0, 2), ("hu0", 0, 0), ("wg02", 0, 0), ("gp1", 0, 0), ("sd0", 0, 3), ("wg02", 0, 1),
    ("r", 6, 2), ("wg01", 0, 0), ("gp1", 0, 1), ("ag0", 0, 3), ("ab0", 3, 3), ("r", 6, 1),
    ("sd0", 0, 2), ("qb0", 0, 3), ("gp0", 2, 0), ("r", 6, 0), ("ag0", 0, 2), ("ab0", 3, 2),
    ("wg01", 0, 1), ("qb0", 0, 2), ("gp0", 2, 3), ("sd0", 0, 1), ("gp0", 2, 1), ("gp0", 2, 2),
    ("gf", 2, 1), ("r", 7, 3), ("r", 7, 2), ("ag0", 0, 1), ("sd0", 0, 0), ("ab0", 3, 1),
    ("qb0", 0, 1), ("gp0", 1, 1), ("gp0", 1, 0), ("ag0", 0, 0), ("ab0", 3, 0), ("sb0", 0, 2),
    ("gf", 1, 1), ("qb0", 0, 0), ("gp0", 1, 3), ("wg00", 0, 0), ("gf", 0, 1), ("gp0", 1, 2),
    ("r", 7, 0), ("wg00", 0, 1), ("r", 7, 1), ("sb0", 0, 1), ("sb0", 0, 0), ("gf", 1, 0),
    ("sb0", 0, 3), ("gp0", 0, 1), ("gp0", 0, 0), ("gg0", 0, 0), ("gf", 2, 0), ("gp0", 0, 3),
    ("gp0", 0, 2), ("gg1", 0, 0), ("gg2", 0, 0), ("gg3", 0, 0), ("gf", 0, 0),
)


def run_blocks(inputs, cotangent, weights, gain_rows, lengths, depth, inside):
    buckets, chunk, width = inputs.shape
    rows = CHUNKS * chunk
    part = chunk // 2
    heads = width // 4 // HEAD
    vmem, dma = pltpu.VMEM, pltpu.SemaphoreType.DMA
    scratch = dict(
        W=vmem((2, PARTS, width, width), BF16),
        X0=vmem((CHUNKS * part, width), BF16),
        Y0=vmem((CHUNKS * part, width), BF16),
        CT=vmem((rows, width), BF16),
        DR=vmem((rows, width), BF16),
        N1=vmem((2, rows, width), BF16),
        N2=vmem((2, rows, width), BF16),
        Q=vmem((2, heads, rows, 2 * HEAD), BF16),
        KV=vmem((2, heads, rows, 2 * HEAD), BF16),
        KT=vmem((2, heads, HEAD, rows), BF16),
        ATT=vmem((2, rows, (heads + 1) * HEAD), BF16),
        LSE=vmem((2, 8, rows), F32),
        PRE=vmem((2, rows, width), BF16),
        HID=vmem((rows, width), BF16),
        DPRE=vmem((rows, width), BF16),
        DQKV=vmem((rows, 3 * heads * HEAD), BF16),
        DA=vmem((2, rows, width), BF16),
        DKV=vmem((heads, rows, 2 * HEAD), F32),
        GRAD=vmem((heads, chunk, 2 * HEAD), BF16),
        GRADT=vmem((8, chunk), F32),
        DQT=vmem((heads, HEAD, chunk), F32),
        MID=vmem((2, CHUNKS * part, width), F32),
        DMID=vmem((CHUNKS * part, width), F32),
        PART=vmem((2, rows, width), BF16),
        RC=vmem((2, CHUNKS, part, width), BF16),
        RX=vmem((3, CHUNKS, part, width), BF16),
        STG=vmem((4, width // 2, width), BF16),
        GAINS=vmem((8, width), F32),
        BIAS=vmem((8, chunk), F32),
        GACC=vmem((2, 8, width), F32),
        in_send=dma((2, 3)),
        in_recv=dma((2, CHUNKS)),
        mate_send=dma((CHUNKS,)),
        mate_recv=dma((CHUNKS,)),
        pair_send=dma((7, CHUNKS)),
        pair_recv=dma((7, CHUNKS)),
        rs_send=dma((8, 2, CHUNKS)),
        rs_recv=dma((8, 2, CHUNKS)),
        w_recv=dma((2, PARTS, depth if inside else 1)),
        stg_send=dma((2, PARTS, 4)),
        out_send=dma((4, CHUNKS)),
        out_recv=dma((4, 2, 2)),
    )
    outs = dict(
        acts=jax.ShapeDtypeStruct(inputs.shape, BF16), igr=jax.ShapeDtypeStruct(inputs.shape, BF16)
    )
    if inside:
        slab = width // depth
        scratch.update(
            GR=vmem((2, PARTS, width, width), BF16),
            ZR=vmem((depth - 1, PARTS, slab, width), BF16),
            FIN=vmem((2, slab, width), F32),
            GIN=vmem((2, depth) + gain_rows.shape, F32),
            GC=vmem((8, width), F32),
            GX=vmem((8, width), F32),
            GY=vmem((8, width), F32),
            GZ=vmem((depth - 1, 8, width), F32),
            w_send=dma((PARTS, depth)),
            relay_send=dma((2, PARTS, depth)),
            onward_send=dma((2, PARTS, depth)),
            gr_recv=dma((2, PARTS, 4)),
            z_send=dma((PARTS, depth)),
            z_recv=dma((PARTS, depth - 1)),
            fin_send=dma((PARTS,)),
            gin_send=dma((2, depth)),
            gin_recv=dma((2, depth)),
            gg_send=dma((3 + depth,)),
            gg_recv=dma((4 + depth,)),
        )
        own = dict(own_a=weights[0], own_b=weights[1], own_c=weights[2])
        outs["gsum"] = jax.ShapeDtypeStruct((PARTS, slab, width), F32)
    else:
        own = dict(w_whole=weights)
        outs["grads"] = jax.ShapeDtypeStruct(weights.shape, BF16)
    outs["gain_out"] = jax.ShapeDtypeStruct((8, width), F32)
    given = dict(inp=inputs, cot=cotangent, **own, gain_rows=gain_rows, lengths=lengths)
    hbm = pl.BlockSpec(memory_space=pl.ANY)
    in_vmem = pl.BlockSpec(memory_space=pltpu.VMEM)
    small = ("gain_rows", "gain_out")
    in_smem = pl.BlockSpec(memory_space=pltpu.SMEM)
    return pl.pallas_call(
        functools.partial(
            block_kernel, inside, STEPS, list(given) + list(outs) + list(scratch)
        ),
        out_shape=tuple(outs.values()),
        in_specs=[
            in_vmem if name in small else in_smem if name == "lengths" else hbm for name in given
        ],
        out_specs=tuple(in_vmem if name in small else hbm for name in outs),
        scratch_shapes=list(scratch.values()),
        compiler_params=pltpu.CompilerParams(
            collective_id=0, has_side_effects=True, vmem_limit_bytes=VMEM_LIMIT
        ),
        cost_estimate=pl.CostEstimate(
            flops=27_000_000_000, bytes_accessed=40_000_000, transcendentals=20_000_000
        ),
        name="blocks",
    )(*given.values())


def pack_kernel(w_qkv, w_out, gains, own_a, gain_rows):
    heads = w_qkv.shape[2] // HEAD
    q, k, v = (w_qkv[i] for i in range(3))
    columns = []
    for h in range(heads):
        here = slice(h * HEAD, (h + 1) * HEAD)
        columns += [k[:, here], v[:, here]]
    turned = w_out[...].astype(F32).T.astype(BF16)
    own_a[...] = jnp.concatenate(columns + [q, turned], axis=1)
    gain_rows[...] = jnp.zeros_like(gain_rows)
    gain_rows[0:2, 0 : gains.shape[1]] = gains[...].astype(F32)


def pack_weights(w_qkv, w_out, gains):
    _, slab, columns = w_qkv.shape
    in_vmem = pl.BlockSpec(memory_space=pltpu.VMEM)
    return pl.pallas_call(
        pack_kernel,
        out_shape=(
            jax.ShapeDtypeStruct((slab, 4 * columns), BF16),
            jax.ShapeDtypeStruct((8, slab + -slab % 128), F32),
        ),
        in_specs=[in_vmem] * 3,
        out_specs=(in_vmem,) * 2,
        name="pack",
    )(w_qkv, w_out, gains)


def unpack_kernel(gsum, acts, igr, gain_part, *outs):
    acts_out, igr_out, gain_out, qkv_out, out_out, up_out, down_out = outs
    columns = qkv_out.shape[2]
    heads = columns // HEAD
    first = gsum[0]
    kv = [first[:, i * HEAD : (i + 1) * HEAD] for i in range(2 * heads)]
    qkv_out[0] = first[:, 2 * columns : 3 * columns]
    qkv_out[1] = jnp.concatenate(kv[0::2], axis=1)
    qkv_out[2] = jnp.concatenate(kv[1::2], axis=1)
    out_out[0] = first[:, 3 * columns :].T
    up_out[0] = gsum[1]
    down_out[...] = gsum[2]
    acts_out[0] = acts[...]
    igr_out[0] = igr[...]
    width, share = gain_part.shape[1], gain_out.shape[2]
    at = lax.axis_index("tensor") * lax.axis_size("dp") + lax.axis_index("dp")
    turned = pltpu.roll(gain_part[...], width - at * share, 1)
    gain_out[0] = turned[0:2, 0:share]


def unpack_results(total, acts, input_grads, gain_part, shapes):
    in_vmem = pl.BlockSpec(memory_space=pltpu.VMEM)
    return pl.pallas_call(
        unpack_kernel,
        out_shape=tuple(jax.ShapeDtypeStruct(shape, kind) for shape, kind in shapes),
        in_specs=[in_vmem] * 4,
        out_specs=(in_vmem,) * 7,
        name="unpack",
    )(total, acts, input_grads, gain_part)


def shards(inputs, lengths, gains, w_qkv, w_out, w_up, w_down, cotangent):
    local_rows, width = inputs.shape[1:]
    slab = w_up.shape[1]
    heads = w_qkv.shape[3] // HEAD
    depth = lax.axis_size("dp")
    y = lax.div(lax.axis_index("tensor"), 2)
    section = lax.axis_index("section")
    inside = slab % 16 == 0 and depth == 4
    axes = ("section", "tensor")
    if inside:
        own_a, gain_rows = pack_weights(w_qkv[0].transpose(1, 0, 2), w_out[0], gains[0])
        own = (own_a, w_up[0], w_down[0].T)
        acts, input_grads, total, gain_part = run_blocks(
            inputs, cotangent, own, gain_rows, lengths, depth, inside
        )
        columns = heads * HEAD
        results = unpack_results(
            total,
            acts,
            input_grads,
            gain_part,
            (
                ((1,) + acts.shape, BF16),
                ((1,) + acts.shape, BF16),
                ((1, 2, width // (depth * lax.axis_size("tensor"))), F32),
                ((3, slab, columns), F32),
                (w_out.shape, F32),
                (w_up.shape, F32),
                ((slab, width), F32),
            ),
        )
        acts, input_grads, gain_grads, qkv_grads, out_grads, up_grads, down_grads = results
        return (
            acts,
            input_grads,
            gain_grads,
            qkv_grads.transpose(1, 0, 2)[None],
            out_grads,
            up_grads,
            down_grads.T[None],
        )
    else:
        split = (slab, heads, HEAD)
        kv = jnp.stack([w_qkv[0, :, 1].reshape(split), w_qkv[0, :, 2].reshape(split)], axis=2)
        own = (
            jnp.concatenate([kv.reshape(slab, -1), w_qkv[0, :, 0], w_out[0].T], axis=1),
            w_up[0],
            w_down[0].T,
        )
        whole = lax.all_gather(jnp.stack(own), "dp", axis=1, tiled=True)
        weights = []
        for l in range(2):
            parts = []
            for to_y in range(2):
                pairs = [
                    (4 * l + 2 * c + x, 4 * c + 2 * to_y + x) for c in range(2) for x in range(2)
                ]
                parts.append(lax.ppermute(whole, axes, pairs))
            weights.append(jnp.where(y == 0, parts[0], parts[1]))
        weights = jnp.stack(weights)
        gain_rows = lax.all_gather(gains, "dp", axis=2, tiled=True)
        gain_rows = lax.all_gather(gain_rows, "section", axis=0, tiled=True)
        gain_rows = jnp.pad(gain_rows.reshape(4, width).astype(F32), ((0, 4), (0, 0)))
        acts, input_grads, partial, gain_part = run_blocks(
            inputs, cotangent, weights, gain_rows, lengths, depth, inside
        )
        total = jnp.zeros(partial.shape[1:], F32)
        for l in range(2):
            for from_y in range(2):
                pairs = [
                    (4 * c + 2 * from_y + x, 4 * l + 2 * c + x) for c in range(2) for x in range(2)
                ]
                total = total + lax.ppermute(partial[l], axes, pairs).astype(F32)
        total = lax.psum_scatter(total.astype(BF16), "dp", scatter_dimension=1, tiled=True)
        total = total.astype(F32)
        gain_part = lax.psum(gain_part[:4].reshape(2, 2, width), "section")
        gain_part = lax.dynamic_slice_in_dim(gain_part, section, 1, 0)
        first = (section == 0) & (jnp.arange(2) == 0)
        gain_part = gain_part * jnp.where(first, 1.0, 0.5)[None, :, None]
        gain_grads = lax.psum_scatter(
            gain_part, ("tensor", "dp"), scatter_dimension=2, tiled=True
        )
    columns = heads * HEAD
    kv = total[0, :, : 2 * columns].reshape(slab, heads, 2, HEAD)
    q = total[0, :, 2 * columns : 3 * columns]
    qkv_grads = jnp.stack([q, kv[:, :, 0].reshape(q.shape), kv[:, :, 1].reshape(q.shape)], axis=1)
    return (
        acts[None],
        input_grads[None],
        gain_grads,
        qkv_grads[None],
        total[0, :, 3 * columns :].T[None],
        total[1][None],
        total[2].T[None],
    )


def solution(mesh):
    in_specs = (
        P("dp", "tensor", None),
        P("dp"),
        P("section", None, "dp"),
        P("section", "dp", None, "tensor"),
        P("section", "tensor", "dp"),
        P("section", "dp", "tensor"),
        P("section", "tensor", "dp"),
        P("dp", "tensor", None),
    )
    out_specs = (
        P("section", "dp", "tensor", None),
        P("section", "dp", "tensor", None),
        P("section", None, ("tensor", "dp")),
        P("section", "dp", None, "tensor"),
        P("section", "tensor", "dp"),
        P("section", "dp", "tensor"),
        P("section", "tensor", "dp"),
    )
    return jax.shard_map(shards, mesh=mesh, in_specs=in_specs, out_specs=out_specs, check_vma=False)
```

```python
import functools

import jax
import jax.numpy as jnp
from jax import lax
from jax.experimental import pallas as pl
from jax.experimental.pallas import tpu as pltpu
from jax.sharding import PartitionSpec as P

HEAD = 64
EPSILON = 1e-05
MASKED = -1e30
CHUNKS = 4
PARTS = 3
VMEM_LIMIT = 63 << 20
TILE = 256
BF16 = jnp.bfloat16
F32 = jnp.float32
MESH = pl.DeviceIdType.MESH

SUM_ATTN = (0, 2)
SUM_MLP = (1, 3)
SUM_DMLP = (6, 4)
SUM_DATTN = (7, 5)
PAIR_N2 = (0, 1)
PAIR_N1 = (6, 2)
PAIR_DA = (4, 3)
PAIR_DR = 5


def nn(left, right):
    return lax.dot_general(left, right, (((1,), (0,)), ((), ())), preferred_element_type=F32)


def nt(left, right):
    return lax.dot_general(left, right, (((1,), (1,)), ((), ())), preferred_element_type=F32)


def tn(left, right):
    return lax.dot_general(left, right, (((0,), (0,)), ((), ())), preferred_element_type=F32)


def unit_rows(rows):
    centre = rows - jnp.mean(rows, axis=-1, keepdims=True)
    spread = jnp.mean(centre * centre, axis=-1, keepdims=True)
    scale = lax.rsqrt(spread + EPSILON)
    return centre * scale, scale


def norm_back(unit, scale, gain, grad):
    wide = grad * gain
    inner = jnp.mean(wide * unit, axis=-1, keepdims=True)
    return scale * (wide - jnp.mean(wide, axis=-1, keepdims=True) - unit * inner)


def gelu_parts(x):
    root = 0.7978845608028654
    square = x * x
    bend = jnp.tanh(root * x * (1.0 + 0.044715 * square))
    half = 0.5 + 0.5 * bend
    slope = half + 0.5 * x * (1.0 - bend * bend) * (root * (1.0 + 0.134145 * square))
    return x * half, slope


class Names:
    pass


def block_kernel(inside, steps, names, *refs):
    n = Names()
    for name, ref in zip(names, refs, strict=True):
        setattr(n, name, ref)
    s = lax.axis_index("section")
    t = lax.axis_index("tensor")
    z = lax.axis_index("dp")
    x = lax.rem(t, 2)
    y = lax.div(t, 2)
    t_y = 2 * (1 - y) + x
    mate = (1 - s, t, z)
    peer_x = (s, 2 * y + 1 - x, z)
    peer_y = (s, t_y, z)
    hub = s == y
    rows_all, width = n.CT.shape
    chunk = rows_all // CHUNKS
    part = chunk // 2
    half = CHUNKS // 2
    heads = n.KT.shape[1]
    tiles = width // TILE
    depth = lax.axis_size("dp")
    slab = width // depth
    q_columns = 2 * heads * HEAD
    o_columns = 3 * heads * HEAD

    def remote(src, dst, send_sem, recv_sem, device):
        return pltpu.make_async_remote_copy(
            src_ref=src,
            dst_ref=dst,
            send_sem=send_sem,
            recv_sem=recv_sem,
            device_id=device,
            device_id_type=MESH,
        )

    def done(ref, sem):
        pltpu.make_async_copy(ref, ref, sem).wait()

    def rows_of(j):
        return pl.ds(pl.multiple_of(j * chunk, chunk), chunk)

    def half_of(j, c):
        return pl.ds(pl.multiple_of(j * chunk + c * part, part), part)

    def own_of(j):
        return pl.ds(pl.multiple_of(j * part, part), part)

    def slab_of(i):
        return pl.ds(pl.multiple_of(i * slab, slab), slab)

    def bytes_of(count):
        return n.PART.at[0, 0:count]

    if inside:
        q, k, v = (n.w_qkv[i] for i in range(3))
        columns = []
        for h in range(heads):
            here = slice(h * HEAD, (h + 1) * HEAD)
            columns += [k[:, here], v[:, here]]
        turned = n.w_out[...].astype(F32).T.astype(BF16)
        n.own_a[...] = jnp.concatenate(columns + [q, turned], axis=1)
        n.OWN_GAINS[...] = jnp.zeros_like(n.OWN_GAINS)
        n.OWN_GAINS[0:2, 0:slab] = n.gain_rows[...].astype(F32)

    n.GACC[...] = jnp.zeros_like(n.GACC)
    n.BIAS[...] = jnp.where(n.lengths[y] == rows_all, 0.0, MASKED) + jnp.zeros_like(n.BIAS)

    barrier = pltpu.get_barrier_semaphore()
    greeted = 0
    for other_s in range(2):
        for other in range(CHUNKS):
            greeted += 1

            @pl.when((s != other_s) | (t != other))
            def _():
                pl.semaphore_signal(
                    barrier, inc=1, device_id=(other_s, other, z), device_id_type=MESH
                )

        if inside:
            for other in range(depth):
                greeted += 1

                @pl.when(z != other)
                def _():
                    pl.semaphore_signal(
                        barrier, inc=1, device_id=(other_s, t, other), device_id_type=MESH
                    )

    pl.semaphore_wait(barrier, greeted - 1 - (2 if inside else 0))

    def pick(index, values):
        value = values[0]
        for at in range(1, len(values)):
            value = jnp.where(index == at, values[at], value)
        return value

    def not_far(end):
        if end == 0:
            return z < depth // 2
        if end == depth - 1:
            return z >= depth // 2
        return z >= 0

    def weights_send(l, p):
        if not inside:
            pltpu.make_async_copy(n.w_whole.at[l, p], n.W.at[l, p], n.w_recv.at[l, p, 0]).start()
            return
        own = (n.own_a, n.own_b, n.own_c)[p]

        @pl.when(s == l)
        def _():
            for far in range(depth):
                @pl.when(hub & (z == far))
                def _():
                    pltpu.make_async_copy(
                        own, n.W.at[l, p, slab_of(z)], n.w_recv.at[l, p, z]
                    ).start()

                @pl.when(jnp.logical_not(hub & (z == far)) & not_far(far))
                def _():
                    remote(
                        own,
                        n.W.at[l, p, slab_of(z)],
                        n.w_send.at[p, far],
                        n.w_recv.at[l, p, z],
                        (y, t, far),
                    ).start()

    def weights_sent(p):
        own = (n.own_a, n.own_b, n.own_c)[p]
        for far in range(depth):

            @pl.when(jnp.logical_not(hub & (z == far)) & not_far(far))
            def _():
                done(own, n.w_send.at[p, far])

    def weights_relay(l, p, step):
        if not inside:
            return

        @pl.when(hub)
        def _():
            beside = z + 1 - 2 * lax.rem(z, 2)
            low = z < 2
            far = pick(step, [z, beside, jnp.where(low, 2, 1), jnp.where(low, 3, 0)])
            here = n.W.at[l, p, slab_of(far)]
            done(here, n.w_recv.at[l, p, far])
            remote(
                here, here, n.relay_send.at[l, p, far], n.w_recv.at[l, p, far], peer_y
            ).start()
            for place, end in ((1, 0), (2, 3)):

                @pl.when((z == place) & (far >= 2 if place == 1 else far < 2))
                def _():
                    remote(
                        here,
                        here,
                        n.onward_send.at[l, p, far],
                        n.w_recv.at[l, p, far],
                        (s, t, end),
                    ).start()

    def weights_wait(l, p):
        if not inside:
            done(n.W.at[l, p], n.w_recv.at[l, p, 0])
            return

        @pl.when(jnp.logical_not(hub))
        def _():
            for far in range(depth):
                done(n.W.at[l, p, slab_of(far)], n.w_recv.at[l, p, far])

    t_x = 2 * y + 1 - x
    t_far = 2 * (1 - y) + 1 - x

    def landing(which, target, source_t):
        return target.at[own_of(source_t)] if which == 0 else target.at[half_of(source_t, s)]

    def spread(which, source, target):
        here = source.at[y, half_of(0, s)]
        own = landing(which, target, t)
        remote(
            source.at[1 - y, half_of(0, s)],
            own,
            n.in_send.at[which, 0],
            n.in_recv.at[which, t],
            peer_y,
        ).start()
        remote(here, own, n.in_send.at[which, 1], n.in_recv.at[which, t], peer_x).start()
        pltpu.make_async_copy(here, own, n.in_recv.at[which, t]).start()

    def spread_pass(which, target):
        near = landing(which, target, t_y)
        done(near, n.in_recv.at[which, t_y])
        remote(near, near, n.in_send.at[which, 2], n.in_recv.at[which, t_y], peer_x).start()

    def spread_wait(which, j):
        @pl.when(j != t_y)
        def _():
            done(bytes_of(part), n.in_recv.at[which, j])

    def inputs_pass(j):
        spread_wait(0, j)
        norm_first(0, n.X0[own_of(j), :].astype(F32), j)

    def cotangent_pass(j):
        here = n.CT.at[half_of(j, s)]
        spread_wait(1, j)
        remote(here, here, n.mate_send.at[j], n.mate_recv.at[j], mate).start()

    def cotangent_wait(j):
        done(bytes_of(part), n.mate_recv.at[j])

    def spread_done(which):
        for way in range(3):
            done(bytes_of(part), n.in_send.at[which, way])
        if which == 1:
            for j in range(CHUNKS):
                done(bytes_of(part), n.mate_send.at[j])

    def pair_start(stage, ref, j):
        here = ref.at[half_of(j, s)]
        remote(here, here, n.pair_send.at[stage, j], n.pair_recv.at[stage, j], mate).start()

    def pair_wait(stage, j):
        done(bytes_of(part), n.pair_recv.at[stage, j])

    def sum_start(stage, j):
        b = stage % 2
        remote(
            n.PART.at[b, half_of(j, 1 - s)],
            n.RC.at[b, j],
            n.rs_send.at[stage, 0, j],
            n.rs_recv.at[stage, 0, j],
            mate,
        ).start()

    def sum_pass(stage, j):
        b = lax.rem(stage, 2)
        here = half_of(j, s)
        done(n.RC.at[b, j], n.rs_recv.at[stage, 0, j])
        n.PART[b, here, :] = (
            n.PART[b, here, :].astype(F32) + n.RC[b, j].astype(F32)
        ).astype(BF16)
        arriving = jnp.where(stage == SUM_DMLP[1], 2, b)
        one_way = (stage == SUM_MLP[1]) | (stage == SUM_DATTN[0])

        @pl.when(jnp.logical_not(one_way) | (lax.rem(j, 2) != x))
        def _():
            remote(
                n.PART.at[b, here],
                n.RX.at[arriving, j],
                n.rs_send.at[stage, 1, j],
                n.rs_recv.at[stage, 1, j],
                peer_x,
            ).start()

        done(n.RC.at[b, j], n.rs_send.at[stage, 0, j])

    def sum_sent(stage, j):
        done(n.RX.at[stage % 2, j], n.rs_send.at[stage, 1, j])

    def sum_wait(stage, j):
        b = stage % 2
        arriving = 2 if stage == SUM_DMLP[1] else b
        done(n.RX.at[arriving, j], n.rs_recv.at[stage, 1, j])
        total = n.PART[b, half_of(j, s), :].astype(F32) + n.RX[arriving, j].astype(F32)
        if stage not in (SUM_MLP[1], SUM_DATTN[0]):
            sum_sent(stage, j)
        return total

    first_index = lax.broadcasted_iota(jnp.int32, (chunk, chunk), 0)
    second_index = lax.broadcasted_iota(jnp.int32, (chunk, chunk), 1)

    def scores(l, st, i, j, diagonal, keys_first):
        if l == 0:
            grown = st * st + 1.0
            inverse = lax.rsqrt(grown)
            magnitude = grown * inverse
            sign = st * inverse
        else:
            inverse, magnitude, sign = None, st, None
        if diagonal:
            seen = first_index <= second_index if keys_first else second_index <= first_index
            magnitude = jnp.where(seen, magnitude, MASKED)
        else:
            apart = (j >= half) & (i < half)
            magnitude = magnitude + jnp.where(apart, n.BIAS[0:1, :], 0.0)
        return inverse, magnitude, sign

    def norm_first(l, own_rows, j):
        unit, _ = unit_rows(own_rows)
        n.N1[l, half_of(j, s), :] = (unit * n.GAINS[2 * l : 2 * l + 1, :]).astype(BF16)
        pair_start(PAIR_N1[l], n.N1.at[l], j)

    def qkv_product(l, j):
        rows = rows_of(j)
        pair_wait(PAIR_N1[l], j)
        kv = nn(n.N1[l, rows, :], n.W[l, 0, :, 0:q_columns])
        kv_low = kv.astype(BF16)
        turned = kv.T.astype(BF16)
        for h in range(heads):
            n.KV[l, h, rows, :] = kv_low[:, 2 * h * HEAD : 2 * (h + 1) * HEAD]
            n.KT[l, h, :, rows] = turned[2 * h * HEAD : (2 * h + 1) * HEAD]
        q = nn(n.N1[l, rows, :], n.W[l, 0, :, q_columns:o_columns]).astype(BF16)
        blank = jnp.zeros((chunk, HEAD), BF16)
        for h in range(heads):
            q_h = q[:, h * HEAD : (h + 1) * HEAD] * jnp.asarray(HEAD**-0.5, BF16)
            n.Q[l, h, rows, :] = jnp.concatenate([q_h, blank], axis=1)

    def attend(l, j):
        rows = rows_of(j)

        def block(i, carry, diagonal):
            keys = rows_of(i)
            new = []
            for h in range(heads):
                top, total, out = carry[h]
                kv = n.KV[l, h, keys, :]
                st = nt(n.Q[l, h, rows, :], kv)
                _, magnitude, sign = scores(l, st, i, j, diagonal, False)
                new_top = jnp.maximum(top, jnp.max(magnitude, axis=1, keepdims=True))
                weights = jnp.exp(magnitude - new_top)
                shrink = jnp.exp(top - new_top)
                total = total * shrink + jnp.sum(weights, axis=1, keepdims=True)
                signed = weights if l == 1 else sign * weights
                out = out * shrink + nn(signed.astype(BF16), kv)
                new.append((new_top, total, out))
            return tuple(new)

        carry = (
            jnp.full((chunk, 1), MASKED, F32),
            jnp.zeros((chunk, 1), F32),
            jnp.zeros((chunk, 2 * HEAD), F32),
        )
        carry = block(j, (carry,) * heads, True)
        carry = lax.fori_loop(0, j, lambda i, c: block(i, c, False), carry)
        lane = lax.broadcasted_iota(jnp.int32, (chunk, 128), 1)
        logs = jnp.zeros((chunk, 128), F32)
        outs = [jnp.zeros((chunk, HEAD), BF16)]
        for h in range(heads):
            top, total, out = carry[h]
            outs.append((out / total)[:, HEAD:].astype(BF16))
            logs = jnp.where(lane == h, top + jnp.log(total), logs)
        n.ATT[l, rows, :] = jnp.concatenate(outs, axis=1)
        n.LSE[l, :, rows] = logs.T[0:8]

    def out_product(l, j):
        rows = rows_of(j)
        for i in range(tiles):
            here = slice(i * TILE, (i + 1) * TILE)
            n.PART[0, rows, here] = nt(
                n.ATT[l, rows, :], n.W[l, 0, here, o_columns - HEAD : width]
            ).astype(BF16)
        sum_start(SUM_ATTN[l], j)

    def attn_sum(l, j):
        source = n.X0 if l == 0 else n.Y0
        own = half_of(j, s)
        middle = source[own_of(j), :].astype(F32) + sum_wait(SUM_ATTN[l], j)
        n.MID[l, own_of(j), :] = middle
        unit, _ = unit_rows(middle)
        n.N2[l, own, :] = (unit * n.GAINS[2 * l + 1 : 2 * l + 2, :]).astype(BF16)
        pair_start(PAIR_N2[l], n.N2.at[l], j)

    def up_product(l, j):
        rows = rows_of(j)
        pair_wait(PAIR_N2[l], j)
        for i in range(tiles):
            here = slice(i * TILE, (i + 1) * TILE)
            pre = nn(n.N2[l, rows, :], n.W[l, 1, :, here])
            n.PRE[l, rows, here] = pre.astype(BF16)
            n.HID[rows, here] = gelu_parts(pre)[0].astype(BF16)
        for i in range(tiles):
            here = slice(i * TILE, (i + 1) * TILE)
            n.PART[1, rows, here] = nt(n.HID[rows, :], n.W[l, 2, here, :]).astype(BF16)
        sum_start(SUM_MLP[l], j)

    def mlp_sum(l, j):
        if l == 0:
            result = (n.MID[l, own_of(j), :] + sum_wait(SUM_MLP[l], j)).astype(BF16)
            n.Y0[own_of(j), :] = result
            norm_first(1, result.astype(F32), j)
            give_out(2, 0, n.Y0.at[own_of(j)], n.acts, j)
        else:

            @pl.when(lax.rem(j, 2) == x)
            def _():
                result = n.MID[l, own_of(j), :] + sum_wait(SUM_MLP[l], j)
                n.PART[1, half_of(j, s), :] = result.astype(BF16)
                give_out(0, 1, n.PART.at[1, half_of(j, s)], n.acts, j)

            @pl.when(lax.rem(j, 2) != x)
            def _():
                sum_sent(SUM_MLP[l], j)

    def give_out(which, section, here, out, j):
        target = out.at[y, half_of(0, s)]

        @pl.when((s == section) & (t == j))
        def _():
            copy = pltpu.make_async_copy(here, target, n.out_send.at[which, j])
            copy.start()
            copy.wait()

        @pl.when((lax.rem(j, 2) == x) & ((s != section) | (t != j)))
        def _():
            remote(
                here,
                target,
                n.out_send.at[which, j],
                n.out_recv.at[which, y, s],
                (section, j, z),
            ).start()

    def given_out(which, section, j):
        @pl.when((lax.rem(j, 2) == x) & ((s != section) | (t != j)))
        def _():
            done(bytes_of(part), n.out_send.at[which, j])

    def got_out(which, section):
        @pl.when(s == section)
        def _():
            for m in range(2):
                for c in range(2):

                    @pl.when((y != m) | (s != c))
                    def _():
                        done(bytes_of(part), n.out_recv.at[which, m, c])

    def hidden_back(l, j):
        rows = rows_of(j)
        if l == 1:
            cotangent_wait(j)
        else:
            pair_wait(PAIR_DR, j)
        source = n.CT if l == 1 else n.DR
        for i in range(tiles):
            here = slice(i * TILE, (i + 1) * TILE)
            back = nn(source[rows, :], n.W[l, 2, :, here])
            hidden, slope = gelu_parts(n.PRE[l, rows, here].astype(F32))
            n.HID[rows, here] = hidden.astype(BF16)
            n.DPRE[rows, here] = (slope * back).astype(BF16)
        for i in range(tiles):
            here = slice(i * TILE, (i + 1) * TILE)
            n.PART[0, rows, here] = nt(n.DPRE[rows, :], n.W[l, 1, here, :]).astype(BF16)
        sum_start(SUM_DMLP[l], j)

    def mlp_back_sum(l, j):
        total = sum_wait(SUM_DMLP[l], j)
        source = n.CT if l == 1 else n.DR
        own = half_of(j, s)
        unit, scale = unit_rows(n.MID[l, own_of(j), :])
        n.GACC[l, 1:2, :] += jnp.sum(total * unit, axis=0, keepdims=True)
        gain = n.GAINS[2 * l + 1 : 2 * l + 2, :]
        grad = source[own, :].astype(F32) + norm_back(unit, scale, gain, total)
        n.MID[l, own_of(j), :] = grad
        n.DA[l, own, :] = grad.astype(BF16)
        pair_start(PAIR_DA[l], n.DA.at[l], j)

    def attn_grad(l, j):
        rows = rows_of(j)
        pair_wait(PAIR_DA[l], j)

        @pl.when(j == CHUNKS - 1)
        def _():
            n.DKV[...] = jnp.zeros_like(n.DKV)

        low = nn(n.DA[l, rows, :], n.W[l, 0, :, o_columns - HEAD : width]).astype(BF16)
        product = low.astype(F32) * n.ATT[l, rows, :].astype(F32)
        blank = jnp.zeros((chunk, HEAD), BF16)
        lane = lax.broadcasted_iota(jnp.int32, (chunk, 128), 1)
        inner = jnp.zeros((chunk, 128), F32)
        for h in range(heads):
            here = slice((h + 1) * HEAD, (h + 2) * HEAD)
            n.GRAD[h] = jnp.concatenate([blank, low[:, here]], axis=1)
            inner = jnp.where(
                lane == h, jnp.sum(product[:, here], axis=1, keepdims=True), inner
            )
        n.GRADT[...] = inner.T[0:8]

    def attend_back(l, j):
        rows = rows_of(j)

        def block(i, carry, diagonal):
            keys = rows_of(i)
            new = []
            for h in range(heads):
                kv = n.KV[l, h, keys, :]
                st = nt(kv, n.Q[l, h, rows, :])
                dp = nt(kv, n.GRAD[h])
                inverse, magnitude, sign = scores(l, st, i, j, diagonal, True)
                weights = jnp.exp(magnitude - n.LSE[l, h : h + 1, rows])
                inner = n.GRADT[h : h + 1, :]
                if l == 0:
                    signed = sign * weights
                    ds = weights * (
                        sign * (sign * dp - inner) + dp * (inverse * inverse * inverse)
                    )
                else:
                    signed = weights
                    ds = weights * (dp - inner)
                ds = ds.astype(BF16)
                n.DKV[h, keys, :] += nn(ds, n.Q[l, h, rows, :]) + nn(
                    signed.astype(BF16), n.GRAD[h]
                )
                new.append(carry[h] + nn(n.KT[l, h, :, keys], ds))
            return tuple(new)

        blank = jnp.zeros((HEAD, chunk), F32)
        query_grad = block(j, (blank,) * heads, True)
        query_grad = lax.fori_loop(0, j, lambda i, c: block(i, c, False), query_grad)
        for h in range(heads):
            n.DQT[h] = query_grad[h] * HEAD**-0.5

    def qkv_back(l, j):
        rows = rows_of(j)
        turned = jnp.concatenate([n.DQT[h] for h in range(heads)], axis=0).T
        for h in range(heads):
            n.DQKV[rows, 2 * h * HEAD : 2 * (h + 1) * HEAD] = n.DKV[h, rows, :].astype(BF16)
        n.DQKV[rows, q_columns:] = turned.astype(BF16)
        if l == 1:
            given_out(0, 1, j)
        for i in range(tiles):
            here = slice(i * TILE, (i + 1) * TILE)
            n.PART[1, rows, here] = nt(n.DQKV[rows, :], n.W[l, 0, here, 0:o_columns]).astype(
                BF16
            )
        sum_start(SUM_DATTN[l], j)

    def attn_back_result(l, j):
        total = sum_wait(SUM_DATTN[l], j)
        source = n.X0 if l == 0 else n.Y0
        unit, scale = unit_rows(source[own_of(j), :].astype(F32))
        n.GACC[l, 0:1, :] += jnp.sum(total * unit, axis=0, keepdims=True)
        gain = n.GAINS[2 * l : 2 * l + 1, :]
        return n.MID[l, own_of(j), :] + norm_back(unit, scale, gain, total)

    def attn_back_sum(l, j):
        own = half_of(j, s)
        if l == 1:
            n.DR[own, :] = attn_back_result(l, j).astype(BF16)
            pair_start(PAIR_DR, n.DR, j)
            give_out(3, 1, n.DR.at[own], n.igr, j)
        else:

            @pl.when(lax.rem(j, 2) == x)
            def _():
                n.PART[1, own, :] = attn_back_result(l, j).astype(BF16)
                give_out(1, 0, n.PART.at[1, own], n.igr, j)

            @pl.when(lax.rem(j, 2) != x)
            def _():
                sum_sent(SUM_DATTN[l], j)

    long = width // 2
    grad_order = ((1, 2), (1, 1), (1, 0), (0, 2), (0, 1), (0, 0))
    grad_to = 2 * s + x

    def kept_here(l):
        return hub & (s == l)

    def grad_sent(l, p, i):
        if not inside:
            done(n.STG.at[0], n.stg_send.at[l, p, i])
            return

        @pl.when(jnp.logical_not(kept_here(l)))
        def _():
            for k in range(2):
                done(n.STG.at[0, 0:slab], n.stg_send.at[l, p, 2 * i + k])

    def weight_grad(l, p, i):
        at = grad_order.index((l, p))
        slot = 2 * (at % 2) + i
        if at > 1:
            grad_sent(*grad_order[at - 2], i)
        rows = pl.ds(pl.multiple_of(i * long, long), long)
        if p == 0:
            left = n.N1[l, :, rows]
            n.STG[slot, :, 0:256] = tn(left, n.DQKV[:, 0:256]).astype(BF16)
            n.STG[slot, :, 256:512] = tn(left, n.DQKV[:, 256:512]).astype(BF16)
            last = tn(left, n.DQKV[:, 512:o_columns])
            out_part = tn(n.DA[l, :, rows], n.ATT[l])
            n.STG[slot, :, 512:width] = jnp.concatenate([last, out_part[:, HEAD:]], axis=1).astype(
                BF16
            )
        else:
            if p == 1:
                left, right = n.N2[l, :, rows], n.DPRE
            else:
                left, right = (n.CT if l == 1 else n.DR)[:, rows], n.HID
            for k in range(tiles):
                here = slice(k * TILE, (k + 1) * TILE)
                n.STG[slot, :, here] = tn(left, right[:, here]).astype(BF16)
        if not inside:
            pltpu.make_async_copy(
                n.STG.at[slot], n.grads.at[l, p, rows], n.stg_send.at[l, p, i]
            ).start()
            return

        @pl.when(kept_here(l))
        def _():
            n.GR[0, p, rows, :] = n.STG[slot]

        @pl.when(jnp.logical_not(kept_here(l)))
        def _():
            way = jnp.where(hub, 0, 1)
            for k in range(2):
                k_at = jnp.where(i == 0, k, 1 - k)
                at_slab = 2 * i + k_at
                remote(
                    n.STG.at[slot, slab_of(k_at)],
                    n.GR.at[way, p, slab_of(at_slab)],
                    n.stg_send.at[l, p, at_slab],
                    n.gr_recv.at[way, p, at_slab],
                    (l, grad_to, z),
                ).start()

    def slot_of(source, target):
        return jnp.where(source > target, source - 1, source)

    def grad_pass(l, p, far):
        if not inside:
            return

        @pl.when(s == l)
        def _():
            here = slab_of(far)

            @pl.when(jnp.logical_not(hub))
            def _():
                done(n.GR.at[0, p, here], n.gr_recv.at[0, p, far])

            done(n.GR.at[1, p, here], n.gr_recv.at[1, p, far])

            @pl.when(z != far)
            def _():
                n.GR[0, p, here, :] = (
                    n.GR[0, p, here, :].astype(F32) + n.GR[1, p, here, :].astype(F32)
                ).astype(BF16)
                slot = slot_of(z, far)
                remote(
                    n.GR.at[0, p, here],
                    n.ZR.at[slot, p],
                    n.z_send.at[p, far],
                    n.z_recv.at[p, slot],
                    (s, t, far),
                ).start()

    def grad_final(l, p):
        if not inside:
            return

        @pl.when(s == l)
        def _():
            here = slab_of(z)
            total = n.GR[0, p, here, :].astype(F32) + n.GR[1, p, here, :].astype(F32)
            for slot in range(depth - 1):
                done(n.ZR.at[slot, p], n.z_recv.at[p, slot])
                total = total + n.ZR[slot, p].astype(F32)
            slot = lax.rem(p, 2)

            @pl.when(p == 0)
            def _():
                done(n.FIN.at[0], n.fin_send.at[2])

            n.FIN[slot] = total
            pltpu.make_async_copy(n.FIN.at[slot], n.gsum.at[p], n.fin_send.at[p]).start()

    def grads_done():
        for i in range(2):
            grad_sent(*grad_order[-1], i)
        if not inside:
            return
        for far in range(depth):

            @pl.when(z != far)
            def _():
                done(n.ZR.at[0, 0], n.z_send.at[0, far])

        done(n.FIN.at[0], n.fin_send.at[0])
        done(n.FIN.at[1], n.fin_send.at[1])

    def gains_send():
        if not inside:
            n.GAINS[...] = n.gain_rows[...]
            return
        n.GIN[s, z] = n.OWN_GAINS[...]
        for c in range(2):
            for far in range(depth):

                @pl.when((s != c) | (z != far))
                def _():
                    remote(
                        n.OWN_GAINS,
                        n.GIN.at[s, z],
                        n.gin_send.at[c, far],
                        n.gin_recv.at[s, z],
                        (c, t, far),
                    ).start()

    def gains_wait():
        if not inside:
            return
        for c in range(2):
            for far in range(depth):

                @pl.when((s != c) | (z != far))
                def _():
                    done(n.OWN_GAINS, n.gin_recv.at[c, far])
                    done(n.OWN_GAINS, n.gin_send.at[c, far])

                for k in range(2):
                    n.GAINS[2 * c + k : 2 * c + k + 1, far * slab : (far + 1) * slab] = n.GIN[
                        c, far, k : k + 1, 0:slab
                    ]

    def gain_grads(step):
        if not inside:
            return
        if step == 0:
            remote(n.GACC.at[1 - s], n.GC, n.gg_send.at[0], n.gg_recv.at[0], mate).start()
        elif step == 1:
            done(n.GC, n.gg_recv.at[0])
            n.GACC[s] += n.GC[...]
            remote(n.GACC.at[s], n.GX, n.gg_send.at[6], n.gg_recv.at[4], peer_x).start()
        elif step == 2:
            done(n.GX, n.gg_recv.at[4])
            done(n.GX, n.gg_send.at[6])
            row = lax.broadcasted_iota(jnp.int32, n.GX.shape, 0)
            n.GACC[s] += jnp.where((row == 0) & (s == 0), n.GX[...], 0.0)
            remote(n.GACC.at[s], n.GY, n.gg_send.at[1], n.gg_recv.at[1], peer_y).start()
        else:
            done(n.GY, n.gg_recv.at[1])
            n.GC[...] = n.GACC[s] + n.GY[...]
            for far in range(depth):

                @pl.when(z != far)
                def _():
                    slot = slot_of(z, far)
                    remote(
                        n.GC,
                        n.GZ.at[slot],
                        n.gg_send.at[2 + far],
                        n.gg_recv.at[5 + slot],
                        (s, t, far),
                    ).start()

    def gain_grads_done():
        if not inside:
            n.gain_out[...] = jnp.concatenate([n.GACC[0, 0:2], n.GACC[1, 0:2], n.GACC[0, 4:8]])
            return
        total = n.GC[...]
        for slot in range(depth - 1):
            done(n.GZ.at[slot], n.gg_recv.at[5 + slot])
            total = total + n.GZ[slot]
        n.gain_out[...] = total
        done(n.GC, n.gg_send.at[0])
        done(n.GC, n.gg_send.at[1])
        for far in range(depth):

            @pl.when(z != far)
            def _():
                done(n.GC, n.gg_send.at[2 + far])

    def early_sends():
        if inside:
            for p in range(PARTS):
                weights_sent(p)
                for l in range(2):

                    @pl.when(hub)
                    def _():
                        for far in range(depth):
                            done(n.W.at[l, p, slab_of(far)], n.relay_send.at[l, p, far])

                            @pl.when((z == 1) if far >= 2 else (z == 2))
                            def _():
                                done(n.W.at[l, p, slab_of(far)], n.onward_send.at[l, p, far])

            for p in (1, 2):
                for far in range(depth):

                    @pl.when(z != far)
                    def _():
                        done(n.ZR.at[0, p], n.z_send.at[p, far])

        spread_done(0)
        spread_done(1)

        @pl.loop(0, CHUNKS)
        def _(j):
            for stage in range(7):
                done(bytes_of(part), n.pair_send.at[stage, j])
            for which, section in ((1, 0), (2, 0), (3, 1)):
                given_out(which, section, j)

        for which, section in ((0, 1), (2, 0), (3, 1)):
            got_out(which, section)
        for i in range(2):
            grad_sent(*grad_order[-2], i)

    tasks = {"none": lambda h, j: None}
    for l in range(2):
        tasks[f"nq{l}"] = lambda h, j, l=l: qkv_product(l, j)
        tasks[f"at{l}"] = lambda h, j, l=l: attend(l, j)
        tasks[f"op{l}"] = lambda h, j, l=l: out_product(l, j)
        tasks[f"sa{l}"] = lambda h, j, l=l: attn_sum(l, j)
        tasks[f"ud{l}"] = lambda h, j, l=l: up_product(l, j)
        tasks[f"sm{l}"] = lambda h, j, l=l: mlp_sum(l, j)
        tasks[f"hu{l}"] = lambda h, j, l=l: hidden_back(l, j)
        tasks[f"sd{l}"] = lambda h, j, l=l: mlp_back_sum(l, j)
        tasks[f"ag{l}"] = lambda h, j, l=l: attn_grad(l, j)
        tasks[f"ab{l}"] = lambda h, j, l=l: attend_back(l, j)
        tasks[f"qb{l}"] = lambda h, j, l=l: qkv_back(l, j)
        tasks[f"sb{l}"] = lambda h, j, l=l: attn_back_sum(l, j)
        for p in range(PARTS):
            tasks[f"wg{l}{p}"] = lambda h, j, l=l, p=p: weight_grad(l, p, j)
    for p in range(PARTS):
        tasks[f"ws{p}"] = lambda h, j, p=p: weights_send(1, p)
        tasks[f"wt{p}"] = lambda h, j, p=p: weights_send(0, p)
    tasks["r"] = lambda h, j: sum_pass(h, j)
    tasks["x0"] = lambda h, j: inputs_pass(j)
    tasks["x1"] = lambda h, j: cotangent_pass(j)
    tasks["wr"] = lambda h, j: weights_relay(lax.div(h, PARTS), lax.rem(h, PARTS), j)
    tasks["ww"] = lambda h, j: weights_wait(h, j)
    for l in range(2):
        tasks[f"gp{l}"] = lambda h, j, l=l: grad_pass(l, h, j)
    tasks["es"] = lambda h, j: early_sends()
    tasks["gf"] = lambda h, j: grad_final(j, h)
    for step in range(4):
        tasks[f"gg{step}"] = lambda h, j, step=step: gain_grads(step)
    tasks["gw"] = lambda h, j: gains_wait()
    tasks["xp"] = lambda h, j: spread_pass(0, n.X0)
    tasks["cp"] = lambda h, j: spread_pass(1, n.CT)
    tasks["cs"] = lambda h, j: spread(1, n.cot, n.CT)
    used = {"none"} | {name for name, _, _ in steps}
    order = [name for name in tasks if name in used]
    run = [tasks[name] for name in order]

    weights_send(0, 0)
    gains_send()
    spread(0, n.inp, n.X0)

    group = 6
    codes = [order.index(name) * 32 + h * 4 + j for name, h, j in steps]
    codes = [0] * (-len(codes) % group) + codes
    pairs = [codes[i] + 4096 * codes[i + 1] for i in range(0, len(codes), 2)]
    per_group = group // 2
    groups = len(pairs) // per_group

    def dispatch(low, high, op, h, j):
        if high - low == 1:
            run[low](h, j)
            return
        middle = (low + high) // 2
        lax.cond(
            op < middle,
            lambda: dispatch(low, middle, op, h, j),
            lambda: dispatch(middle, high, op, h, j),
        )

    @pl.loop(0, groups)
    def _(g):
        words = [
            pick(g, [pairs[q * per_group + w] for q in range(groups)]) for w in range(per_group)
        ]

        @pl.loop(0, group)
        def _(i):
            word = pick(lax.shift_right_logical(i, 1), words)
            code = jnp.where((i & 1) == 0, word & 4095, lax.shift_right_logical(word, 12))
            dispatch(
                0,
                len(run),
                lax.shift_right_logical(code, 5),
                lax.shift_right_logical(code, 2) & 7,
                code & 3,
            )

    got_out(1, 0)
    grads_done()
    gain_grads_done()


STEPS = (
    ("cs", 0, 0), ("wt2", 0, 0), ("wt1", 0, 0), ("wr", 0, 0), ("xp", 0, 0), ("wr", 0, 1),
    ("wr", 0, 2), ("gw", 0, 0), ("wr", 0, 3), ("x0", 0, 0), ("x0", 0, 1), ("wr", 2, 2),
    ("x0", 0, 2), ("wr", 2, 0), ("cp", 0, 0), ("wr", 2, 1), ("ww", 0, 0), ("nq0", 0, 1),
    ("nq0", 0, 0), ("at0", 3, 1), ("nq0", 0, 2), ("op0", 0, 1), ("wr", 1, 2), ("x0", 0, 3),
    ("x1", 0, 3), ("at0", 3, 2), ("wr", 1, 0), ("wr", 1, 1), ("wr", 1, 3), ("op0", 0, 2),
    ("ws0", 0, 0), ("at0", 3, 0), ("op0", 0, 0), ("nq0", 0, 3), ("wr", 2, 3), ("r", 0, 1),
    ("r", 0, 2), ("r", 0, 0), ("at0", 3, 3), ("ws2", 0, 0), ("op0", 0, 3), ("wr", 3, 2),
    ("wr", 3, 0), ("ws1", 0, 0), ("sa0", 0, 1), ("sa0", 0, 0), ("x1", 0, 0), ("ww", 0, 1),
    ("wr", 3, 1), ("r", 0, 3), ("ww", 0, 2), ("ud0", 0, 0), ("wr", 3, 3), ("ud0", 0, 1),
    ("r", 1, 0), ("sa0", 0, 3), ("wr", 4, 2), ("ud0", 0, 3), ("r", 1, 1), ("wr", 5, 3),
    ("sa0", 0, 2), ("x1", 0, 1), ("ud0", 0, 2), ("r", 1, 2), ("sm0", 0, 1), ("sm0", 0, 0),
    ("ww", 1, 0), ("wr", 4, 0), ("nq1", 0, 0), ("wr", 4, 1), ("r", 1, 3), ("nq1", 0, 1),
    ("at1", 3, 1), ("at1", 3, 0), ("op1", 0, 1), ("sm0", 0, 2), ("op1", 0, 0), ("wr", 5, 2),
    ("nq1", 0, 2), ("r", 2, 1), ("sm0", 0, 3), ("at1", 3, 2), ("op1", 0, 2), ("x1", 0, 2),
    ("r", 2, 0), ("wr", 4, 3), ("nq1", 0, 3), ("at1", 3, 3), ("wr", 5, 1), ("op1", 0, 3),
    ("r", 2, 2), ("r", 2, 3), ("wr", 5, 0), ("sa1", 0, 0), ("ww", 1, 1), ("sa1", 0, 1),
    ("sa1", 0, 2), ("ww", 1, 2), ("ud1", 0, 1), ("ud1", 0, 2), ("sa1", 0, 3), ("hu1", 0, 1),
    ("r", 3, 1), ("ud1", 0, 3), ("hu1", 0, 2), ("r", 3, 2), ("r", 3, 3), ("ud1", 0, 0),
    ("hu1", 0, 3), ("hu1", 0, 0), ("wg12", 0, 1), ("sm1", 0, 3), ("r", 4, 3), ("r", 3, 0),
    ("wg12", 0, 0), ("sm1", 0, 1), ("wg11", 0, 1), ("r", 4, 1), ("sd1", 0, 3), ("gp1", 2, 2),
    ("sm1", 0, 2), ("sm1", 0, 0), ("r", 4, 2), ("ag1", 0, 3), ("gp1", 2, 3), ("ab1", 3, 3),
    ("gp1", 2, 0), ("qb1", 0, 3), ("sd1", 0, 2), ("r", 4, 0), ("wg11", 0, 0), ("gp1", 2, 1),
    ("sd1", 0, 1), ("r", 5, 3), ("ag1", 0, 2), ("ab1", 3, 2), ("gp1", 1, 3), ("qb1", 0, 2),
    ("ag1", 0, 1), ("sd1", 0, 0), ("ab1", 3, 1), ("r", 5, 2), ("qb1", 0, 1), ("sb1", 0, 3),
    ("ag1", 0, 0), ("ab1", 3, 0), ("gp1", 1, 2), ("qb1", 0, 0), ("r", 5, 1), ("wg10", 0, 1),
    ("gp1", 1, 0), ("hu0", 0, 3), ("wg10", 0, 0), ("gp1", 1, 1), ("sb1", 0, 2), ("r", 5, 0),
    ("r", 6, 3), ("sb1", 0, 1), ("hu0", 0, 2), ("gp1", 0, 3), ("sb1", 0, 0), ("hu0", 0, 1),
    ("gp1", 0, 2), ("hu0", 0, 0), ("wg02", 0, 0), ("gp1", 0, 0), ("sd0", 0, 3), ("wg02", 0, 1),
    ("r", 6, 2), ("wg01", 0, 0), ("gp1", 0, 1), ("ag0", 0, 3), ("ab0", 3, 3), ("r", 6, 1),
    ("sd0", 0, 2), ("qb0", 0, 3), ("gp0", 2, 0), ("r", 6, 0), ("ag0", 0, 2), ("ab0", 3, 2),
    ("wg01", 0, 1), ("qb0", 0, 2), ("gp0", 2, 3), ("sd0", 0, 1), ("gp0", 2, 1), ("gp0", 2, 2),
    ("gf", 2, 1), ("r", 7, 3), ("r", 7, 2), ("ag0", 0, 1), ("sd0", 0, 0), ("ab0", 3, 1),
    ("qb0", 0, 1), ("gp0", 1, 1), ("gp0", 1, 0), ("ag0", 0, 0), ("ab0", 3, 0), ("sb0", 0, 2),
    ("gf", 1, 1), ("qb0", 0, 0), ("gp0", 1, 3), ("wg00", 0, 0), ("gf", 0, 1), ("gp0", 1, 2),
    ("r", 7, 0), ("wg00", 0, 1), ("r", 7, 1), ("sb0", 0, 1), ("sb0", 0, 0), ("gf", 1, 0),
    ("sb0", 0, 3), ("gp0", 0, 1), ("gp0", 0, 0), ("gg0", 0, 0), ("gf", 2, 0), ("gp0", 0, 3),
    ("gp0", 0, 2), ("gg1", 0, 0), ("gg2", 0, 0), ("gg3", 0, 0), ("es", 0, 0), ("gf", 0, 0),
)


def run_blocks(inputs, cotangent, weights, gain_rows, lengths, depth, inside):
    buckets, chunk, width = inputs.shape
    rows = CHUNKS * chunk
    part = chunk // 2
    heads = width // 4 // HEAD
    vmem, dma = pltpu.VMEM, pltpu.SemaphoreType.DMA
    scratch = dict(
        W=vmem((2, PARTS, width, width), BF16),
        X0=vmem((CHUNKS * part, width), BF16),
        Y0=vmem((CHUNKS * part, width), BF16),
        CT=vmem((rows, width), BF16),
        DR=vmem((rows, width), BF16),
        N1=vmem((2, rows, width), BF16),
        N2=vmem((2, rows, width), BF16),
        Q=vmem((2, heads, rows, 2 * HEAD), BF16),
        KV=vmem((2, heads, rows, 2 * HEAD), BF16),
        KT=vmem((2, heads, HEAD, rows), BF16),
        ATT=vmem((2, rows, (heads + 1) * HEAD), BF16),
        LSE=vmem((2, 8, rows), F32),
        PRE=vmem((2, rows, width), BF16),
        HID=vmem((rows, width), BF16),
        DPRE=vmem((rows, width), BF16),
        DQKV=vmem((rows, 3 * heads * HEAD), BF16),
        DA=vmem((2, rows, width), BF16),
        DKV=vmem((heads, rows, 2 * HEAD), F32),
        GRAD=vmem((heads, chunk, 2 * HEAD), BF16),
        GRADT=vmem((8, chunk), F32),
        DQT=vmem((heads, HEAD, chunk), F32),
        MID=vmem((2, CHUNKS * part, width), F32),
        PART=vmem((2, rows, width), BF16),
        RC=vmem((2, CHUNKS, part, width), BF16),
        RX=vmem((3, CHUNKS, part, width), BF16),
        STG=vmem((4, width // 2, width), BF16),
        GAINS=vmem((8, width), F32),
        BIAS=vmem((8, chunk), F32),
        GACC=vmem((2, 8, width), F32),
        in_send=dma((2, 3)),
        in_recv=dma((2, CHUNKS)),
        mate_send=dma((CHUNKS,)),
        mate_recv=dma((CHUNKS,)),
        pair_send=dma((7, CHUNKS)),
        pair_recv=dma((7, CHUNKS)),
        rs_send=dma((8, 2, CHUNKS)),
        rs_recv=dma((8, 2, CHUNKS)),
        w_recv=dma((2, PARTS, depth if inside else 1)),
        stg_send=dma((2, PARTS, 4)),
        out_send=dma((4, CHUNKS)),
        out_recv=dma((4, 2, 2)),
    )
    outs = dict(
        acts=jax.ShapeDtypeStruct(inputs.shape, BF16), igr=jax.ShapeDtypeStruct(inputs.shape, BF16)
    )
    if inside:
        slab = width // depth
        scratch.update(
            GR=vmem((2, PARTS, width, width), BF16),
            ZR=vmem((depth - 1, PARTS, slab, width), BF16),
            FIN=vmem((2, slab, width), F32),
            GIN=vmem((2, depth, 8, slab + -slab % 128), F32),
            OWN_GAINS=vmem((8, slab + -slab % 128), F32),
            own_a=vmem((slab, width), BF16),
            GC=vmem((8, width), F32),
            GX=vmem((8, width), F32),
            GY=vmem((8, width), F32),
            GZ=vmem((depth - 1, 8, width), F32),
            w_send=dma((PARTS, depth)),
            relay_send=dma((2, PARTS, depth)),
            onward_send=dma((2, PARTS, depth)),
            gr_recv=dma((2, PARTS, 4)),
            z_send=dma((PARTS, depth)),
            z_recv=dma((PARTS, depth - 1)),
            fin_send=dma((PARTS,)),
            gin_send=dma((2, depth)),
            gin_recv=dma((2, depth)),
            gg_send=dma((3 + depth,)),
            gg_recv=dma((4 + depth,)),
        )
        own = dict(w_qkv=weights[0], w_out=weights[1], own_b=weights[2], own_c=weights[3])
        outs["gsum"] = jax.ShapeDtypeStruct((PARTS, slab, width), F32)
    else:
        own = dict(w_whole=weights)
        outs["grads"] = jax.ShapeDtypeStruct(weights.shape, BF16)
    outs["gain_out"] = jax.ShapeDtypeStruct((8, width), F32)
    given = dict(inp=inputs, cot=cotangent, **own, gain_rows=gain_rows, lengths=lengths)
    hbm = pl.BlockSpec(memory_space=pl.ANY)
    in_vmem = pl.BlockSpec(memory_space=pltpu.VMEM)
    small = ("gain_rows", "gain_out", "w_qkv", "w_out")
    in_smem = pl.BlockSpec(memory_space=pltpu.SMEM)
    return pl.pallas_call(
        functools.partial(
            block_kernel, inside, STEPS, list(given) + list(outs) + list(scratch)
        ),
        out_shape=tuple(outs.values()),
        in_specs=[
            in_vmem if name in small else in_smem if name == "lengths" else hbm for name in given
        ],
        out_specs=tuple(in_vmem if name in small else hbm for name in outs),
        scratch_shapes=list(scratch.values()),
        compiler_params=pltpu.CompilerParams(
            collective_id=0, has_side_effects=True, vmem_limit_bytes=VMEM_LIMIT
        ),
        cost_estimate=pl.CostEstimate(
            flops=27_000_000_000, bytes_accessed=40_000_000, transcendentals=20_000_000
        ),
        name="blocks",
    )(*given.values())


def unpack_kernel(gsum, acts, igr, gain_part, *outs):
    acts_out, igr_out, gain_out, qkv_out, out_out, up_out, down_out = outs
    columns = qkv_out.shape[2]
    heads = columns // HEAD
    first = gsum[0]
    kv = [first[:, i * HEAD : (i + 1) * HEAD] for i in range(2 * heads)]
    qkv_out[0] = first[:, 2 * columns : 3 * columns]
    qkv_out[1] = jnp.concatenate(kv[0::2], axis=1)
    qkv_out[2] = jnp.concatenate(kv[1::2], axis=1)
    out_out[0] = first[:, 3 * columns :].T
    up_out[0] = gsum[1]
    down_out[...] = gsum[2]
    acts_out[0] = acts[...]
    igr_out[0] = igr[...]
    width, share = gain_part.shape[1], gain_out.shape[2]
    at = lax.axis_index("tensor") * lax.axis_size("dp") + lax.axis_index("dp")
    turned = pltpu.roll(gain_part[...], width - at * share, 1)
    gain_out[0] = turned[0:2, 0:share]


def unpack_results(total, acts, input_grads, gain_part, shapes):
    in_vmem = pl.BlockSpec(memory_space=pltpu.VMEM)
    return pl.pallas_call(
        unpack_kernel,
        out_shape=tuple(jax.ShapeDtypeStruct(shape, kind) for shape, kind in shapes),
        in_specs=[in_vmem] * 4,
        out_specs=(in_vmem,) * 7,
        name="unpack",
    )(total, acts, input_grads, gain_part)


def shards(inputs, lengths, gains, w_qkv, w_out, w_up, w_down, cotangent):
    local_rows, width = inputs.shape[1:]
    slab = w_up.shape[1]
    heads = w_qkv.shape[3] // HEAD
    depth = lax.axis_size("dp")
    y = lax.div(lax.axis_index("tensor"), 2)
    section = lax.axis_index("section")
    inside = slab % 16 == 0 and depth == 4
    axes = ("section", "tensor")
    if inside:
        own = (w_qkv[0].transpose(1, 0, 2), w_out[0], w_up[0], w_down[0].T)
        acts, input_grads, total, gain_part = run_blocks(
            inputs, cotangent, own, gains[0], lengths, depth, inside
        )
        columns = heads * HEAD
        results = unpack_results(
            total,
            acts,
            input_grads,
            gain_part,
            (
                ((1,) + acts.shape, BF16),
                ((1,) + acts.shape, BF16),
                ((1, 2, width // (depth * lax.axis_size("tensor"))), F32),
                ((3, slab, columns), F32),
                (w_out.shape, F32),
                (w_up.shape, F32),
                ((slab, width), F32),
            ),
        )
        acts, input_grads, gain_grads, qkv_grads, out_grads, up_grads, down_grads = results
        return (
            acts,
            input_grads,
            gain_grads,
            qkv_grads.transpose(1, 0, 2)[None],
            out_grads,
            up_grads,
            down_grads.T[None],
        )
    else:
        split = (slab, heads, HEAD)
        kv = jnp.stack([w_qkv[0, :, 1].reshape(split), w_qkv[0, :, 2].reshape(split)], axis=2)
        own = (
            jnp.concatenate([kv.reshape(slab, -1), w_qkv[0, :, 0], w_out[0].T], axis=1),
            w_up[0],
            w_down[0].T,
        )
        whole = lax.all_gather(jnp.stack(own), "dp", axis=1, tiled=True)
        weights = []
        for l in range(2):
            parts = []
            for to_y in range(2):
                pairs = [
                    (4 * l + 2 * c + x, 4 * c + 2 * to_y + x) for c in range(2) for x in range(2)
                ]
                parts.append(lax.ppermute(whole, axes, pairs))
            weights.append(jnp.where(y == 0, parts[0], parts[1]))
        weights = jnp.stack(weights)
        gain_rows = lax.all_gather(gains, "dp", axis=2, tiled=True)
        gain_rows = lax.all_gather(gain_rows, "section", axis=0, tiled=True)
        gain_rows = jnp.pad(gain_rows.reshape(4, width).astype(F32), ((0, 4), (0, 0)))
        acts, input_grads, partial, gain_part = run_blocks(
            inputs, cotangent, weights, gain_rows, lengths, depth, inside
        )
        total = jnp.zeros(partial.shape[1:], F32)
        for l in range(2):
            for from_y in range(2):
                pairs = [
                    (4 * c + 2 * from_y + x, 4 * l + 2 * c + x) for c in range(2) for x in range(2)
                ]
                total = total + lax.ppermute(partial[l], axes, pairs).astype(F32)
        total = lax.psum_scatter(total.astype(BF16), "dp", scatter_dimension=1, tiled=True)
        total = total.astype(F32)
        gain_part = lax.psum(gain_part[:4].reshape(2, 2, width), "section")
        gain_part = lax.dynamic_slice_in_dim(gain_part, section, 1, 0)
        first = (section == 0) & (jnp.arange(2) == 0)
        gain_part = gain_part * jnp.where(first, 1.0, 0.5)[None, :, None]
        gain_grads = lax.psum_scatter(
            gain_part, ("tensor", "dp"), scatter_dimension=2, tiled=True
        )
    columns = heads * HEAD
    kv = total[0, :, : 2 * columns].reshape(slab, heads, 2, HEAD)
    q = total[0, :, 2 * columns : 3 * columns]
    qkv_grads = jnp.stack([q, kv[:, :, 0].reshape(q.shape), kv[:, :, 1].reshape(q.shape)], axis=1)
    return (
        acts[None],
        input_grads[None],
        gain_grads,
        qkv_grads[None],
        total[0, :, 3 * columns :].T[None],
        total[1][None],
        total[2].T[None],
    )


def solution(mesh):
    in_specs = (
        P("dp", "tensor", None),
        P("dp"),
        P("section", None, "dp"),
        P("section", "dp", None, "tensor"),
        P("section", "tensor", "dp"),
        P("section", "dp", "tensor"),
        P("section", "tensor", "dp"),
        P("dp", "tensor", None),
    )
    out_specs = (
        P("section", "dp", "tensor", None),
        P("section", "dp", "tensor", None),
        P("section", None, ("tensor", "dp")),
        P("section", "dp", None, "tensor"),
        P("section", "tensor", "dp"),
        P("section", "dp", "tensor"),
        P("section", "tensor", "dp"),
    )
    return jax.shard_map(shards, mesh=mesh, in_specs=in_specs, out_specs=out_specs, check_vma=False)
```

```python
import functools

import jax
import jax.numpy as jnp
from jax import lax
from jax.experimental import pallas as pl
from jax.experimental.pallas import tpu as pltpu
from jax.sharding import PartitionSpec as P

HEAD = 64
EPSILON = 1e-05
MASKED = -1e30
CHUNKS = 4
PARTS = 3
VMEM_LIMIT = 63 << 20
TILE = 256
BF16 = jnp.bfloat16
F32 = jnp.float32
MESH = pl.DeviceIdType.MESH

SUM_ATTN = (0, 2)
SUM_MLP = (1, 3)
SUM_DMLP = (6, 4)
SUM_DATTN = (7, 5)
PAIR_N2 = (0, 1)
PAIR_N1 = (6, 2)
PAIR_DA = (4, 3)
PAIR_DR = 5


def nn(left, right):
    return lax.dot_general(left, right, (((1,), (0,)), ((), ())), preferred_element_type=F32)


def nt(left, right):
    return lax.dot_general(left, right, (((1,), (1,)), ((), ())), preferred_element_type=F32)


def tn(left, right):
    return lax.dot_general(left, right, (((0,), (0,)), ((), ())), preferred_element_type=F32)


def unit_rows(rows):
    centre = rows - jnp.mean(rows, axis=-1, keepdims=True)
    spread = jnp.mean(centre * centre, axis=-1, keepdims=True)
    scale = lax.rsqrt(spread + EPSILON)
    return centre * scale, scale


def norm_back(unit, scale, gain, grad):
    wide = grad * gain
    inner = jnp.mean(wide * unit, axis=-1, keepdims=True)
    return scale * (wide - jnp.mean(wide, axis=-1, keepdims=True) - unit * inner)


def gelu_parts(x):
    root = 0.7978845608028654
    square = x * x
    bend = jnp.tanh(root * x * (1.0 + 0.044715 * square))
    half = 0.5 + 0.5 * bend
    slope = half + 0.5 * x * (1.0 - bend * bend) * (root * (1.0 + 0.134145 * square))
    return x * half, slope


class Names:
    pass


def block_kernel(inside, steps, names, *refs):
    n = Names()
    for name, ref in zip(names, refs, strict=True):
        setattr(n, name, ref)
    s = lax.axis_index("section")
    t = lax.axis_index("tensor")
    z = lax.axis_index("dp")
    x = lax.rem(t, 2)
    y = lax.div(t, 2)
    t_y = 2 * (1 - y) + x
    mate = (1 - s, t, z)
    peer_x = (s, 2 * y + 1 - x, z)
    peer_y = (s, t_y, z)
    hub = s == y
    rows_all, width = n.CT.shape
    chunk = rows_all // CHUNKS
    part = chunk // 2
    half = CHUNKS // 2
    heads = n.KT.shape[1]
    tiles = width // TILE
    depth = lax.axis_size("dp")
    slab = width // depth
    q_columns = 2 * heads * HEAD
    o_columns = 3 * heads * HEAD

    def remote(src, dst, send_sem, recv_sem, device):
        return pltpu.make_async_remote_copy(
            src_ref=src,
            dst_ref=dst,
            send_sem=send_sem,
            recv_sem=recv_sem,
            device_id=device,
            device_id_type=MESH,
        )

    def done(ref, sem):
        pltpu.make_async_copy(ref, ref, sem).wait()

    def rows_of(j):
        return pl.ds(pl.multiple_of(j * chunk, chunk), chunk)

    def half_of(j, c):
        return pl.ds(pl.multiple_of(j * chunk + c * part, part), part)

    def own_of(j):
        return pl.ds(pl.multiple_of(j * part, part), part)

    def slab_of(i):
        return pl.ds(pl.multiple_of(i * slab, slab), slab)

    def bytes_of(count):
        return n.PART.at[0, 0:count]

    if inside:
        q, k, v = (n.w_qkv[i] for i in range(3))
        columns = []
        for h in range(heads):
            here = slice(h * HEAD, (h + 1) * HEAD)
            columns += [k[:, here], v[:, here]]
        turned = n.w_out[...].astype(F32).T.astype(BF16)
        n.own_a[...] = jnp.concatenate(columns + [q, turned], axis=1)
        n.OWN_GAINS[...] = jnp.zeros_like(n.OWN_GAINS)
        n.OWN_GAINS[0:2, 0:slab] = n.gain_rows[...].astype(F32)

    n.GACC[...] = jnp.zeros_like(n.GACC)
    n.BIAS[...] = jnp.where(n.lengths[y] == rows_all, 0.0, MASKED) + jnp.zeros_like(n.BIAS)

    barrier = pltpu.get_barrier_semaphore()
    greeted = 0
    for other_s in range(2):
        for other in range(CHUNKS):
            greeted += 1

            @pl.when((s != other_s) | (t != other))
            def _():
                pl.semaphore_signal(
                    barrier, inc=1, device_id=(other_s, other, z), device_id_type=MESH
                )

        if inside:
            for other in range(depth):
                greeted += 1

                @pl.when(z != other)
                def _():
                    pl.semaphore_signal(
                        barrier, inc=1, device_id=(other_s, t, other), device_id_type=MESH
                    )

    pl.semaphore_wait(barrier, greeted - 1 - (2 if inside else 0))

    def pick(index, values):
        value = values[0]
        for at in range(1, len(values)):
            value = jnp.where(index == at, values[at], value)
        return value

    def not_far(end):
        if end == 0:
            return z < depth // 2
        if end == depth - 1:
            return z >= depth // 2
        return z >= 0

    def weights_send(l, p):
        if not inside:
            pltpu.make_async_copy(n.w_whole.at[l, p], n.W.at[l, p], n.w_recv.at[l, p, 0]).start()
            return
        own = (n.own_a, n.own_b, n.own_c)[p]

        @pl.when(s == l)
        def _():
            for far in range(depth):
                @pl.when(hub & (z == far))
                def _():
                    pltpu.make_async_copy(
                        own, n.W.at[l, p, slab_of(z)], n.w_recv.at[l, p, z]
                    ).start()

                @pl.when(jnp.logical_not(hub & (z == far)) & not_far(far))
                def _():
                    remote(
                        own,
                        n.W.at[l, p, slab_of(z)],
                        n.w_send.at[p, far],
                        n.w_recv.at[l, p, z],
                        (y, t, far),
                    ).start()

    def weights_sent(p):
        own = (n.own_a, n.own_b, n.own_c)[p]
        for far in range(depth):

            @pl.when(jnp.logical_not(hub & (z == far)) & not_far(far))
            def _():
                done(own, n.w_send.at[p, far])

    def weights_relay(l, p, step):
        if not inside:
            return

        @pl.when(hub)
        def _():
            beside = z + 1 - 2 * lax.rem(z, 2)
            low = z < 2
            far = pick(step, [z, beside, jnp.where(low, 2, 1), jnp.where(low, 3, 0)])
            here = n.W.at[l, p, slab_of(far)]
            done(here, n.w_recv.at[l, p, far])
            remote(
                here, here, n.relay_send.at[l, p, far], n.w_recv.at[l, p, far], peer_y
            ).start()
            for place, end in ((1, 0), (2, 3)):

                @pl.when((z == place) & (far >= 2 if place == 1 else far < 2))
                def _():
                    remote(
                        here,
                        here,
                        n.onward_send.at[l, p, far],
                        n.w_recv.at[l, p, far],
                        (s, t, end),
                    ).start()

    def weights_wait(l, p):
        if not inside:
            done(n.W.at[l, p], n.w_recv.at[l, p, 0])
            return

        @pl.when(jnp.logical_not(hub))
        def _():
            for far in range(depth):
                done(n.W.at[l, p, slab_of(far)], n.w_recv.at[l, p, far])

    t_x = 2 * y + 1 - x
    t_far = 2 * (1 - y) + 1 - x

    def landing(which, target, source_t):
        return target.at[own_of(source_t)] if which == 0 else target.at[half_of(source_t, s)]

    def spread(which, source, target):
        here = source.at[y, half_of(0, s)]
        own = landing(which, target, t)
        remote(
            source.at[1 - y, half_of(0, s)],
            own,
            n.in_send.at[which, 0],
            n.in_recv.at[which, t],
            peer_y,
        ).start()
        remote(here, own, n.in_send.at[which, 1], n.in_recv.at[which, t], peer_x).start()
        pltpu.make_async_copy(here, own, n.in_recv.at[which, t]).start()

    def spread_pass(which, target):
        near = landing(which, target, t_y)
        done(near, n.in_recv.at[which, t_y])
        remote(near, near, n.in_send.at[which, 2], n.in_recv.at[which, t_y], peer_x).start()

    def spread_wait(which, j):
        @pl.when(j != t_y)
        def _():
            done(bytes_of(part), n.in_recv.at[which, j])

    def inputs_pass(j):
        spread_wait(0, j)
        norm_first(0, n.X0[own_of(j), :].astype(F32), j)

    def cotangent_pass(j):
        here = n.CT.at[half_of(j, s)]
        spread_wait(1, j)
        remote(here, here, n.mate_send.at[j], n.mate_recv.at[j], mate).start()

    def cotangent_wait(j):
        done(bytes_of(part), n.mate_recv.at[j])

    def spread_done(which):
        for way in range(3):
            done(bytes_of(part), n.in_send.at[which, way])
        if which == 1:
            for j in range(CHUNKS):
                done(bytes_of(part), n.mate_send.at[j])

    def pair_start(stage, ref, j):
        here = ref.at[half_of(j, s)]
        remote(here, here, n.pair_send.at[stage, j], n.pair_recv.at[stage, j], mate).start()

    def pair_wait(stage, j):
        done(bytes_of(part), n.pair_recv.at[stage, j])

    def sum_start(stage, j):
        b = stage % 2
        remote(
            n.PART.at[b, half_of(j, 1 - s)],
            n.RC.at[b, j],
            n.rs_send.at[stage, 0, j],
            n.rs_recv.at[stage, 0, j],
            mate,
        ).start()

    def sum_pass(stage, j):
        b = lax.rem(stage, 2)
        here = half_of(j, s)
        done(n.RC.at[b, j], n.rs_recv.at[stage, 0, j])
        n.PART[b, here, :] = (
            n.PART[b, here, :].astype(F32) + n.RC[b, j].astype(F32)
        ).astype(BF16)
        arriving = jnp.where(stage == SUM_DMLP[1], 2, b)
        one_way = (stage == SUM_MLP[1]) | (stage == SUM_DATTN[0])

        @pl.when(jnp.logical_not(one_way) | (lax.rem(j, 2) != x))
        def _():
            remote(
                n.PART.at[b, here],
                n.RX.at[arriving, j],
                n.rs_send.at[stage, 1, j],
                n.rs_recv.at[stage, 1, j],
                peer_x,
            ).start()

        done(n.RC.at[b, j], n.rs_send.at[stage, 0, j])

    def sum_sent(stage, j):
        done(n.RX.at[stage % 2, j], n.rs_send.at[stage, 1, j])

    def sum_wait(stage, j):
        b = stage % 2
        arriving = 2 if stage == SUM_DMLP[1] else b
        done(n.RX.at[arriving, j], n.rs_recv.at[stage, 1, j])
        total = n.PART[b, half_of(j, s), :].astype(F32) + n.RX[arriving, j].astype(F32)
        if stage not in (SUM_MLP[1], SUM_DATTN[0]):
            sum_sent(stage, j)
        return total

    first_index = lax.broadcasted_iota(jnp.int32, (chunk, chunk), 0)
    second_index = lax.broadcasted_iota(jnp.int32, (chunk, chunk), 1)

    def scores(l, st, i, j, diagonal, keys_first):
        if l == 0:
            grown = st * st + 1.0
            inverse = lax.rsqrt(grown)
            magnitude = grown * inverse
            sign = st * inverse
        else:
            inverse, magnitude, sign = None, st, None
        if diagonal:
            seen = first_index <= second_index if keys_first else second_index <= first_index
            magnitude = jnp.where(seen, magnitude, MASKED)
        else:
            apart = (j >= half) & (i < half)
            magnitude = magnitude + jnp.where(apart, n.BIAS[0:1, :], 0.0)
        return inverse, magnitude, sign

    def norm_first(l, own_rows, j):
        unit, _ = unit_rows(own_rows)
        n.N1[l, half_of(j, s), :] = (unit * n.GAINS[2 * l : 2 * l + 1, :]).astype(BF16)
        pair_start(PAIR_N1[l], n.N1.at[l], j)

    def qkv_product(l, j):
        rows = rows_of(j)
        pair_wait(PAIR_N1[l], j)
        kv = nn(n.N1[l, rows, :], n.W[l, 0, :, 0:q_columns])
        kv_low = kv.astype(BF16)
        turned = kv.T.astype(BF16)
        for h in range(heads):
            n.KV[l, h, rows, :] = kv_low[:, 2 * h * HEAD : 2 * (h + 1) * HEAD]
            n.KT[l, h, :, rows] = turned[2 * h * HEAD : (2 * h + 1) * HEAD]
        q = nn(n.N1[l, rows, :], n.W[l, 0, :, q_columns:o_columns]).astype(BF16)
        blank = jnp.zeros((chunk, HEAD), BF16)
        for h in range(heads):
            q_h = q[:, h * HEAD : (h + 1) * HEAD] * jnp.asarray(HEAD**-0.5, BF16)
            n.Q[l, h, rows, :] = jnp.concatenate([q_h, blank], axis=1)

    def attend(l, j):
        rows = rows_of(j)

        def block(i, carry, diagonal):
            keys = rows_of(i)
            new = []
            for h in range(heads):
                top, total, out = carry[h]
                kv = n.KV[l, h, keys, :]
                st = nt(n.Q[l, h, rows, :], kv)
                _, magnitude, sign = scores(l, st, i, j, diagonal, False)
                new_top = jnp.maximum(top, jnp.max(magnitude, axis=1, keepdims=True))
                weights = jnp.exp(magnitude - new_top)
                shrink = jnp.exp(top - new_top)
                total = total * shrink + jnp.sum(weights, axis=1, keepdims=True)
                signed = weights if l == 1 else sign * weights
                out = out * shrink + nn(signed.astype(BF16), kv)
                new.append((new_top, total, out))
            return tuple(new)

        carry = (
            jnp.full((chunk, 1), MASKED, F32),
            jnp.zeros((chunk, 1), F32),
            jnp.zeros((chunk, 2 * HEAD), F32),
        )
        carry = block(j, (carry,) * heads, True)
        carry = lax.fori_loop(0, j, lambda i, c: block(i, c, False), carry)
        lane = lax.broadcasted_iota(jnp.int32, (chunk, 128), 1)
        logs = jnp.zeros((chunk, 128), F32)
        outs = [jnp.zeros((chunk, HEAD), BF16)]
        for h in range(heads):
            top, total, out = carry[h]
            outs.append((out / total)[:, HEAD:].astype(BF16))
            logs = jnp.where(lane == h, top + jnp.log(total), logs)
        n.ATT[l, rows, :] = jnp.concatenate(outs, axis=1)
        n.LSE[l, :, rows] = logs.T[0:8]

    def out_product(l, j):
        rows = rows_of(j)
        for i in range(tiles):
            here = slice(i * TILE, (i + 1) * TILE)
            n.PART[0, rows, here] = nt(
                n.ATT[l, rows, :], n.W[l, 0, here, o_columns - HEAD : width]
            ).astype(BF16)
        sum_start(SUM_ATTN[l], j)

    def attn_sum(l, j):
        source = n.X0 if l == 0 else n.Y0
        own = half_of(j, s)
        middle = source[own_of(j), :].astype(F32) + sum_wait(SUM_ATTN[l], j)
        n.MID[l, own_of(j), :] = middle
        unit, _ = unit_rows(middle)
        n.N2[l, own, :] = (unit * n.GAINS[2 * l + 1 : 2 * l + 2, :]).astype(BF16)
        pair_start(PAIR_N2[l], n.N2.at[l], j)

    def up_product(l, j):
        rows = rows_of(j)
        pair_wait(PAIR_N2[l], j)
        for i in range(tiles):
            here = slice(i * TILE, (i + 1) * TILE)
            pre = nn(n.N2[l, rows, :], n.W[l, 1, :, here])
            n.PRE[l, rows, here] = pre.astype(BF16)
            n.HID[rows, here] = gelu_parts(pre)[0].astype(BF16)
        for i in range(tiles):
            here = slice(i * TILE, (i + 1) * TILE)
            n.PART[1, rows, here] = nt(n.HID[rows, :], n.W[l, 2, here, :]).astype(BF16)
        sum_start(SUM_MLP[l], j)

    def mlp_sum(l, j):
        if l == 0:
            result = (n.MID[l, own_of(j), :] + sum_wait(SUM_MLP[l], j)).astype(BF16)
            n.Y0[own_of(j), :] = result
            norm_first(1, result.astype(F32), j)
            give_out(2, 0, n.Y0.at[own_of(j)], n.acts, j)
        else:

            @pl.when(lax.rem(j, 2) == x)
            def _():
                result = n.MID[l, own_of(j), :] + sum_wait(SUM_MLP[l], j)
                n.PART[1, half_of(j, s), :] = result.astype(BF16)
                give_out(0, 1, n.PART.at[1, half_of(j, s)], n.acts, j)

            @pl.when(lax.rem(j, 2) != x)
            def _():
                sum_sent(SUM_MLP[l], j)

    def give_out(which, section, here, out, j):
        target = out.at[y, half_of(0, s)]

        @pl.when((s == section) & (t == j))
        def _():
            copy = pltpu.make_async_copy(here, target, n.out_send.at[which, j])
            copy.start()
            copy.wait()

        @pl.when((lax.rem(j, 2) == x) & ((s != section) | (t != j)))
        def _():
            remote(
                here,
                target,
                n.out_send.at[which, j],
                n.out_recv.at[which, y, s],
                (section, j, z),
            ).start()

    def given_out(which, section, j):
        @pl.when((lax.rem(j, 2) == x) & ((s != section) | (t != j)))
        def _():
            done(bytes_of(part), n.out_send.at[which, j])

    def got_out(which, section):
        @pl.when(s == section)
        def _():
            for m in range(2):
                for c in range(2):

                    @pl.when((y != m) | (s != c))
                    def _():
                        done(bytes_of(part), n.out_recv.at[which, m, c])

    def hidden_back(l, j):
        rows = rows_of(j)
        if l == 1:
            cotangent_wait(j)
        else:
            pair_wait(PAIR_DR, j)
        source = n.CT if l == 1 else n.DR
        for i in range(tiles):
            here = slice(i * TILE, (i + 1) * TILE)
            back = nn(source[rows, :], n.W[l, 2, :, here])
            hidden, slope = gelu_parts(n.PRE[l, rows, here].astype(F32))
            n.HID[rows, here] = hidden.astype(BF16)
            n.DPRE[rows, here] = (slope * back).astype(BF16)
        for i in range(tiles):
            here = slice(i * TILE, (i + 1) * TILE)
            n.PART[0, rows, here] = nt(n.DPRE[rows, :], n.W[l, 1, here, :]).astype(BF16)
        sum_start(SUM_DMLP[l], j)

    def mlp_back_sum(l, j):
        total = sum_wait(SUM_DMLP[l], j)
        source = n.CT if l == 1 else n.DR
        own = half_of(j, s)
        unit, scale = unit_rows(n.MID[l, own_of(j), :])
        n.GACC[l, 1:2, :] += jnp.sum(total * unit, axis=0, keepdims=True)
        gain = n.GAINS[2 * l + 1 : 2 * l + 2, :]
        grad = source[own, :].astype(F32) + norm_back(unit, scale, gain, total)
        n.MID[l, own_of(j), :] = grad
        n.DA[l, own, :] = grad.astype(BF16)
        pair_start(PAIR_DA[l], n.DA.at[l], j)

    def attn_grad(l, j):
        rows = rows_of(j)
        pair_wait(PAIR_DA[l], j)

        @pl.when(j == CHUNKS - 1)
        def _():
            n.DKV[...] = jnp.zeros_like(n.DKV)

        low = nn(n.DA[l, rows, :], n.W[l, 0, :, o_columns - HEAD : width]).astype(BF16)
        product = low.astype(F32) * n.ATT[l, rows, :].astype(F32)
        blank = jnp.zeros((chunk, HEAD), BF16)
        lane = lax.broadcasted_iota(jnp.int32, (chunk, 128), 1)
        inner = jnp.zeros((chunk, 128), F32)
        for h in range(heads):
            here = slice((h + 1) * HEAD, (h + 2) * HEAD)
            n.GRAD[h] = jnp.concatenate([blank, low[:, here]], axis=1)
            inner = jnp.where(
                lane == h, jnp.sum(product[:, here], axis=1, keepdims=True), inner
            )
        n.GRADT[...] = inner.T[0:8]

    def attend_back(l, j):
        rows = rows_of(j)

        def block(i, carry, diagonal):
            keys = rows_of(i)
            new = []
            for h in range(heads):
                kv = n.KV[l, h, keys, :]
                st = nt(kv, n.Q[l, h, rows, :])
                dp = nt(kv, n.GRAD[h])
                inverse, magnitude, sign = scores(l, st, i, j, diagonal, True)
                weights = jnp.exp(magnitude - n.LSE[l, h : h + 1, rows])
                inner = n.GRADT[h : h + 1, :]
                if l == 0:
                    signed = sign * weights
                    ds = weights * (
                        sign * (sign * dp - inner) + dp * (inverse * inverse * inverse)
                    )
                else:
                    signed = weights
                    ds = weights * (dp - inner)
                ds = ds.astype(BF16)
                n.DKV[h, keys, :] += nn(ds, n.Q[l, h, rows, :]) + nn(
                    signed.astype(BF16), n.GRAD[h]
                )
                new.append(carry[h] + nn(n.KT[l, h, :, keys], ds))
            return tuple(new)

        blank = jnp.zeros((HEAD, chunk), F32)
        query_grad = block(j, (blank,) * heads, True)
        query_grad = lax.fori_loop(0, j, lambda i, c: block(i, c, False), query_grad)
        for h in range(heads):
            n.DQT[h] = query_grad[h] * HEAD**-0.5

    def qkv_back(l, j):
        rows = rows_of(j)
        turned = jnp.concatenate([n.DQT[h] for h in range(heads)], axis=0).T
        for h in range(heads):
            n.DQKV[rows, 2 * h * HEAD : 2 * (h + 1) * HEAD] = n.DKV[h, rows, :].astype(BF16)
        n.DQKV[rows, q_columns:] = turned.astype(BF16)
        if l == 1:
            given_out(0, 1, j)
        for i in range(tiles):
            here = slice(i * TILE, (i + 1) * TILE)
            n.PART[1, rows, here] = nt(n.DQKV[rows, :], n.W[l, 0, here, 0:o_columns]).astype(
                BF16
            )
        sum_start(SUM_DATTN[l], j)

    def attn_back_result(l, j):
        total = sum_wait(SUM_DATTN[l], j)
        source = n.X0 if l == 0 else n.Y0
        unit, scale = unit_rows(source[own_of(j), :].astype(F32))
        n.GACC[l, 0:1, :] += jnp.sum(total * unit, axis=0, keepdims=True)
        gain = n.GAINS[2 * l : 2 * l + 1, :]
        return n.MID[l, own_of(j), :] + norm_back(unit, scale, gain, total)

    def attn_back_sum(l, j):
        own = half_of(j, s)
        if l == 1:
            n.DR[own, :] = attn_back_result(l, j).astype(BF16)
            pair_start(PAIR_DR, n.DR, j)
            give_out(3, 1, n.DR.at[own], n.igr, j)
        else:

            @pl.when(lax.rem(j, 2) == x)
            def _():
                n.PART[1, own, :] = attn_back_result(l, j).astype(BF16)
                give_out(1, 0, n.PART.at[1, own], n.igr, j)

            @pl.when(lax.rem(j, 2) != x)
            def _():
                sum_sent(SUM_DATTN[l], j)

    long = width // 2
    grad_order = ((1, 2), (1, 1), (1, 0), (0, 2), (0, 1), (0, 0))
    grad_to = 2 * s + x

    def kept_here(l):
        return hub & (s == l)

    def grad_sent(l, p, i):
        if not inside:
            done(n.STG.at[0], n.stg_send.at[l, p, i])
            return

        @pl.when(jnp.logical_not(kept_here(l)))
        def _():
            for k in range(2):
                done(n.STG.at[0, 0:slab], n.stg_send.at[l, p, 2 * i + k])

    def weight_grad(l, p, i):
        at = grad_order.index((l, p))
        slot = 2 * (at % 2) + i
        if at > 1:
            grad_sent(*grad_order[at - 2], i)
        rows = pl.ds(pl.multiple_of(i * long, long), long)
        if p == 0:
            left = n.N1[l, :, rows]
            n.STG[slot, :, 0:256] = tn(left, n.DQKV[:, 0:256]).astype(BF16)
            n.STG[slot, :, 256:512] = tn(left, n.DQKV[:, 256:512]).astype(BF16)
            last = tn(left, n.DQKV[:, 512:o_columns])
            out_part = tn(n.DA[l, :, rows], n.ATT[l])
            n.STG[slot, :, 512:width] = jnp.concatenate([last, out_part[:, HEAD:]], axis=1).astype(
                BF16
            )
        else:
            if p == 1:
                left, right = n.N2[l, :, rows], n.DPRE
            else:
                left, right = (n.CT if l == 1 else n.DR)[:, rows], n.HID
            for k in range(tiles):
                here = slice(k * TILE, (k + 1) * TILE)
                n.STG[slot, :, here] = tn(left, right[:, here]).astype(BF16)
        if not inside:
            pltpu.make_async_copy(
                n.STG.at[slot], n.grads.at[l, p, rows], n.stg_send.at[l, p, i]
            ).start()
            return

        @pl.when(kept_here(l))
        def _():
            n.GR[0, p, rows, :] = n.STG[slot]

        @pl.when(jnp.logical_not(kept_here(l)))
        def _():
            way = jnp.where(hub, 0, 1)
            for k in range(2):
                k_at = jnp.where(i == 0, k, 1 - k)
                at_slab = 2 * i + k_at
                remote(
                    n.STG.at[slot, slab_of(k_at)],
                    n.GR.at[way, p, slab_of(at_slab)],
                    n.stg_send.at[l, p, at_slab],
                    n.gr_recv.at[way, p, at_slab],
                    (l, grad_to, z),
                ).start()

    def slot_of(source, target):
        return jnp.where(source > target, source - 1, source)

    def grad_pass(l, p, far):
        if not inside:
            return

        @pl.when(s == l)
        def _():
            here = slab_of(far)

            @pl.when(jnp.logical_not(hub))
            def _():
                done(n.GR.at[0, p, here], n.gr_recv.at[0, p, far])

            done(n.GR.at[1, p, here], n.gr_recv.at[1, p, far])

            @pl.when(z != far)
            def _():
                n.GR[0, p, here, :] = (
                    n.GR[0, p, here, :].astype(F32) + n.GR[1, p, here, :].astype(F32)
                ).astype(BF16)
                slot = slot_of(z, far)
                remote(
                    n.GR.at[0, p, here],
                    n.ZR.at[slot, p],
                    n.z_send.at[p, far],
                    n.z_recv.at[p, slot],
                    (s, t, far),
                ).start()

    def grad_final(l, p):
        if not inside:
            return

        @pl.when(s == l)
        def _():
            here = slab_of(z)
            total = n.GR[0, p, here, :].astype(F32) + n.GR[1, p, here, :].astype(F32)
            for slot in range(depth - 1):
                done(n.ZR.at[slot, p], n.z_recv.at[p, slot])
                total = total + n.ZR[slot, p].astype(F32)
            slot = lax.rem(p, 2)

            @pl.when(p == 0)
            def _():
                done(n.FIN.at[0], n.fin_send.at[2])

            n.FIN[slot] = total
            pltpu.make_async_copy(n.FIN.at[slot], n.gsum.at[p], n.fin_send.at[p]).start()

    def grads_done():
        for i in range(2):
            grad_sent(*grad_order[-1], i)
        if not inside:
            return
        for far in range(depth):

            @pl.when(z != far)
            def _():
                done(n.ZR.at[0, 0], n.z_send.at[0, far])

        done(n.FIN.at[0], n.fin_send.at[0])
        done(n.FIN.at[1], n.fin_send.at[1])

    def gains_send():
        if not inside:
            n.GAINS[...] = n.gain_rows[...]
            return
        n.GIN[s, z] = n.OWN_GAINS[...]
        for c in range(2):
            for far in range(depth):

                @pl.when((s != c) | (z != far))
                def _():
                    remote(
                        n.OWN_GAINS,
                        n.GIN.at[s, z],
                        n.gin_send.at[c, far],
                        n.gin_recv.at[s, z],
                        (c, t, far),
                    ).start()

    def gains_wait():
        if not inside:
            return
        for c in range(2):
            for far in range(depth):

                @pl.when((s != c) | (z != far))
                def _():
                    done(n.OWN_GAINS, n.gin_recv.at[c, far])
                    done(n.OWN_GAINS, n.gin_send.at[c, far])

                for k in range(2):
                    n.GAINS[2 * c + k : 2 * c + k + 1, far * slab : (far + 1) * slab] = n.GIN[
                        c, far, k : k + 1, 0:slab
                    ]

    def gain_grads(step):
        if not inside:
            return
        if step == 0:
            remote(n.GACC.at[1 - s], n.GC, n.gg_send.at[0], n.gg_recv.at[0], mate).start()
        elif step == 1:
            done(n.GC, n.gg_recv.at[0])
            n.GACC[s] += n.GC[...]
            remote(n.GACC.at[s], n.GX, n.gg_send.at[6], n.gg_recv.at[4], peer_x).start()
        elif step == 2:
            done(n.GX, n.gg_recv.at[4])
            done(n.GX, n.gg_send.at[6])
            row = lax.broadcasted_iota(jnp.int32, n.GX.shape, 0)
            n.GACC[s] += jnp.where((row == 0) & (s == 0), n.GX[...], 0.0)
            remote(n.GACC.at[s], n.GY, n.gg_send.at[1], n.gg_recv.at[1], peer_y).start()
        else:
            done(n.GY, n.gg_recv.at[1])
            n.GC[...] = n.GACC[s] + n.GY[...]
            for far in range(depth):

                @pl.when(z != far)
                def _():
                    slot = slot_of(z, far)
                    remote(
                        n.GC,
                        n.GZ.at[slot],
                        n.gg_send.at[2 + far],
                        n.gg_recv.at[5 + slot],
                        (s, t, far),
                    ).start()

    def gain_grads_done():
        if not inside:
            n.gain_out[...] = jnp.concatenate([n.GACC[0, 0:2], n.GACC[1, 0:2], n.GACC[0, 4:8]])
            return
        total = n.GC[...]
        for slot in range(depth - 1):
            done(n.GZ.at[slot], n.gg_recv.at[5 + slot])
            total = total + n.GZ[slot]
        n.gain_out[...] = total
        done(n.GC, n.gg_send.at[0])
        done(n.GC, n.gg_send.at[1])
        for far in range(depth):

            @pl.when(z != far)
            def _():
                done(n.GC, n.gg_send.at[2 + far])

    def early_sends():
        if inside:
            for p in range(PARTS):
                weights_sent(p)
                for l in range(2):

                    @pl.when(hub)
                    def _():
                        for far in range(depth):
                            done(n.W.at[l, p, slab_of(far)], n.relay_send.at[l, p, far])

                            @pl.when((z == 1) if far >= 2 else (z == 2))
                            def _():
                                done(n.W.at[l, p, slab_of(far)], n.onward_send.at[l, p, far])

            for p in (1, 2):
                for far in range(depth):

                    @pl.when(z != far)
                    def _():
                        done(n.ZR.at[0, p], n.z_send.at[p, far])

        spread_done(0)
        spread_done(1)

        @pl.loop(0, CHUNKS)
        def _(j):
            for stage in range(7):
                done(bytes_of(part), n.pair_send.at[stage, j])
            for which, section in ((1, 0), (2, 0), (3, 1)):
                given_out(which, section, j)

        for which, section in ((0, 1), (2, 0), (3, 1)):
            got_out(which, section)
        for i in range(2):
            grad_sent(*grad_order[-2], i)

    tasks = {"none": lambda h, j: None}
    for l in range(2):
        tasks[f"nq{l}"] = lambda h, j, l=l: qkv_product(l, j)
        tasks[f"at{l}"] = lambda h, j, l=l: attend(l, j)
        tasks[f"op{l}"] = lambda h, j, l=l: out_product(l, j)
        tasks[f"sa{l}"] = lambda h, j, l=l: attn_sum(l, j)
        tasks[f"ud{l}"] = lambda h, j, l=l: up_product(l, j)
        tasks[f"sm{l}"] = lambda h, j, l=l: mlp_sum(l, j)
        tasks[f"hu{l}"] = lambda h, j, l=l: hidden_back(l, j)
        tasks[f"sd{l}"] = lambda h, j, l=l: mlp_back_sum(l, j)
        tasks[f"ag{l}"] = lambda h, j, l=l: attn_grad(l, j)
        tasks[f"ab{l}"] = lambda h, j, l=l: attend_back(l, j)
        tasks[f"qb{l}"] = lambda h, j, l=l: qkv_back(l, j)
        tasks[f"sb{l}"] = lambda h, j, l=l: attn_back_sum(l, j)
        for p in range(PARTS):
            tasks[f"wg{l}{p}"] = lambda h, j, l=l, p=p: weight_grad(l, p, j)
    for p in range(PARTS):
        tasks[f"ws{p}"] = lambda h, j, p=p: weights_send(1, p)
        tasks[f"wt{p}"] = lambda h, j, p=p: weights_send(0, p)
    tasks["r"] = lambda h, j: sum_pass(h, j)
    tasks["x0"] = lambda h, j: inputs_pass(j)
    tasks["x1"] = lambda h, j: cotangent_pass(j)
    tasks["wr"] = lambda h, j: weights_relay(lax.div(h, PARTS), lax.rem(h, PARTS), j)
    tasks["ww"] = lambda h, j: weights_wait(h, j)
    for l in range(2):
        tasks[f"gp{l}"] = lambda h, j, l=l: grad_pass(l, h, j)
    tasks["es"] = lambda h, j: early_sends()
    tasks["gf"] = lambda h, j: grad_final(j, h)
    for step in range(4):
        tasks[f"gg{step}"] = lambda h, j, step=step: gain_grads(step)
    tasks["gw"] = lambda h, j: gains_wait()
    tasks["xp"] = lambda h, j: spread_pass(0, n.X0)
    tasks["cp"] = lambda h, j: spread_pass(1, n.CT)
    tasks["cs"] = lambda h, j: spread(1, n.cot, n.CT)
    used = {"none"} | {name for name, _, _ in steps}
    order = [name for name in tasks if name in used]
    run = [tasks[name] for name in order]

    weights_send(0, 0)
    gains_send()
    spread(0, n.inp, n.X0)

    group = 6
    codes = [order.index(name) * 32 + h * 4 + j for name, h, j in steps]
    codes = [0] * (-len(codes) % group) + codes
    pairs = [codes[i] + 4096 * codes[i + 1] for i in range(0, len(codes), 2)]
    per_group = group // 2
    groups = len(pairs) // per_group

    def dispatch(low, high, op, h, j):
        if high - low == 1:
            run[low](h, j)
            return
        middle = (low + high) // 2
        lax.cond(
            op < middle,
            lambda: dispatch(low, middle, op, h, j),
            lambda: dispatch(middle, high, op, h, j),
        )

    @pl.loop(0, groups)
    def _(g):
        words = [
            pick(g, [pairs[q * per_group + w] for q in range(groups)]) for w in range(per_group)
        ]

        @pl.loop(0, group)
        def _(i):
            word = pick(lax.shift_right_logical(i, 1), words)
            code = jnp.where((i & 1) == 0, word & 4095, lax.shift_right_logical(word, 12))
            dispatch(
                0,
                len(run),
                lax.shift_right_logical(code, 5),
                lax.shift_right_logical(code, 2) & 7,
                code & 3,
            )

    got_out(1, 0)
    grads_done()
    gain_grads_done()


STEPS = (
    ("cs", 0, 0),
    ("wt2", 0, 0),
    ("wt1", 0, 0),
    ("wr", 0, 0),
    ("xp", 0, 0),
    ("wr", 0, 1),
    ("wr", 0, 2),
    ("gw", 0, 0),
    ("wr", 0, 3),
    ("x0", 0, 0),
    ("x0", 0, 1),
    ("wr", 2, 2),
    ("x0", 0, 2),
    ("wr", 2, 0),
    ("cp", 0, 0),
    ("wr", 2, 1),
    ("ww", 0, 0),
    ("nq0", 0, 1),
    ("nq0", 0, 0),
    ("at0", 3, 1),
    ("nq0", 0, 2),
    ("op0", 0, 1),
    ("wr", 1, 2),
    ("x0", 0, 3),
    ("x1", 0, 3),
    ("at0", 3, 2),
    ("wr", 1, 0),
    ("wr", 1, 1),
    ("wr", 1, 3),
    ("op0", 0, 2),
    ("ws0", 0, 0),
    ("at0", 3, 0),
    ("op0", 0, 0),
    ("nq0", 0, 3),
    ("wr", 2, 3),
    ("r", 0, 1),
    ("r", 0, 2),
    ("r", 0, 0),
    ("at0", 3, 3),
    ("ws2", 0, 0),
    ("op0", 0, 3),
    ("wr", 3, 2),
    ("wr", 3, 0),
    ("ws1", 0, 0),
    ("sa0", 0, 1),
    ("sa0", 0, 0),
    ("x1", 0, 0),
    ("ww", 0, 1),
    ("wr", 3, 1),
    ("r", 0, 3),
    ("ww", 0, 2),
    ("ud0", 0, 0),
    ("wr", 3, 3),
    ("ud0", 0, 1),
    ("r", 1, 0),
    ("sa0", 0, 3),
    ("wr", 4, 2),
    ("ud0", 0, 3),
    ("r", 1, 1),
    ("wr", 5, 3),
    ("sa0", 0, 2),
    ("x1", 0, 1),
    ("ud0", 0, 2),
    ("r", 1, 2),
    ("sm0", 0, 1),
    ("sm0", 0, 0),
    ("ww", 1, 0),
    ("wr", 4, 0),
    ("nq1", 0, 0),
    ("wr", 4, 1),
    ("r", 1, 3),
    ("nq1", 0, 1),
    ("at1", 3, 1),
    ("at1", 3, 0),
    ("op1", 0, 1),
    ("sm0", 0, 2),
    ("op1", 0, 0),
    ("wr", 5, 2),
    ("nq1", 0, 2),
    ("r", 2, 1),
    ("sm0", 0, 3),
    ("at1", 3, 2),
    ("op1", 0, 2),
    ("x1", 0, 2),
    ("r", 2, 0),
    ("wr", 4, 3),
    ("nq1", 0, 3),
    ("at1", 3, 3),
    ("wr", 5, 1),
    ("op1", 0, 3),
    ("r", 2, 2),
    ("r", 2, 3),
    ("wr", 5, 0),
    ("sa1", 0, 0),
    ("ww", 1, 1),
    ("sa1", 0, 1),
    ("sa1", 0, 2),
    ("ww", 1, 2),
    ("ud1", 0, 1),
    ("ud1", 0, 2),
    ("sa1", 0, 3),
    ("hu1", 0, 1),
    ("r", 3, 1),
    ("ud1", 0, 3),
    ("hu1", 0, 2),
    ("r", 3, 2),
    ("r", 3, 3),
    ("ud1", 0, 0),
    ("hu1", 0, 3),
    ("hu1", 0, 0),
    ("wg12", 0, 1),
    ("sm1", 0, 3),
    ("r", 4, 3),
    ("r", 3, 0),
    ("wg12", 0, 0),
    ("sm1", 0, 1),
    ("wg11", 0, 1),
    ("r", 4, 1),
    ("sd1", 0, 3),
    ("gp1", 2, 2),
    ("sm1", 0, 2),
    ("sm1", 0, 0),
    ("r", 4, 2),
    ("ag1", 0, 3),
    ("gp1", 2, 3),
    ("ab1", 3, 3),
    ("gp1", 2, 0),
    ("qb1", 0, 3),
    ("sd1", 0, 2),
    ("r", 4, 0),
    ("wg11", 0, 0),
    ("gp1", 2, 1),
    ("sd1", 0, 1),
    ("r", 5, 3),
    ("ag1", 0, 2),
    ("ab1", 3, 2),
    ("gp1", 1, 3),
    ("qb1", 0, 2),
    ("ag1", 0, 1),
    ("sd1", 0, 0),
    ("ab1", 3, 1),
    ("r", 5, 2),
    ("qb1", 0, 1),
    ("sb1", 0, 3),
    ("ag1", 0, 0),
    ("ab1", 3, 0),
    ("gp1", 1, 2),
    ("qb1", 0, 0),
    ("r", 5, 1),
    ("wg10", 0, 1),
    ("gp1", 1, 0),
    ("hu0", 0, 3),
    ("wg10", 0, 0),
    ("gp1", 1, 1),
    ("sb1", 0, 2),
    ("r", 5, 0),
    ("r", 6, 3),
    ("sb1", 0, 1),
    ("hu0", 0, 2),
    ("gp1", 0, 3),
    ("sb1", 0, 0),
    ("hu0", 0, 1),
    ("gp1", 0, 2),
    ("hu0", 0, 0),
    ("wg02", 0, 0),
    ("gp1", 0, 0),
    ("sd0", 0, 3),
    ("wg02", 0, 1),
    ("r", 6, 2),
    ("wg01", 0, 0),
    ("gp1", 0, 1),
    ("ag0", 0, 3),
    ("ab0", 3, 3),
    ("r", 6, 1),
    ("sd0", 0, 2),
    ("qb0", 0, 3),
    ("gp0", 2, 0),
    ("r", 6, 0),
    ("ag0", 0, 2),
    ("ab0", 3, 2),
    ("wg01", 0, 1),
    ("qb0", 0, 2),
    ("gp0", 2, 3),
    ("sd0", 0, 1),
    ("gp0", 2, 1),
    ("gp0", 2, 2),
    ("gf", 2, 1),
    ("r", 7, 3),
    ("r", 7, 2),
    ("ag0", 0, 1),
    ("sd0", 0, 0),
    ("ab0", 3, 1),
    ("qb0", 0, 1),
    ("gp0", 1, 1),
    ("gp0", 1, 0),
    ("ag0", 0, 0),
    ("ab0", 3, 0),
    ("sb0", 0, 2),
    ("gf", 1, 1),
    ("qb0", 0, 0),
    ("wg00", 0, 0),
    ("wg00", 0, 1),
    ("r", 7, 0),
    ("r", 7, 1),
    ("gp0", 1, 3),
    ("gp0", 1, 2),
    ("sb0", 0, 1),
    ("sb0", 0, 0),
    ("sb0", 0, 3),
    ("gg0", 0, 0),
    ("gf", 0, 1),
    ("gp0", 0, 1),
    ("gp0", 0, 0),
    ("gg1", 0, 0),
    ("gp0", 0, 3),
    ("gg2", 0, 0),
    ("gp0", 0, 2),
    ("gg3", 0, 0),
    ("gf", 2, 0),
    ("gf", 1, 0),
    ("es", 0, 0),
    ("gf", 0, 0),
)


def run_blocks(inputs, cotangent, weights, gain_rows, lengths, depth, inside):
    buckets, chunk, width = inputs.shape
    rows = CHUNKS * chunk
    part = chunk // 2
    heads = width // 4 // HEAD
    vmem, dma = pltpu.VMEM, pltpu.SemaphoreType.DMA
    scratch = dict(
        W=vmem((2, PARTS, width, width), BF16),
        X0=vmem((CHUNKS * part, width), BF16),
        Y0=vmem((CHUNKS * part, width), BF16),
        CT=vmem((rows, width), BF16),
        DR=vmem((rows, width), BF16),
        N1=vmem((2, rows, width), BF16),
        N2=vmem((2, rows, width), BF16),
        Q=vmem((2, heads, rows, 2 * HEAD), BF16),
        KV=vmem((2, heads, rows, 2 * HEAD), BF16),
        KT=vmem((2, heads, HEAD, rows), BF16),
        ATT=vmem((2, rows, (heads + 1) * HEAD), BF16),
        LSE=vmem((2, 8, rows), F32),
        PRE=vmem((2, rows, width), BF16),
        HID=vmem((rows, width), BF16),
        DPRE=vmem((rows, width), BF16),
        DQKV=vmem((rows, 3 * heads * HEAD), BF16),
        DA=vmem((2, rows, width), BF16),
        DKV=vmem((heads, rows, 2 * HEAD), F32),
        GRAD=vmem((heads, chunk, 2 * HEAD), BF16),
        GRADT=vmem((8, chunk), F32),
        DQT=vmem((heads, HEAD, chunk), F32),
        MID=vmem((2, CHUNKS * part, width), F32),
        PART=vmem((2, rows, width), BF16),
        RC=vmem((2, CHUNKS, part, width), BF16),
        RX=vmem((3, CHUNKS, part, width), BF16),
        STG=vmem((4, width // 2, width), BF16),
        GAINS=vmem((8, width), F32),
        BIAS=vmem((8, chunk), F32),
        GACC=vmem((2, 8, width), F32),
        in_send=dma((2, 3)),
        in_recv=dma((2, CHUNKS)),
        mate_send=dma((CHUNKS,)),
        mate_recv=dma((CHUNKS,)),
        pair_send=dma((7, CHUNKS)),
        pair_recv=dma((7, CHUNKS)),
        rs_send=dma((8, 2, CHUNKS)),
        rs_recv=dma((8, 2, CHUNKS)),
        w_recv=dma((2, PARTS, depth if inside else 1)),
        stg_send=dma((2, PARTS, 4)),
        out_send=dma((4, CHUNKS)),
        out_recv=dma((4, 2, 2)),
    )
    outs = dict(
        acts=jax.ShapeDtypeStruct(inputs.shape, BF16), igr=jax.ShapeDtypeStruct(inputs.shape, BF16)
    )
    if inside:
        slab = width // depth
        scratch.update(
            GR=vmem((2, PARTS, width, width), BF16),
            ZR=vmem((depth - 1, PARTS, slab, width), BF16),
            FIN=vmem((2, slab, width), F32),
            GIN=vmem((2, depth, 8, slab + -slab % 128), F32),
            OWN_GAINS=vmem((8, slab + -slab % 128), F32),
            own_a=vmem((slab, width), BF16),
            GC=vmem((8, width), F32),
            GX=vmem((8, width), F32),
            GY=vmem((8, width), F32),
            GZ=vmem((depth - 1, 8, width), F32),
            w_send=dma((PARTS, depth)),
            relay_send=dma((2, PARTS, depth)),
            onward_send=dma((2, PARTS, depth)),
            gr_recv=dma((2, PARTS, 4)),
            z_send=dma((PARTS, depth)),
            z_recv=dma((PARTS, depth - 1)),
            fin_send=dma((PARTS,)),
            gin_send=dma((2, depth)),
            gin_recv=dma((2, depth)),
            gg_send=dma((3 + depth,)),
            gg_recv=dma((4 + depth,)),
        )
        own = dict(w_qkv=weights[0], w_out=weights[1], own_b=weights[2], own_c=weights[3])
        outs["gsum"] = jax.ShapeDtypeStruct((PARTS, slab, width), F32)
    else:
        own = dict(w_whole=weights)
        outs["grads"] = jax.ShapeDtypeStruct(weights.shape, BF16)
    outs["gain_out"] = jax.ShapeDtypeStruct((8, width), F32)
    given = dict(inp=inputs, cot=cotangent, **own, gain_rows=gain_rows, lengths=lengths)
    hbm = pl.BlockSpec(memory_space=pl.ANY)
    in_vmem = pl.BlockSpec(memory_space=pltpu.VMEM)
    small = ("gain_rows", "gain_out", "w_qkv", "w_out")
    in_smem = pl.BlockSpec(memory_space=pltpu.SMEM)
    return pl.pallas_call(
        functools.partial(
            block_kernel, inside, STEPS, list(given) + list(outs) + list(scratch)
        ),
        out_shape=tuple(outs.values()),
        in_specs=[
            in_vmem if name in small else in_smem if name == "lengths" else hbm for name in given
        ],
        out_specs=tuple(in_vmem if name in small else hbm for name in outs),
        scratch_shapes=list(scratch.values()),
        compiler_params=pltpu.CompilerParams(
            collective_id=0, has_side_effects=True, vmem_limit_bytes=VMEM_LIMIT
        ),
        cost_estimate=pl.CostEstimate(
            flops=27_000_000_000, bytes_accessed=40_000_000, transcendentals=20_000_000
        ),
        name="blocks",
    )(*given.values())


def unpack_kernel(gsum, acts, igr, gain_part, *outs):
    acts_out, igr_out, gain_out, qkv_out, out_out, up_out, down_out = outs
    columns = qkv_out.shape[2]
    heads = columns // HEAD
    first = gsum[0]
    kv = [first[:, i * HEAD : (i + 1) * HEAD] for i in range(2 * heads)]
    qkv_out[0] = first[:, 2 * columns : 3 * columns]
    qkv_out[1] = jnp.concatenate(kv[0::2], axis=1)
    qkv_out[2] = jnp.concatenate(kv[1::2], axis=1)
    out_out[0] = first[:, 3 * columns :].T
    up_out[0] = gsum[1]
    down_out[...] = gsum[2]
    acts_out[0] = acts[...]
    igr_out[0] = igr[...]
    width, share = gain_part.shape[1], gain_out.shape[2]
    at = lax.axis_index("tensor") * lax.axis_size("dp") + lax.axis_index("dp")
    turned = pltpu.roll(gain_part[...], width - at * share, 1)
    gain_out[0] = turned[0:2, 0:share]


def unpack_results(total, acts, input_grads, gain_part, shapes):
    in_vmem = pl.BlockSpec(memory_space=pltpu.VMEM)
    return pl.pallas_call(
        unpack_kernel,
        out_shape=tuple(jax.ShapeDtypeStruct(shape, kind) for shape, kind in shapes),
        in_specs=[in_vmem] * 4,
        out_specs=(in_vmem,) * 7,
        name="unpack",
    )(total, acts, input_grads, gain_part)


def shards(inputs, lengths, gains, w_qkv, w_out, w_up, w_down, cotangent):
    local_rows, width = inputs.shape[1:]
    slab = w_up.shape[1]
    heads = w_qkv.shape[3] // HEAD
    depth = lax.axis_size("dp")
    y = lax.div(lax.axis_index("tensor"), 2)
    section = lax.axis_index("section")
    inside = slab % 16 == 0 and depth == 4
    axes = ("section", "tensor")
    if inside:
        own = (w_qkv[0].transpose(1, 0, 2), w_out[0], w_up[0], w_down[0].T)
        acts, input_grads, total, gain_part = run_blocks(
            inputs, cotangent, own, gains[0], lengths, depth, inside
        )
        columns = heads * HEAD
        results = unpack_results(
            total,
            acts,
            input_grads,
            gain_part,
            (
                ((1,) + acts.shape, BF16),
                ((1,) + acts.shape, BF16),
                ((1, 2, width // (depth * lax.axis_size("tensor"))), F32),
                ((3, slab, columns), F32),
                (w_out.shape, F32),
                (w_up.shape, F32),
                ((slab, width), F32),
            ),
        )
        acts, input_grads, gain_grads, qkv_grads, out_grads, up_grads, down_grads = results
        return (
            acts,
            input_grads,
            gain_grads,
            qkv_grads.transpose(1, 0, 2)[None],
            out_grads,
            up_grads,
            down_grads.T[None],
        )
    else:
        split = (slab, heads, HEAD)
        kv = jnp.stack([w_qkv[0, :, 1].reshape(split), w_qkv[0, :, 2].reshape(split)], axis=2)
        own = (
            jnp.concatenate([kv.reshape(slab, -1), w_qkv[0, :, 0], w_out[0].T], axis=1),
            w_up[0],
            w_down[0].T,
        )
        whole = lax.all_gather(jnp.stack(own), "dp", axis=1, tiled=True)
        weights = []
        for l in range(2):
            parts = []
            for to_y in range(2):
                pairs = [
                    (4 * l + 2 * c + x, 4 * c + 2 * to_y + x) for c in range(2) for x in range(2)
                ]
                parts.append(lax.ppermute(whole, axes, pairs))
            weights.append(jnp.where(y == 0, parts[0], parts[1]))
        weights = jnp.stack(weights)
        gain_rows = lax.all_gather(gains, "dp", axis=2, tiled=True)
        gain_rows = lax.all_gather(gain_rows, "section", axis=0, tiled=True)
        gain_rows = jnp.pad(gain_rows.reshape(4, width).astype(F32), ((0, 4), (0, 0)))
        acts, input_grads, partial, gain_part = run_blocks(
            inputs, cotangent, weights, gain_rows, lengths, depth, inside
        )
        total = jnp.zeros(partial.shape[1:], F32)
        for l in range(2):
            for from_y in range(2):
                pairs = [
                    (4 * c + 2 * from_y + x, 4 * l + 2 * c + x) for c in range(2) for x in range(2)
                ]
                total = total + lax.ppermute(partial[l], axes, pairs).astype(F32)
        total = lax.psum_scatter(total.astype(BF16), "dp", scatter_dimension=1, tiled=True)
        total = total.astype(F32)
        gain_part = lax.psum(gain_part[:4].reshape(2, 2, width), "section")
        gain_part = lax.dynamic_slice_in_dim(gain_part, section, 1, 0)
        first = (section == 0) & (jnp.arange(2) == 0)
        gain_part = gain_part * jnp.where(first, 1.0, 0.5)[None, :, None]
        gain_grads = lax.psum_scatter(
            gain_part, ("tensor", "dp"), scatter_dimension=2, tiled=True
        )
    columns = heads * HEAD
    kv = total[0, :, : 2 * columns].reshape(slab, heads, 2, HEAD)
    q = total[0, :, 2 * columns : 3 * columns]
    qkv_grads = jnp.stack([q, kv[:, :, 0].reshape(q.shape), kv[:, :, 1].reshape(q.shape)], axis=1)
    return (
        acts[None],
        input_grads[None],
        gain_grads,
        qkv_grads[None],
        total[0, :, 3 * columns :].T[None],
        total[1][None],
        total[2].T[None],
    )


def solution(mesh):
    in_specs = (
        P("dp", "tensor", None),
        P("dp"),
        P("section", None, "dp"),
        P("section", "dp", None, "tensor"),
        P("section", "tensor", "dp"),
        P("section", "dp", "tensor"),
        P("section", "tensor", "dp"),
        P("dp", "tensor", None),
    )
    out_specs = (
        P("section", "dp", "tensor", None),
        P("section", "dp", "tensor", None),
        P("section", None, ("tensor", "dp")),
        P("section", "dp", None, "tensor"),
        P("section", "tensor", "dp"),
        P("section", "dp", "tensor"),
        P("section", "tensor", "dp"),
    )
    return jax.shard_map(shards, mesh=mesh, in_specs=in_specs, out_specs=out_specs, check_vma=False)
```
